32 devices in a mesh: dp: 4 (over z), expert: 8 (over y, x, core).
Axes of the slice: x: 2, y: 2, z: 4, core: 2. Of those that a mesh axis runs over, the one named last changes fastest.
Arguments:
- tokens: bfloat16 [128, 144, 512], P(('dp', 'expert')), may hold values from -6 to 6
- patch_counts: int32 [128], P(('dp', 'expert')), may hold values from 49 to 144, as said below
- expert_ids: int32 [128, 144, 2], P(('dp', 'expert')), may hold values from 0 to 7, all different within a row
- priority: int32 [32, 576], P(('dp', 'expert')), may hold values from 0 to 575, each once within a row
- out_grad: bfloat16 [128, 144, 512], P(('dp', 'expert')), may hold values from -6 to 6
- first_gain: bfloat16 [512], P(('dp', 'expert')), may hold values from 0.5 to 1.5
- first_shift: bfloat16 [512], P(('dp', 'expert')), may hold values from -1.25 to 1.25
- qkv_weight: bfloat16 [512, 1536], P(('dp', 'expert')), may hold values from -0.25 to 0.25
- query_bias: bfloat16 [512], P(('dp', 'expert')), may hold values from -1.75 to 1.75
- value_bias: bfloat16 [512], P(('dp', 'expert')), may hold values from -1.75 to 1.75
- proj_weight: bfloat16 [512, 512], P(('dp', 'expert')), may hold values from -2 to 2
- proj_bias: bfloat16 [512], P(('dp', 'expert')), may hold values from -1.75 to 1.75
- second_gain: bfloat16 [512], P(('dp', 'expert')), may hold values from 0.5 to 1.5
- second_shift: bfloat16 [512], P(('dp', 'expert')), may hold values from -1.25 to 1.25
- router_weight: bfloat16 [512, 8], P(('dp', 'expert')), may hold values from -0.1875 to 0.1875
- hidden_weight: bfloat16 [8, 2048, 512], P('expert', 'dp'), may hold values from -0.25 to 0.25
- hidden_bias: bfloat16 [8, 2048], P('expert', 'dp'), may hold values from -1.25 to 1.25
- return_weight: bfloat16 [8, 2048, 512], P('expert', 'dp'), may hold values from -0.875 to 0.875
- return_bias: bfloat16 [8, 512], P('expert', 'dp'), may hold values from -6 to 6
Outputs:
- block_out: bfloat16 [128, 144, 512], P(('dp', 'expert'))
- tokens_grad: bfloat16 [128, 144, 512], P(('dp', 'expert'))
- first_gain_grad: float32 [512], P(('dp', 'expert'))
- first_shift_grad: float32 [512], P(('dp', 'expert'))
- qkv_weight_grad: float32 [512, 1536], P(('dp', 'expert'))
- query_bias_grad: float32 [512], P(('dp', 'expert'))
- value_bias_grad: float32 [512], P(('dp', 'expert'))
- proj_weight_grad: float32 [512, 512], P(('dp', 'expert'))
- proj_bias_grad: float32 [512], P(('dp', 'expert'))
- second_gain_grad: float32 [512], P(('dp', 'expert'))
- second_shift_grad: float32 [512], P(('dp', 'expert'))
- router_weight_grad: float32 [512, 8], P(('dp', 'expert'))
- hidden_weight_grad: float32 [8, 2048, 512], P('expert', 'dp')
- hidden_bias_grad: float32 [8, 2048], P('expert', 'dp')
- return_weight_grad: float32 [8, 2048, 512], P('expert', 'dp')
- return_bias_grad: float32 [8, 512], P('expert', 'dp')
The draws below stay inside these ranges and needn't reach their ends.
Inputs may be any that keep to these rules, and one draw needn't show every extreme that they name: Image i has its patches at its first patch_counts[i] positions and padding after them; every count is 49 or 144. `expert_ids`: the 2 experts of a position differ. `priority`: each row is a permutation of the ranks 0 to 575 of its group's positions.
All inputs are finite; a program needn't handle non-finite values.
Results may differ from the reference program's by a relative error of at most 0.017.
Values may be sent and summed in bfloat16 or wider, within the bound.
No kernel may reach another device: no remote copies, remote signals or barrier semaphores. Data moves between devices by JAX's collectives and lax.ppermute only.
A program may use at most 128 MiB of HBM per device.

```python
import math
from functools import partial
import jax
import jax.numpy as jnp
from jax import lax

D = 512
FF = 2048
HEADS = 8
HEAD_DIM = 64
TOP = 2
PATCH = 144
SMALL_PATCH = 49
IMG_DEV = 4
EXPERTS = 8
GROUPS = 32
TOK_DEV = 576
IMAGES = 128
TOKENS = 18432
CAP = 152


def draw_patch_counts(key, part):
    key = jax.random.fold_in(key, 11)
    coin_flip = jax.random.randint(key, (IMAGES,), 0, 2)
    counts = jnp.where(coin_flip == 1, PATCH, SMALL_PATCH)
    counts = counts.at[0].set(PATCH).at[1].set(SMALL_PATCH)
    return counts.astype(jnp.int32)


def spiked(array, stream_key, source, target, parts, factor):
    def block_of(position):
        return (jnp.arange(array.shape[position]) // (array.shape[position] // parts)).reshape((-1,) + (1,) * (array.ndim - 1 - position))

    first = jax.random.permutation(stream_key, parts)[block_of(target)]
    other_side = (block_of(target) + parts // 2) % parts
    return jnp.where((block_of(source) == first) | (block_of(source) == other_side), factor * array, array)


def steps_of(own_key, extent, pieces, low, largest):
    def one(dim, parts):
        heights = jax.random.uniform(jax.random.fold_in(jax.random.fold_in(own_key, 6), dim), (parts,), jnp.float32, low / len(pieces), largest / len(pieces))
        return jnp.repeat(jnp.exp(heights), extent[dim] // parts).reshape((-1,) + (1,) * (len(extent) - dim - 1))

    factor_of = one(*pieces[0])
    for cut in pieces[1:]:
        factor_of = factor_of * one(*cut)
    return factor_of


def picks_of(key, rows, number_of, top, lift):
    ranking = jax.random.permutation(jax.random.fold_in(key, 1), number_of)
    pull = ranking
    for power in range(3):
        pull = pull * pull // number_of
    pull = pull * lift // number_of
    tickets = jax.random.randint(jax.random.fold_in(key, 2), (rows, number_of), 0, 4096) + pull
    sure = jax.random.permutation(jax.random.fold_in(key, 3), rows)[jnp.arange(number_of) % rows]
    tickets = jnp.where(jnp.arange(rows)[:, None] == sure[None, :], 1 << 14, tickets)
    score = tickets * number_of + jnp.arange(number_of)
    return lax.top_k(score.astype(jnp.int32), top)[1].astype(jnp.int32)


def centred(stream_key, dims, width, bound, cuts=(), held_as=jnp.bfloat16):
    values = width * jax.random.normal(stream_key, dims, jnp.float32)
    if cuts:
        values = values * steps_of(stream_key, dims, cuts, -0.22, 0.18)
    return jnp.clip(values, -bound, bound).astype(held_as)


def gaussian_with(rng, dims, width, reach, pieces, heavy, held_as=jnp.bfloat16):
    array = width * jax.random.normal(rng, dims, jnp.float32)
    if pieces:
        array = array * steps_of(rng, dims, pieces, -0.22, 0.18)
    return jnp.clip(spiked(array, jax.random.fold_in(rng, 3), *heavy), -reach, reach).astype(held_as)


def setup_inputs(seed: int = 0) -> dict:
    splits = jax.random.split(jax.random.key(seed), 20)
    tokens = centred(splits[0], (IMAGES, PATCH, D), 1.0, 6.0, ((0, 32),))
    patch_counts = draw_patch_counts(jax.random.fold_in(splits[19], 71), 0)
    expert_ids = picks_of(splits[2], IMAGES * PATCH, EXPERTS, TOP, 2048).reshape((IMAGES, PATCH, TOP))
    priority = jax.vmap(lambda own: jax.random.permutation(own, TOK_DEV))(jax.random.split(splits[3], GROUPS)).reshape((GROUPS, TOK_DEV)).astype(jnp.int32)
    out_grad = gaussian_with(splits[4], (IMAGES, PATCH, D), 1.0, 6.0, ((0, 32),), (0, 2, 32, 2.75))
    first_gain = jnp.clip(1.0 + 0.1 * jax.random.normal(splits[5], (D,), jnp.float32), 0.5, 1.5).astype(jnp.bfloat16)
    first_shift = centred(splits[6], (D,), 0.2, 1.25, ((0, 32),))
    qkv_weight = centred(splits[7], (D, 3 * D), D ** -0.5, 0.25, ((0, 32),))
    query_bias = centred(splits[8], (D,), 0.3, 1.75, ((0, 32),))
    value_bias = centred(splits[9], (D,), 0.3, 1.75, ((0, 32),))
    proj_weight = centred(splits[10], (D, D), (D // 64) ** -0.5, 2.0, ((0, 32),))
    proj_bias = centred(splits[11], (D,), 0.3, 1.75, ((0, 32),))
    second_gain = jnp.clip(1.0 + 0.1 * jax.random.normal(splits[12], (D,), jnp.float32), 0.5, 1.5).astype(jnp.bfloat16)
    second_shift = centred(splits[13], (D,), 0.2, 1.25, ((0, 32),))
    router_weight = centred(splits[14], (D, EXPERTS), (2 * D) ** -0.5, 0.1875, ((0, 32),))
    hidden_weight = centred(splits[15], (EXPERTS, FF, D), D ** -0.5, 0.25, ((0, 8), (1, 4)))
    hidden_bias = centred(splits[16], (EXPERTS, FF), 0.2, 1.25, ((0, 8), (1, 4)))
    return_weight = centred(splits[17], (EXPERTS, FF, D), (max(1, (3 * FF) // (2 * EXPERTS * EXPERTS))) ** -0.5, 0.875, ((0, 8), (1, 4)))
    return_bias = centred(splits[18], (EXPERTS, D), 1.0, 6.0, ((0, 8), (1, 4)))
    return dict(tokens=tokens, patch_counts=patch_counts, expert_ids=expert_ids, priority=priority, out_grad=out_grad, first_gain=first_gain, first_shift=first_shift, qkv_weight=qkv_weight, query_bias=query_bias, value_bias=value_bias, proj_weight=proj_weight, proj_bias=proj_bias, second_gain=second_gain, second_shift=second_shift, router_weight=router_weight, hidden_weight=hidden_weight, hidden_bias=hidden_bias, return_weight=return_weight, return_bias=return_bias)


norm_eps = 1e-06
neg_large = -1e+30
HIGHEST = lax.Precision.HIGHEST

@jax.custom_vjp
def low(v):
    return lax.optimization_barrier(v.astype(jnp.bfloat16)).astype(jnp.float32)

@jax.custom_vjp
def low_back(v):
    return v

def low_keep(v):
    return (low(v), None)

def low_pass(kept, grad):
    return (grad,)

def back_keep(v):
    return (v, None)

def back_low(kept, grad):
    return (low(grad),)
low.defvjp(low_keep, low_pass)
low_back.defvjp(back_keep, back_low)

def both_round(values):
    return low_back(low(values))

def layer_norm(values, norm_gain, norm_shift):
    center = values - lax.optimization_barrier(jnp.mean(values, axis=-1, keepdims=True))
    spread = lax.optimization_barrier(jnp.mean(center * center, axis=-1, keepdims=True))
    return center * lax.rsqrt(spread + norm_eps) * norm_gain + norm_shift

def router_softmax(logits):
    highest = lax.optimization_barrier(jnp.max(logits, axis=-1, keepdims=True))
    raised = jnp.exp(logits - highest)
    return raised / lax.optimization_barrier(jnp.sum(raised, axis=-1, keepdims=True))

def gelu_tanh(values):
    return jax.nn.gelu(values, approximate=True)

def route_group(choices, valid_rows, rank_rows, experts_all, capacity):
    tok_count = choices.shape[0]
    top_count = choices.shape[1]
    expert_iota = jnp.arange(experts_all, dtype=jnp.int32)
    onehot = ((choices[:, :, None] == expert_iota[None, None, :]) & valid_rows[:, None, None]).astype(jnp.int32)
    order_key = (jnp.arange(top_count, dtype=jnp.int32)[None, :] * tok_count + rank_rows[:, None]).astype(jnp.int32).reshape(-1)
    ordered = jnp.zeros((top_count * tok_count, experts_all), jnp.int32).at[order_key].set(onehot.reshape(-1, experts_all))
    earlier = (jnp.cumsum(ordered, axis=0) - ordered).astype(jnp.int32)
    slot_index = lax.optimization_barrier(jnp.sum(earlier[order_key].reshape(tok_count, top_count, experts_all) * onehot, axis=-1)).astype(jnp.int32)
    is_kept = valid_rows[:, None] & (slot_index < capacity)
    return (slot_index, is_kept)

def make_table(choices, slot_index, is_kept, experts_all, capacity):
    tok_count = choices.shape[0]
    flat_index = jnp.where(is_kept, choices * capacity + slot_index, experts_all * capacity).astype(jnp.int32).reshape(-1)
    owners = jnp.broadcast_to(jnp.arange(tok_count, dtype=jnp.int32)[:, None], choices.shape).reshape(-1)
    token_table = jnp.full((experts_all * capacity,), tok_count, jnp.int32).at[flat_index].set(owners, mode='drop')
    return (token_table, flat_index)

def reference(tokens, patch_counts, expert_ids, priority, out_grad, first_gain, first_shift, qkv_weight, query_bias, value_bias, proj_weight, proj_bias, second_gain, second_shift, router_weight, hidden_weight, hidden_bias, return_weight, return_bias):
    scale_factor = 1.0 / math.sqrt(HEAD_DIM)
    key_valid = jnp.arange(PATCH, dtype=jnp.int32)[None, :] < patch_counts[:, None]
    group_choices = expert_ids.reshape(GROUPS, TOK_DEV, TOP)
    group_valid = key_valid.reshape(GROUPS, TOK_DEV)
    router_rows = partial(route_group, experts_all=EXPERTS, capacity=CAP)
    slot_index, is_kept = jax.vmap(router_rows)(group_choices, group_valid, priority)
    table_rows = partial(make_table, experts_all=EXPERTS, capacity=CAP)
    token_table, flat_unused = jax.vmap(table_rows)(group_choices, slot_index, is_kept)
    group_iota = jnp.arange(GROUPS, dtype=jnp.int32)
    global_table = jnp.where(token_table < TOK_DEV, token_table + group_iota[:, None] * TOK_DEV, TOKENS).astype(jnp.int32)
    expert_table = jnp.transpose(global_table.reshape(GROUPS, EXPERTS, CAP), (1, 0, 2)).reshape(EXPERTS, GROUPS * CAP)
    positions = (group_choices * (GROUPS * CAP) + group_iota[:, None, None] * CAP + jnp.minimum(slot_index, CAP - 1)).astype(jnp.int32).reshape(TOKENS, TOP)
    kept_float = is_kept.reshape(TOKENS, TOP).astype(jnp.float32)
    choice_hot = (expert_ids.reshape(TOKENS, TOP)[:, :, None] == jnp.arange(EXPERTS, dtype=jnp.int32)[None, None, :]).astype(jnp.float32)
    block_mask = key_valid.reshape(GROUPS, IMG_DEV, PATCH)
    split_shape = (IMG_DEV, PATCH, HEADS, HEAD_DIM)

    def forward(residual_in, gain_one, shift_one, qkv_full, query_add, value_add, proj_full, proj_add, gain_two, shift_two, router_full, hidden_full, hidden_add, return_full, return_add):

        def attend(block_pair):
            block_in, block_valid = block_pair
            normed = low(layer_norm(block_in, gain_one, shift_one))
            projected_qkv = jnp.einsum('bpd,de->bpe', normed, qkv_full, precision=HIGHEST)
            query_rows = both_round(projected_qkv[..., :D] + query_add).reshape(split_shape)
            key_rows = both_round(projected_qkv[..., D:2 * D]).reshape(split_shape)
            value_rows = both_round(projected_qkv[..., 2 * D:] + value_add).reshape(split_shape)
            scores = low_back(jnp.einsum('bqhd,bkhd->bhqk', query_rows, key_rows, precision=HIGHEST) * scale_factor)
            masked = jnp.where(block_valid[:, None, None, :], scores, neg_large)
            highest = lax.optimization_barrier(jnp.max(masked, axis=-1, keepdims=True))
            raised = jnp.exp(masked - highest)
            weights = low(raised / lax.optimization_barrier(jnp.sum(raised, axis=-1, keepdims=True)))
            context = both_round(jnp.einsum('bhqk,bkhd->bqhd', weights, value_rows, precision=HIGHEST)).reshape(IMG_DEV, PATCH, D)
            projected = low_back(jnp.einsum('bpd,de->bpe', context, proj_full, precision=HIGHEST) + proj_add)
            return block_in + projected
        blocks_in = residual_in.reshape(GROUPS, IMG_DEV, PATCH, D)
        hidden_res = lax.map(jax.checkpoint(attend), (blocks_in, block_mask)).reshape(TOKENS, D)
        second_low = low(layer_norm(hidden_res, gain_two, shift_two))
        logits = low_back(jnp.dot(second_low, router_full, precision=HIGHEST))
        router_probs = router_softmax(logits)
        gate_weights = lax.optimization_barrier(jnp.sum(router_probs[:, None, :] * choice_hot, axis=-1)) * kept_float
        padded_second = jnp.concatenate([second_low, jnp.zeros((1, D), jnp.float32)], axis=0)

        def expert_pass(expert_pack):
            rows_index, in_weight, in_add, out_weight, out_add = expert_pack
            rows_in = low_back(padded_second[rows_index])
            pre_act = low_back(jnp.einsum('rd,fd->rf', rows_in, in_weight, precision=HIGHEST) + in_add)
            act_low = low(gelu_tanh(pre_act))
            return both_round(jnp.dot(act_low, out_weight, precision=HIGHEST) + out_add)
        expert_rows = lax.map(jax.checkpoint(expert_pass), (expert_table, hidden_full, hidden_add, return_full, return_add)).reshape(EXPERTS * GROUPS * CAP, D)
        first_pick = expert_rows[positions[:, 0]]
        mixed = hidden_res + gate_weights[:, 0:1] * first_pick
        for choice_rank in range(1, TOP):
            mixed = mixed + gate_weights[:, choice_rank:choice_rank + 1] * expert_rows[positions[:, choice_rank]]
        return mixed.reshape(IMAGES, PATCH, D)
    mixed_out, pull_back = jax.vjp(forward, tokens.astype(jnp.float32), first_gain.astype(jnp.float32), first_shift.astype(jnp.float32), qkv_weight.astype(jnp.float32), query_bias.astype(jnp.float32), value_bias.astype(jnp.float32), proj_weight.astype(jnp.float32), proj_bias.astype(jnp.float32), second_gain.astype(jnp.float32), second_shift.astype(jnp.float32), router_weight.astype(jnp.float32), hidden_weight.astype(jnp.float32), hidden_bias.astype(jnp.float32), return_weight.astype(jnp.float32), return_bias.astype(jnp.float32))
    grads = pull_back(out_grad.astype(jnp.float32))
    return (mixed_out.astype(jnp.bfloat16), grads[0].astype(jnp.bfloat16), grads[1], grads[2], grads[3], grads[4], grads[5], grads[6], grads[7], grads[8], grads[9], grads[10], grads[11], grads[12], grads[13], grads[14])
```

```python
import functools
import math

import jax
import jax.numpy as jnp
import numpy as np
from jax import lax
from jax.experimental import pallas as pl
from jax.experimental.pallas import tpu as pltpu
from jax.sharding import PartitionSpec as P

HEADS = 8
QUAD = 4
norm_eps = 1e-06
neg_large = -1e30
F32 = jnp.float32
BF16 = jnp.bfloat16
ROUTER_COL = 32
MISC = 128
GELU_C = math.sqrt(2.0 / math.pi)
GELU_A = 0.044715

NN = (((1,), (0,)), ((), ()))
NT = (((1,), (1,)), ((), ()))
TN = (((0,), (0,)), ((), ()))


def mm(a, b, dims=NN):
    return lax.dot_general(a, b, dims, preferred_element_type=F32)


def params(mib=56):
    return pltpu.CompilerParams(vmem_limit_bytes=mib * 1024 * 1024)


def vmem():
    return pl.BlockSpec(memory_space=pltpu.VMEM)


def smem():
    return pl.BlockSpec(memory_space=pltpu.SMEM)


def normed(values):
    center = values - jnp.mean(values, axis=-1, keepdims=True)
    rstd = lax.rsqrt(jnp.mean(center * center, axis=-1, keepdims=True) + norm_eps)
    return center * rstd, rstd


def norm_back(grad, gain, unit, rstd):
    q = grad * gain
    return rstd * (
        q
        - jnp.mean(q, axis=-1, keepdims=True)
        - unit * jnp.mean(q * unit, axis=-1, keepdims=True)
    )


def masked_softmax(logits, experts):
    lane = lax.broadcasted_iota(jnp.int32, logits.shape, 1)
    inside = (lane >= ROUTER_COL) & (lane < ROUTER_COL + experts)
    logits = jnp.where(inside, logits, neg_large)
    raised = jnp.exp(logits - jnp.max(logits, axis=-1, keepdims=True))
    return raised / jnp.sum(raised, axis=-1, keepdims=True)


def head_stack(rows, head_size):
    lane = lax.broadcasted_iota(jnp.int32, rows.shape, 1) // head_size
    return jnp.concatenate(
        [jnp.where(lane == h, rows, jnp.zeros_like(rows)) for h in range(QUAD)], axis=0
    )


def head_merge(stacked, patches, head_size):
    lane = lax.broadcasted_iota(jnp.int32, (patches, stacked.shape[1]), 1) // head_size
    total = jnp.zeros((patches, stacked.shape[1]), F32)
    for h in range(QUAD):
        total = jnp.where(lane == h, stacked[h * patches : (h + 1) * patches], total)
    return total


def front_kernel(
    dims, scal_ref, cnt_ref, tok_ref, ga_ref, gb_ref, posrow_ref,
    wa_ref, wb_ref, qkv_ref, probs_ref, ctx_ref, hid_ref, rprob_ref, disp_ref,
):
    images, patches, experts, blocks, rels = dims
    width = tok_ref.shape[1]
    head_size = width // HEADS
    rows = ga_ref.shape[1]
    for slot in range(blocks):
        for ref, out, rel in ((ga_ref, wa_ref, rels[0]), (gb_ref, wb_ref, rels[1])):
            at = pl.multiple_of((scal_ref[0] ^ rel[slot]) * rows, rows)
            out[pl.ds(at, rows), :] = ref[slot]
    misc = wb_ref[:, 2 * width :].astype(F32).T
    x = tok_ref[...].astype(F32)
    unit, _ = normed(x)
    first_low = (unit * misc[0:1] + misc[1:2]).astype(BF16)
    qk = mm(first_low, wa_ref[...])
    qkv_ref[:, :width] = (qk[:, :width] + misc[2:3]).astype(BF16)
    qkv_ref[:, width : 2 * width] = qk[:, width:].astype(BF16)
    qkv_ref[:, 2 * width :] = (mm(first_low, wb_ref[:, :width]) + misc[3:4]).astype(BF16)
    scale = 1.0 / math.sqrt(head_size)
    quad_width = QUAD * head_size
    for i in range(images):
        at = slice(i * patches, (i + 1) * patches)
        valid = lax.broadcasted_iota(jnp.int32, (QUAD * patches, patches), 1) < cnt_ref[i]
        for quad in range(HEADS // QUAD):
            lo = quad * quad_width
            q = qkv_ref[at, lo : lo + quad_width]
            k = qkv_ref[at, width + lo : width + lo + quad_width]
            v = qkv_ref[at, 2 * width + lo : 2 * width + lo + quad_width]
            scores = jnp.where(valid, mm(head_stack(q, head_size), k, NT) * scale, neg_large)
            raised = jnp.exp(scores - jnp.max(scores, axis=-1, keepdims=True))
            probs = (raised / jnp.sum(raised, axis=-1, keepdims=True)).astype(BF16)
            probs_ref[i * (HEADS // QUAD) + quad] = probs
            ctx = head_merge(mm(probs, v), patches, head_size)
            ctx_ref[at, lo : lo + quad_width] = ctx.astype(BF16)
    hidden = x + mm(ctx_ref[...], wb_ref[:, width : 2 * width]) + misc[4:5]
    hid_ref[...] = hidden
    unit2, _ = normed(hidden)
    second_low = (unit2 * misc[5:6] + misc[6:7]).astype(BF16)
    rprob_ref[...] = masked_softmax(mm(second_low, wb_ref[:, 2 * width :]), experts)
    slots = disp_ref.shape[0]
    row = lax.broadcasted_iota(jnp.int32, (slots, tok_ref.shape[0]), 0)
    pick = (row == posrow_ref[0:1]) | (row == posrow_ref[1:2])
    disp_ref[...] = mm(pick.astype(F32).astype(BF16), second_low).astype(BF16)


def expert_kernel(
    dims, scal_ref, x_ref, up_ref, w_ref, misc_ref, rb_ref,
    out_ref, ing_ref, dw_ref, g_scr, acc_o, acc_i, dwh, dwr, drb,
):
    experts, tile, parts = dims
    slots, width = x_ref.shape
    share = (w_ref.shape[1] - 16) // 2
    c = pl.program_id(0)

    @pl.when(c == 0)
    def _():
        prob = masked_softmax(mm(x_ref[...], misc_ref[...]), experts)
        lane = lax.broadcasted_iota(jnp.int32, prob.shape, 1)
        mine = lane == ROUTER_COL + scal_ref[1]
        gate = jnp.sum(jnp.where(mine, prob, 0.0), axis=-1, keepdims=True)
        low = (gate * up_ref[...].astype(F32)).astype(BF16)
        g_scr[...] = low
        drb[...] = jnp.sum(low.astype(F32), axis=0, keepdims=True)
        acc_o[...] = jnp.broadcast_to(rb_ref[...], acc_o.shape)
        acc_i[...] = jnp.zeros_like(acc_i)

    wh = w_ref[0, :share]
    wr = w_ref[0, share : 2 * share]
    hb = w_ref[0, 2 * share : 2 * share + 16].astype(F32)[0:1, :share]
    dwh[...] = jnp.zeros_like(dwh)
    dwr[...] = jnp.zeros_like(dwr)

    def body(t, dhb):
        at = pl.ds(pl.multiple_of(t * tile, 16), tile)
        x = x_ref[at, :]
        g = g_scr[at, :]
        pre = mm(x, wh, NT) + hb
        square = pre * pre
        tanh = jnp.tanh(GELU_C * pre * (1.0 + GELU_A * square))
        half = 0.5 * (1.0 + tanh)
        act = (pre * half).astype(BF16)
        slope = half + (0.5 * GELU_C) * pre * (1.0 - tanh * tanh) * (1.0 + 3.0 * GELU_A * square)
        pg = (mm(g, wr, NT) * slope).astype(BF16)
        acc_o[at, :] += mm(act, wr)
        acc_i[at, :] += mm(pg, wh)
        dwr[...] += mm(act, g, TN)
        dwh[...] += mm(pg, x, TN)
        return dhb + jnp.sum(pg.astype(F32), axis=0, keepdims=True)

    dhb = lax.fori_loop(0, slots // tile, body, jnp.zeros((1, share), F32))
    dw_ref[0, :share] = dwh[...].astype(BF16)
    dw_ref[0, share : 2 * share] = dwr[...].astype(BF16)
    if share < width:
        dhb = jnp.concatenate([dhb, jnp.zeros((1, width - share), F32)], axis=1)
    row = lax.broadcasted_iota(jnp.int32, (16, width), 0)
    piece = width // parts
    for j in range(parts):

        @pl.when(c == j)
        def _():
            own = jnp.concatenate(
                [drb[:, j * piece : (j + 1) * piece], jnp.zeros((1, width - piece), F32)], axis=1
            )
            tail = jnp.where(row == 0, dhb, jnp.where(row == 1, own, 0.0))
            dw_ref[0, 2 * share :] = tail.astype(BF16)

    @pl.when(c == pl.num_programs(0) - 1)
    def _():
        out_ref[...] = acc_o[...].astype(BF16)
        ing_ref[...] = acc_i[...].astype(BF16)


def back_kernel(
    dims, scal_ref, tok_ref, up_ref, ret_ref, ing_ref, hid_ref, rprob_ref, poscol_ref,
    wa_ref, wb_ref, qkv_ref, probs_ref, ctx_ref,
    block_ref, tgrad_ref, ga_ref, gb_ref, dqkv_ref, cg_ref,
):
    images, patches, experts, blocks, slots_of = dims
    tokens, width = tok_ref.shape
    head_size = width // HEADS
    slots = ret_ref.shape[0]
    rows = ga_ref.shape[1]
    misc = wb_ref[:, 2 * width :].astype(F32).T
    hidden = hid_ref[...]
    up = up_ref[...].astype(F32)
    rprob = rprob_ref[...]
    lane = lax.broadcasted_iota(jnp.int32, (tokens, slots), 1)
    rlane = lax.broadcasted_iota(jnp.int32, (tokens, MISC), 1)
    pos = [poscol_ref[:, k : k + 1] for k in range(2)]
    mixed = hidden
    prob_grad = jnp.zeros((tokens, MISC), F32)
    for k in range(2):
        picked = mm((lane == pos[k]).astype(F32).astype(BF16), ret_ref[...])
        hot = (rlane == ROUTER_COL + poscol_ref[:, 2 + k : 3 + k]) & (pos[k] >= 0)
        gate = jnp.sum(jnp.where(hot, rprob, 0.0), axis=-1, keepdims=True)
        mixed = mixed + gate * picked
        gate_grad = jnp.sum(up * picked, axis=-1, keepdims=True)
        prob_grad = prob_grad + jnp.where(hot, gate_grad, 0.0)
    block_ref[...] = mixed.astype(BF16)
    logit_low = (
        rprob * (prob_grad - jnp.sum(prob_grad * rprob, axis=-1, keepdims=True))
    ).astype(BF16)
    unit2, rstd2 = normed(hidden)
    second_low = (unit2 * misc[5:6] + misc[6:7]).astype(BF16)
    router_grad = mm(second_low, logit_low, TN)
    either = ((lane == pos[0]) | (lane == pos[1])).astype(F32).astype(BF16)
    second_grad = mm(logit_low, wb_ref[:, 2 * width :], NT) + mm(either, ing_ref[...])
    gain2_grad = jnp.sum(second_grad * unit2, axis=0, keepdims=True)
    shift2_grad = jnp.sum(second_grad, axis=0, keepdims=True)
    residual = up + norm_back(second_grad, misc[5:6], unit2, rstd2)
    proj_in = residual.astype(BF16)
    proj_b_grad = jnp.sum(proj_in.astype(F32), axis=0, keepdims=True)
    proj_w_grad = mm(ctx_ref[...], proj_in, TN)
    cg_ref[...] = mm(proj_in, wb_ref[:, width : 2 * width], NT).astype(BF16)
    scale = 1.0 / math.sqrt(head_size)
    quad_width = QUAD * head_size
    for i in range(images):
        at = slice(i * patches, (i + 1) * patches)
        for quad in range(HEADS // QUAD):
            lo = quad * quad_width
            q = qkv_ref[at, lo : lo + quad_width]
            k = qkv_ref[at, width + lo : width + lo + quad_width]
            v = qkv_ref[at, 2 * width + lo : 2 * width + lo + quad_width]
            cg = head_stack(cg_ref[at, lo : lo + quad_width], head_size)
            probs_low = probs_ref[i * (HEADS // QUAD) + quad]
            probs = probs_low.astype(F32)
            weight_grad = mm(cg, v, NT)
            value_grad = mm(probs_low, cg, TN)
            score_grad = (
                probs * (weight_grad - jnp.sum(weight_grad * probs, axis=-1, keepdims=True))
            ).astype(BF16)
            query_grad = head_merge(mm(score_grad, k), patches, head_size) * scale
            key_grad = mm(score_grad, head_stack(q, head_size), TN) * scale
            dqkv_ref[at, lo : lo + quad_width] = query_grad.astype(BF16)
            dqkv_ref[at, width + lo : width + lo + quad_width] = key_grad.astype(BF16)
            dqkv_ref[at, 2 * width + lo : 2 * width + lo + quad_width] = value_grad.astype(BF16)
    unit1, rstd1 = normed(tok_ref[...].astype(F32))
    first_low = (unit1 * misc[0:1] + misc[1:2]).astype(BF16)
    query_b_grad = jnp.sum(dqkv_ref[:, :width].astype(F32), axis=0, keepdims=True)
    value_b_grad = jnp.sum(dqkv_ref[:, 2 * width :].astype(F32), axis=0, keepdims=True)
    first_grad = mm(dqkv_ref[:, : 2 * width], wa_ref[...], NT) + mm(
        dqkv_ref[:, 2 * width :], wb_ref[:, :width], NT
    )
    gain1_grad = jnp.sum(first_grad * unit1, axis=0, keepdims=True)
    shift1_grad = jnp.sum(first_grad, axis=0, keepdims=True)
    tgrad_ref[...] = (residual + norm_back(first_grad, misc[0:1], unit1, rstd1)).astype(BF16)
    small = jnp.concatenate(
        [
            gain1_grad, shift1_grad, query_b_grad, value_b_grad,
            proj_b_grad, gain2_grad, shift2_grad, jnp.zeros((MISC - 7, width), F32),
        ],
        axis=0,
    )
    tail = (router_grad + small.T).astype(BF16)
    first_t = first_low.astype(F32).T.astype(BF16)
    da = mm(first_t, dqkv_ref[:, : 2 * width]).astype(BF16)
    dv = mm(first_t, dqkv_ref[:, 2 * width :]).astype(BF16)
    db = jnp.concatenate([dv, proj_w_grad.astype(BF16), tail], axis=1)
    for r in range(blocks):
        ga_ref[slots_of[0][r] ^ scal_ref[2]] = da[r * rows : (r + 1) * rows]
        gb_ref[slots_of[1][r] ^ scal_ref[3]] = db[r * rows : (r + 1) * rows]


def flip(x, stage):
    axis, size, bit = stage
    return lax.ppermute(x, axis, [(i, i ^ bit) for i in range(size)])


def bits_of(size):
    return [1 << b for b in range(size.bit_length() - 1)]


def plan(dp, ex):
    dp_stages = [("dp", dp, b) for b in reversed(bits_of(dp))]
    chip = [("expert", ex, b) for b in bits_of(ex)[1:]]
    half = len(chip) // 2
    core = ("expert", ex, 1)
    return dp_stages, chip, chip[half:] + chip[:half], core


def code_of(stage, ex):
    axis, _, bit = stage
    return bit * ex if axis == "dp" else bit


def slot_codes(stages, ex):
    rel = [0]
    for stage in stages:
        rel = rel + [r ^ code_of(stage, ex) for r in rel]
    return rel


def on_device(
    tokens, patch_counts, expert_ids, priority, out_grad, first_gain, first_shift, qkv_weight,
    query_bias, value_bias, proj_weight, proj_bias, second_gain, second_shift, router_weight,
    hidden_weight, hidden_bias, return_weight, return_bias, *, dp, ex,
):
    images, patches, width = tokens.shape
    count = images * patches
    top = expert_ids.shape[2]
    experts = router_weight.shape[1]
    capacity = (count * top * 105 + 100 * experts - 1) // (100 * experts)
    slots = experts * capacity
    devices = dp * ex
    share_rows = qkv_weight.shape[0]
    ff_share = hidden_weight.shape[1]
    dp_at = lax.axis_index("dp")
    ex_at = lax.axis_index("expert")
    me = dp_at * ex + ex_at

    tail = jnp.zeros((16, width), BF16)
    tail = tail.at[0, :ff_share].set(hidden_bias[0]).at[1, : width // dp].set(return_bias[0])
    pack = jnp.concatenate([hidden_weight[0], return_weight[0], tail], axis=0)
    expert_w = lax.all_gather(pack, "dp", axis=0)
    return_add = expert_w[:, 2 * ff_share + 1, : width // dp].reshape(1, width).astype(F32)

    dp_stages, chip_a, chip_b, core = plan(dp, ex)
    small = jnp.stack(
        [first_gain, first_shift, query_bias, value_bias, proj_bias, second_gain, second_shift],
        axis=1,
    )
    small = jnp.concatenate(
        [
            small,
            jnp.zeros((share_rows, ROUTER_COL - 7), BF16),
            router_weight,
            jnp.zeros((share_rows, MISC - ROUTER_COL - experts), BF16),
        ],
        axis=1,
    )
    packed = jnp.concatenate([qkv_weight, proj_weight, small], axis=1)[None]
    for stage in dp_stages:
        packed = jnp.concatenate([packed, flip(packed, stage)], axis=0)
    parts = [packed[..., : 2 * width], packed[..., 2 * width :]]
    for stages in zip(chip_a, chip_b):
        parts = [jnp.concatenate([p, flip(p, s)], axis=0) for p, s in zip(parts, stages)]
    parts = [jnp.concatenate([p, flip(p, core)], axis=0) for p in parts]
    orders = [dp_stages + list(c) + [core] for c in (chip_a, chip_b)]
    rels = [slot_codes(o, ex) for o in orders]
    in_kernel = share_rows % 16 == 0
    if in_kernel:
        blocks, block_rows, gather_at = devices, share_rows, me
        kernel_rels = rels
    else:
        blocks, block_rows, gather_at = width // 16, 16, jnp.int32(0)
        kernel_rels = [list(range(blocks))] * 2
        back = [np.argsort(np.array(r)) for r in rels]
        parts = [
            p[jnp.asarray(b)[jnp.arange(devices) ^ me]].reshape(blocks, 16, -1)
            for p, b in zip(parts, back)
        ]

    valid = (
        lax.broadcasted_iota(jnp.int32, (images, patches), 1) < patch_counts[:, None]
    ).reshape(count)
    choices = expert_ids.reshape(count, top)
    rank = priority[0]
    earlier = (rank[:, None] > rank[None, :]).astype(BF16)
    iota = jnp.arange(experts, dtype=jnp.int32)
    hot = choices[:, :, None] == iota[None, None, :]
    hot_valid = (hot & valid[:, None, None]).astype(BF16).reshape(count, top * experts)
    before = jnp.dot(earlier, hot_valid, preferred_element_type=F32).reshape(count, top, experts)
    totals = jnp.sum(hot_valid.astype(F32), axis=0).reshape(top, experts)
    start = jnp.cumsum(totals, axis=0) - totals
    slot = jnp.sum(jnp.where(hot, before + start[None], 0.0), axis=-1).astype(jnp.int32)
    kept = valid[:, None] & (slot < capacity)
    pos = jnp.where(kept, choices * capacity + slot, -1)
    pos_row = pos.T
    pos_col = jnp.concatenate([pos, choices], axis=1)

    pick = jnp.zeros((slots, count), jnp.bool_)
    slot_iota = lax.broadcasted_iota(jnp.int32, (slots, count), 0)
    for k in range(top):
        pick = pick | (slot_iota == pos_row[k][None, :])
    up = out_grad.reshape(count, width)
    up_slots = jnp.dot(pick.astype(BF16), up, preferred_element_type=F32).astype(BF16)

    def exchange(x):
        x = lax.all_to_all(
            x.reshape(experts, capacity, width), "expert", split_axis=0, concat_axis=0, tiled=True
        )
        return x.reshape(slots, width)

    up_arrived = exchange(up_slots)

    tables = [np.argsort(np.array(r)) for r in rels]
    if in_kernel:
        send_at = [jnp.asarray(t, jnp.int32)[me] for t in tables]
        kernel_slots = [[int(v) for v in t] for t in tables]
    else:
        send_at = [jnp.int32(0), jnp.int32(0)]
        kernel_slots = [list(range(blocks))] * 2
    scal = jnp.stack([gather_at, ex_at, send_at[0], send_at[1]]).astype(jnp.int32)

    tok = tokens.reshape(count, width)
    pairs = images * (HEADS // QUAD)
    wa, wb, qkv, probs, ctx, hidden, rprob, dispatch = pl.pallas_call(
        functools.partial(front_kernel, (images, patches, experts, blocks, kernel_rels)),
        out_shape=(
            jax.ShapeDtypeStruct((width, 2 * width), BF16),
            jax.ShapeDtypeStruct((width, 2 * width + MISC), BF16),
            jax.ShapeDtypeStruct((count, 3 * width), BF16),
            jax.ShapeDtypeStruct((pairs, QUAD * patches, patches), BF16),
            jax.ShapeDtypeStruct((count, width), BF16),
            jax.ShapeDtypeStruct((count, width), F32),
            jax.ShapeDtypeStruct((count, MISC), F32),
            jax.ShapeDtypeStruct((slots, width), BF16),
        ),
        in_specs=[smem(), smem()] + [vmem()] * 4,
        out_specs=(vmem(),) * 8,
        compiler_params=params(),
        name="front",
    )(scal, patch_counts, tok, parts[0], parts[1], pos_row)

    arrived = exchange(dispatch)

    tile = 304 if slots % 304 == 0 else slots
    whole = lambda shape: pl.BlockSpec(shape, lambda c: (0,) * len(shape))
    pack_rows = pack.shape[0]
    expert_out, in_grad, dw = pl.pallas_call(
        functools.partial(expert_kernel, (experts, tile, dp)),
        grid=(dp,),
        out_shape=(
            jax.ShapeDtypeStruct((slots, width), BF16),
            jax.ShapeDtypeStruct((slots, width), BF16),
            jax.ShapeDtypeStruct((dp, pack_rows, width), BF16),
        ),
        in_specs=[
            smem(),
            whole((slots, width)),
            whole((slots, width)),
            pl.BlockSpec((1, pack_rows, width), lambda c: (c, 0, 0)),
            whole((width, MISC)),
            whole((1, width)),
        ],
        out_specs=(
            whole((slots, width)),
            whole((slots, width)),
            pl.BlockSpec((1, pack_rows, width), lambda c: (c, 0, 0)),
        ),
        scratch_shapes=[
            pltpu.VMEM((slots, width), BF16),
            pltpu.VMEM((slots, width), F32),
            pltpu.VMEM((slots, width), F32),
            pltpu.VMEM((ff_share, width), F32),
            pltpu.VMEM((ff_share, width), F32),
            pltpu.VMEM((1, width), F32),
        ],
        compiler_params=params(),
        name="experts",
    )(scal, arrived, up_arrived, expert_w, wb[:, 2 * width :], return_add)

    returned = exchange(expert_out)
    grad_back = exchange(in_grad)
    dw_sum = lax.psum_scatter(dw, "dp", scatter_dimension=0, tiled=False).astype(F32)

    block_out, tokens_grad, da, db = pl.pallas_call(
        functools.partial(back_kernel, (images, patches, experts, blocks, kernel_slots)),
        out_shape=(
            jax.ShapeDtypeStruct((count, width), BF16),
            jax.ShapeDtypeStruct((count, width), BF16),
            jax.ShapeDtypeStruct((blocks, block_rows, 2 * width), BF16),
            jax.ShapeDtypeStruct((blocks, block_rows, 2 * width + MISC), BF16),
        ),
        in_specs=[smem()] + [vmem()] * 12,
        out_specs=(vmem(),) * 4,
        scratch_shapes=[pltpu.VMEM((count, 3 * width), BF16), pltpu.VMEM((count, width), BF16)],
        compiler_params=params(),
        name="back",
    )(scal, tok, up, returned, grad_back, hidden, rprob, pos_col, wa, wb, qkv, probs, ctx)

    sums = [da, db]
    if not in_kernel:
        sums = [
            s.reshape(devices, share_rows, -1)[jnp.asarray(np.array(r)) ^ me]
            for s, r in zip(sums, rels)
        ]
    for stages in zip(*[list(reversed(o)) for o in orders]):
        halves = [s.reshape(2, -1, *s.shape[1:]) for s in sums]
        came = [flip(h[1], st) for h, st in zip(halves, stages)]
        sums = [
            (h[0].astype(F32) + c.astype(F32)).astype(BF16) for h, c in zip(halves, came)
        ]
    ga, gb = [s[0].astype(F32) for s in sums]
    qkv_sum = jnp.concatenate([ga, gb[:, :width]], axis=1)
    proj_sum = gb[:, width : 2 * width]
    vec = [gb[:, 2 * width + j] for j in range(7)]
    router_sum = gb[:, 2 * width + ROUTER_COL : 2 * width + ROUTER_COL + experts]
    return (
        block_out.reshape(tokens.shape),
        tokens_grad.reshape(tokens.shape),
        vec[0], vec[1], qkv_sum, vec[2], vec[3], proj_sum, vec[4], vec[5], vec[6], router_sum,
        dw_sum[:ff_share][None],
        dw_sum[2 * ff_share, :ff_share][None],
        dw_sum[ff_share : 2 * ff_share][None],
        dw_sum[2 * ff_share + 1, : width // dp][None],
    )


def solution(mesh):
    both, rows = P(("dp", "expert")), P(("dp", "expert"), None)
    cube = P(("dp", "expert"), None, None)
    weight, bias = P("expert", "dp", None), P("expert", "dp")
    in_specs = (
        cube, both, cube, rows, cube, both, both, rows, both, both, rows, both, both, both, rows,
        weight, bias, weight, bias,
    )
    out_specs = (
        cube, cube, both, both, rows, both, both, rows, both, both, both, rows,
        weight, bias, weight, bias,
    )
    return jax.shard_map(
        functools.partial(on_device, dp=mesh.shape["dp"], ex=mesh.shape["expert"]),
        mesh=mesh,
        in_specs=in_specs,
        out_specs=out_specs,
        check_vma=False,
    )
```

```python
import functools
import math

import jax
import jax.numpy as jnp
import numpy as np
from jax import lax
from jax.experimental import pallas as pl
from jax.experimental.pallas import tpu as pltpu
from jax.sharding import PartitionSpec as P

HEADS = 8
QUAD = 4
norm_eps = 1e-06
neg_large = -1e30
F32 = jnp.float32
BF16 = jnp.bfloat16
ROUTER_COL = 32
MISC = 128
VECTOR_ROWS = 16
HOP1_COST, HOP2_COST, HOP3_COST = 10, 40, 40
GELU_C = math.sqrt(2.0 / math.pi)
GELU_A = 0.044715

NN = (((1,), (0,)), ((), ()))
NT = (((1,), (1,)), ((), ()))
TN = (((0,), (0,)), ((), ()))


def mm(a, b, dims=NN):
    return lax.dot_general(a, b, dims, preferred_element_type=F32)


def params(mib=28):
    return pltpu.CompilerParams(vmem_limit_bytes=mib * 1024 * 1024)


def cost(us):
    return pl.CostEstimate(flops=us * 10**9, bytes_accessed=0, transcendentals=0)


def vmem():
    return pl.BlockSpec(memory_space=pltpu.VMEM)


def smem():
    return pl.BlockSpec(memory_space=pltpu.SMEM)


def anywhere():
    return pl.BlockSpec(memory_space=pl.ANY)


def hbm():
    return pl.BlockSpec(memory_space=pltpu.HBM)


def shape(dims, dtype=BF16):
    return jax.ShapeDtypeStruct(dims, dtype)


def one_hot(mask):
    return mask.astype(F32).astype(BF16)


def normed(values):
    center = values - jnp.mean(values, axis=-1, keepdims=True)
    rstd = lax.rsqrt(jnp.mean(center * center, axis=-1, keepdims=True) + norm_eps)
    return center * rstd, rstd


def norm_back(grad, gain, unit, rstd):
    q = grad * gain
    return rstd * (
        q
        - jnp.mean(q, axis=-1, keepdims=True)
        - unit * jnp.mean(q * unit, axis=-1, keepdims=True)
    )


def vectors_of(misc, rows):
    width = misc.shape[0]
    lane = lax.broadcasted_iota(jnp.int32, (rows, width), 1)
    row = lax.broadcasted_iota(jnp.int32, (rows, width), 0)
    spread = mm(misc[:, :rows], one_hot(lane % rows == row))
    lane = lax.broadcasted_iota(jnp.int32, (width, width), 1)
    row = lax.broadcasted_iota(jnp.int32, (width, width), 0)
    spread = jnp.where(lane // rows == row // rows, spread, 0.0)
    return jnp.sum(spread.reshape(width // rows, rows, width), axis=0)


def blocks_of(vectors):
    rows, width = vectors.shape
    spread = jnp.concatenate([vectors] * (width // rows), axis=0)
    lane = lax.broadcasted_iota(jnp.int32, (width, width), 1)
    row = lax.broadcasted_iota(jnp.int32, (width, width), 0)
    spread = jnp.where(lane // rows == row // rows, spread, 0.0).astype(BF16)
    row = lax.broadcasted_iota(jnp.int32, (width, MISC), 0)
    lane = lax.broadcasted_iota(jnp.int32, (width, MISC), 1)
    return mm(spread, one_hot(row % rows == lane))


def masked_softmax(logits, experts):
    lane = lax.broadcasted_iota(jnp.int32, logits.shape, 1)
    inside = (lane >= ROUTER_COL) & (lane < ROUTER_COL + experts)
    logits = jnp.where(inside, logits, neg_large)
    raised = jnp.exp(logits - jnp.max(logits, axis=-1, keepdims=True))
    return raised / jnp.sum(raised, axis=-1, keepdims=True)


def head_stack(rows, head_size):
    lane = lax.broadcasted_iota(jnp.int32, rows.shape, 1) // head_size
    return jnp.concatenate(
        [jnp.where(lane == h, rows, jnp.zeros_like(rows)) for h in range(QUAD)], axis=0
    )


def head_merge(stacked, patches, head_size):
    lane = lax.broadcasted_iota(jnp.int32, (patches, stacked.shape[1]), 1) // head_size
    total = jnp.zeros((patches, stacked.shape[1]), F32)
    for h in range(QUAD):
        total = jnp.where(lane == h, stacked[h * patches : (h + 1) * patches], total)
    return total


def position(dp_ex, in_kernel):
    if not in_kernel:
        return jnp.int32(0)
    return lax.axis_index("dp") * dp_ex[1] + lax.axis_index("expert")


def front_kernel(dims, cnt_ref, tok_ref, meta_ref, *refs):
    images, patches, experts, dp_ex, in_kernel, rels = dims
    pieces, refs = refs[: len(rels)], refs[len(rels) :]
    (
        wa_ref, wb_ref, qkv_ref, probs_ref, ctx_ref, hid_ref, rprob_ref, disp_ref, misc_ref, col_ref,
    ) = refs
    width = tok_ref.shape[1]
    head_size = width // HEADS
    rows = pieces[0].shape[1]
    me = position(dp_ex, in_kernel)
    for ref, rel in zip(pieces, rels):
        for slot, code in enumerate(rel):
            at = pl.multiple_of((me ^ code) * rows, rows)
            wa_ref[pl.ds(at, rows), :] = ref[slot, :, : 2 * width]
            wb_ref[pl.ds(at, rows), :] = ref[slot, :, 2 * width :]
    misc_ref[...] = wb_ref[:, 2 * width :]
    misc = vectors_of(wb_ref[:, 2 * width :], VECTOR_ROWS)
    x = tok_ref[...].astype(F32)
    unit, _ = normed(x)
    first_low = (unit * misc[0:1] + misc[1:2]).astype(BF16)
    qk = mm(first_low, wa_ref[...])
    qkv_ref[:, :width] = (qk[:, :width] + misc[2:3]).astype(BF16)
    qkv_ref[:, width : 2 * width] = qk[:, width:].astype(BF16)
    qkv_ref[:, 2 * width :] = (mm(first_low, wb_ref[:, :width]) + misc[3:4]).astype(BF16)
    scale = 1.0 / math.sqrt(head_size)
    quad_width = QUAD * head_size
    for i in range(images):
        at = slice(i * patches, (i + 1) * patches)
        valid = lax.broadcasted_iota(jnp.int32, (QUAD * patches, patches), 1) < cnt_ref[i]
        for quad in range(HEADS // QUAD):
            lo = quad * quad_width
            q = qkv_ref[at, lo : lo + quad_width]
            k = qkv_ref[at, width + lo : width + lo + quad_width]
            v = qkv_ref[at, 2 * width + lo : 2 * width + lo + quad_width]
            scores = jnp.where(valid, mm(head_stack(q, head_size), k, NT) * scale, neg_large)
            raised = jnp.exp(scores - jnp.max(scores, axis=-1, keepdims=True))
            probs = (raised / jnp.sum(raised, axis=-1, keepdims=True)).astype(BF16)
            probs_ref[i * (HEADS // QUAD) + quad] = probs
            ctx = head_merge(mm(probs, v), patches, head_size)
            ctx_ref[at, lo : lo + quad_width] = ctx.astype(BF16)
    hidden = x + mm(ctx_ref[...], wb_ref[:, width : 2 * width]) + misc[4:5]
    hid_ref[...] = hidden
    unit2, _ = normed(hidden)
    second_low = (unit2 * misc[5:6] + misc[6:7]).astype(BF16)
    rprob_ref[...] = masked_softmax(mm(second_low, wb_ref[:, 2 * width :]), experts)
    slots = disp_ref.shape[0]
    count = tok_ref.shape[0]
    row = lax.broadcasted_iota(jnp.int32, (slots, count), 0)
    pick = (row == meta_ref[0:1, :count]) | (row == meta_ref[1:2, :count])
    disp_ref[...] = mm(one_hot(pick), second_low).astype(BF16)
    meta = meta_ref[...].astype(F32)
    meta = jnp.concatenate([meta, jnp.zeros((MISC - 8, meta.shape[1]), F32)], axis=0)
    col_ref[...] = meta.T[:count].astype(jnp.int32)


def fetch(options, parts, sem):
    def copies(source):
        return [
            pltpu.make_async_copy(source.at[pl.ds(at, dst.shape[0])], dst, sem) for at, dst in parts
        ]

    if len(options) == 1:
        for copy in copies(options[0]):
            copy.start()
    else:
        at = lax.axis_index("dp")
        inner = (at == 1) | (at == 2)

        @pl.when(jnp.logical_not(inner))
        def _():
            for copy in copies(options[0]):
                copy.start()

        @pl.when(inner)
        def _():
            for copy in copies(options[1]):
                copy.start()

    return copies(options[0])


def chunk_parts(share, wh, wr):
    return [(0, wh), (share, wr)]


def bias_kernel(start, *refs):
    sources, (tails, sem) = refs[:-2], refs[-2:]
    copies = [
        pltpu.make_async_copy(source.at[pl.ds(start, 16)], tails.at[pl.ds(c * 16, 16)], sem)
        for c, source in enumerate(sources)
    ]
    for copy in copies:
        copy.start()
    for copy in copies:
        copy.wait()


def biases(chunks, start, us):
    return pl.pallas_call(
        functools.partial(bias_kernel, start),
        out_shape=shape((len(chunks) * 16, chunks[0].shape[1])),
        in_specs=[anywhere()] * len(chunks),
        out_specs=vmem(),
        scratch_shapes=[pltpu.SemaphoreType.DMA],
        compiler_params=params(4),
        cost_estimate=cost(us),
        name="biases",
    )(*chunks)


def tail_of(places):
    tails = [ref[at : at + 16].astype(F32) for ref, at in places]
    if len(tails) == 1:
        return tails[0]
    at = lax.axis_index("dp")
    return jnp.where((at == 1) | (at == 2), tails[1], tails[0])


def expert_pair(x, g, wh, wr, hb):
    pre = mm(x, wh, NT) + hb
    square = pre * pre
    half = 0.5 + 0.5 * jnp.tanh(pre * (GELU_C + (GELU_C * GELU_A) * square))
    act = (pre * half).astype(BF16)
    slope = half * (
        1.0 + (1.0 - half) * (pre * (2.0 * GELU_C + (6.0 * GELU_C * GELU_A) * square))
    )
    pg = (mm(g, wr, NT) * slope).astype(BF16)
    return act, pg


def hidden_bias_of(tail, share):
    return tail[0:1, :share]


def place_of(role, on_line):
    if not on_line:
        return role
    at = lax.axis_index("dp")
    inner = (at == 1) | (at == 2)
    mirror = 3 - at
    step = jnp.where(at < 2, 1, -1)
    return (
        jnp.where(inner, mirror, at + 2 * step),
        jnp.where(inner, mirror + step, at + step),
        at,
        jnp.where(inner, at - step, mirror),
    )[role]


def return_bias_of(tail, role, width):
    piece = width // 4
    row = tail[1:2]
    own = jnp.concatenate([row[:, :piece]] * 4, axis=1)
    lane = lax.broadcasted_iota(jnp.int32, (1, width), 1) // piece
    return jnp.where(lane == place_of(role, True), own, 0.0)


def weight_grads(x, g, act, pg, d_ref):
    share, width = act.shape[1], x.shape[1]
    row = lax.broadcasted_iota(jnp.int32, (16, width), 0)
    d_ref[:share] = mm(act, g, TN).astype(BF16)
    d_ref[share : 2 * share] = mm(pg, x, TN).astype(BF16)
    bias = jnp.sum(pg.astype(F32), axis=0, keepdims=True)
    if share < width:
        bias = jnp.concatenate([bias, jnp.zeros((1, width - share), F32)], axis=1)
    sums = jnp.sum(g.astype(F32), axis=0, keepdims=True)
    d_ref[2 * share :] = jnp.where(row == 0, bias, jnp.where(row == 1, sums, 0.0)).astype(BF16)


def early_expert_kernel(n_opts, experts, on_line, rows_of, *refs):
    options = []
    for n in n_opts:
        options.append(refs[:n])
        refs = refs[n:]
    chunks = len(n_opts)
    tails, refs = refs[:2], refs[2:]
    tails = [tail_of([(tails[i], r) for i, r in role]) for role in rows_of]
    x_ref, up_ref, misc_ref, rb_ref, g_ref, o_ref, i_ref, d_ref = refs[:8]
    acts_ref, pgs_ref, wh_ref, wr_ref, d_scr, sems, d_sems = refs[8:]
    share, width = wh_ref.shape[0] // chunks, x_ref.shape[1]
    rows = [slice(c * share, (c + 1) * share) for c in range(chunks)]
    waits = [
        fetch(
            options[c],
            chunk_parts(
                share, wh_ref.at[pl.ds(c * share, share)], wr_ref.at[pl.ds(c * share, share)]
            ),
            sems.at[c],
        )
        for c in range(chunks)
    ]
    prob = masked_softmax(mm(x_ref[...], misc_ref[...]), experts)
    lane = lax.broadcasted_iota(jnp.int32, prob.shape, 1)
    mine = lane == ROUTER_COL + lax.axis_index("expert")
    gate = jnp.sum(jnp.where(mine, prob, 0.0), axis=-1, keepdims=True)
    g_ref[...] = (gate * up_ref[...].astype(F32)).astype(BF16)
    bias = rb_ref[...]
    copies = []
    for c in reversed(range(chunks)):
        for copy in waits[c]:
            copy.wait()
        act, pg = expert_pair(
            x_ref[...], g_ref[...], wh_ref[rows[c]], wr_ref[rows[c]], hidden_bias_of(tails[c], share)
        )
        acts_ref[:, rows[c]] = act
        pgs_ref[:, rows[c]] = pg
        weight_grads(x_ref[...], g_ref[...], act, pg, d_scr.at[c])
        copies.append(
            pltpu.make_async_copy(d_scr.at[c], d_ref.at[place_of(c, on_line)], d_sems.at[c])
        )
        copies[-1].start()
        if on_line:
            bias = bias + return_bias_of(tails[c], c, width)
    o_ref[...] = mm(acts_ref[...], wr_ref[...]) + bias
    i_ref[...] = mm(pgs_ref[...], wh_ref[...])
    for copy in copies:
        copy.wait()


def last_expert_kernel(n_opt, dims, rows, *refs):
    experts, capacity, stride, on_line = dims
    options, refs = refs[:n_opt], refs[n_opt:]
    tails, refs = refs[:2], refs[2:]
    tail = tail_of([(tails[i], r) for i, r in rows])
    (
        x_ref, g_ref, up_ref, o_ref, i_ref, d_in,
        out_hbm, ing_hbm, d_ref, wh_ref, wr_ref, out_ref, ing_ref, d_scr, sem,
    ) = refs
    del d_in
    slots, width = x_ref.shape
    share = wh_ref.shape[0]
    for copy in fetch(options, chunk_parts(share, wh_ref, wr_ref), sem):
        copy.wait()
    act, pg = expert_pair(
        x_ref[...], g_ref[...], wh_ref[...], wr_ref[...], hidden_bias_of(tail, share)
    )
    ing_ref[...] = (i_ref[...] + mm(pg, wh_ref[...])).astype(BF16)
    out = o_ref[...] + mm(act, wr_ref[...])
    if on_line:
        out = out + return_bias_of(tail, 3, width)
    out = out.astype(BF16)
    out_ref[...] = out
    out_copy = pltpu.make_async_copy(out_ref, out_hbm, sem)
    out_copy.start()
    product = jnp.sum(up_ref[...].astype(F32) * out.astype(F32), axis=-1, keepdims=True)
    lane = lax.broadcasted_iota(jnp.int32, (stride, width), 1)
    row = lax.broadcasted_iota(jnp.int32, (stride, width), 0)
    tail_row = lax.broadcasted_iota(jnp.int32, (16, width), 0) + (stride - 16)
    for s in range(experts):
        own = product[s * stride : (s + 1) * stride]
        line = jnp.sum(jnp.where(lane == row, own, 0.0), axis=0, keepdims=True)
        high = line.astype(BF16).astype(F32)
        at = slice((s + 1) * stride - 16, (s + 1) * stride)
        end = ing_ref[at].astype(F32)
        end = jnp.where(tail_row == capacity, high, end)
        ing_ref[at] = jnp.where(tail_row == capacity + 1, line - high, end).astype(BF16)
    out_copy.wait()
    ing_copy = pltpu.make_async_copy(ing_ref, ing_hbm, sem)
    ing_copy.start()
    weight_grads(x_ref[...], g_ref[...], act, pg, d_scr)
    ing_copy.wait()
    last = place_of(3, True) if on_line else d_ref.shape[0] - 1
    pltpu.sync_copy(d_scr, d_ref.at[last])


def back_kernel(
    dims, tok_ref, up_ref, ing_ref, hid_ref, rprob_ref, poscol_ref,
    wa_ref, wb_ref, qkv_ref, probs_ref, ctx_ref,
    tgrad_ref, keep_ref, send_ref, dqkv_ref, cg_ref,
):
    images, patches, experts, capacity, stride, dp_ex, in_kernel = dims
    tokens, width = tok_ref.shape
    head_size = width // HEADS
    slots = ing_ref.shape[0]
    half, rows = keep_ref.shape[:2]
    misc = vectors_of(wb_ref[:, 2 * width :], VECTOR_ROWS)
    hidden = hid_ref[...]
    up = up_ref[...].astype(F32)
    rprob = rprob_ref[...]
    lane = lax.broadcasted_iota(jnp.int32, (stride, width), 1)
    row = lax.broadcasted_iota(jnp.int32, (stride, width), 0)
    mlane = lax.broadcasted_iota(jnp.int32, (stride, MISC), 1)
    columns = []
    for e in range(experts):
        tail = ing_ref[(e + 1) * stride - 16 : (e + 1) * stride].astype(F32)
        block = jnp.zeros((stride, MISC), F32)
        for part in range(2):
            at = capacity - stride + 16 + part
            line = tail[at : at + 1]
            column = jnp.sum(jnp.where(lane == row, line, 0.0), axis=-1, keepdims=True)
            block = jnp.where(mlane == ROUTER_COL * (1 + part) + e, column, block)
        columns.append(block.astype(BF16))
    gate_grads = jnp.concatenate(columns, axis=0)
    slane = lax.broadcasted_iota(jnp.int32, (tokens, slots), 1)
    either = one_hot((slane == poscol_ref[:, 0:1]) | (slane == poscol_ref[:, 1:2]))
    spread = mm(either, gate_grads)
    rlane = lax.broadcasted_iota(jnp.int32, (tokens, MISC), 1)
    inside = (rlane >= ROUTER_COL) & (rlane < ROUTER_COL + experts)
    prob_grad = jnp.where(inside, spread + pltpu.roll(spread, MISC - ROUTER_COL, 1), 0.0)
    logit_low = (
        rprob * (prob_grad - jnp.sum(prob_grad * rprob, axis=-1, keepdims=True))
    ).astype(BF16)
    unit2, rstd2 = normed(hidden)
    second_low = (unit2 * misc[5:6] + misc[6:7]).astype(BF16)
    router_grad = mm(second_low, logit_low, TN)
    second_grad = mm(logit_low, wb_ref[:, 2 * width :], NT) + mm(either, ing_ref[...])
    gain2_grad = jnp.sum(second_grad * unit2, axis=0, keepdims=True)
    shift2_grad = jnp.sum(second_grad, axis=0, keepdims=True)
    residual = up + norm_back(second_grad, misc[5:6], unit2, rstd2)
    proj_in = residual.astype(BF16)
    proj_b_grad = jnp.sum(proj_in.astype(F32), axis=0, keepdims=True)
    proj_w_grad = mm(ctx_ref[...], proj_in, TN)
    cg_ref[...] = mm(proj_in, wb_ref[:, width : 2 * width], NT).astype(BF16)
    scale = 1.0 / math.sqrt(head_size)
    quad_width = QUAD * head_size
    for i in range(images):
        at = slice(i * patches, (i + 1) * patches)
        for quad in range(HEADS // QUAD):
            lo = quad * quad_width
            q = qkv_ref[at, lo : lo + quad_width]
            k = qkv_ref[at, width + lo : width + lo + quad_width]
            v = qkv_ref[at, 2 * width + lo : 2 * width + lo + quad_width]
            cg = head_stack(cg_ref[at, lo : lo + quad_width], head_size)
            probs_low = probs_ref[i * (HEADS // QUAD) + quad]
            probs = probs_low.astype(F32)
            weight_grad = mm(cg, v, NT)
            value_grad = mm(probs_low, cg, TN)
            score_grad = (
                probs * (weight_grad - jnp.sum(weight_grad * probs, axis=-1, keepdims=True))
            ).astype(BF16)
            query_grad = head_merge(mm(score_grad, k), patches, head_size) * scale
            key_grad = mm(score_grad, head_stack(q, head_size), TN) * scale
            dqkv_ref[at, lo : lo + quad_width] = query_grad.astype(BF16)
            dqkv_ref[at, width + lo : width + lo + quad_width] = key_grad.astype(BF16)
            dqkv_ref[at, 2 * width + lo : 2 * width + lo + quad_width] = value_grad.astype(BF16)
    unit1, rstd1 = normed(tok_ref[...].astype(F32))
    first_low = (unit1 * misc[0:1] + misc[1:2]).astype(BF16)
    query_b_grad = jnp.sum(dqkv_ref[:, :width].astype(F32), axis=0, keepdims=True)
    value_b_grad = jnp.sum(dqkv_ref[:, 2 * width :].astype(F32), axis=0, keepdims=True)
    first_grad = mm(dqkv_ref[:, : 2 * width], wa_ref[...], NT) + mm(
        dqkv_ref[:, 2 * width :], wb_ref[:, :width], NT
    )
    gain1_grad = jnp.sum(first_grad * unit1, axis=0, keepdims=True)
    shift1_grad = jnp.sum(first_grad, axis=0, keepdims=True)
    tgrad_ref[...] = (residual + norm_back(first_grad, misc[0:1], unit1, rstd1)).astype(BF16)
    small = jnp.concatenate(
        [
            gain1_grad, shift1_grad, query_b_grad, value_b_grad,
            proj_b_grad, gain2_grad, shift2_grad, jnp.zeros((VECTOR_ROWS - 7, width), F32),
        ],
        axis=0,
    )
    tail = (router_grad + blocks_of(small)).astype(BF16)
    first_t = first_low.astype(F32).T.astype(BF16)
    da = mm(first_t, dqkv_ref[:, : 2 * width]).astype(BF16)
    dv = mm(first_t, dqkv_ref[:, 2 * width :]).astype(BF16)
    grads = jnp.concatenate([da, dv, proj_w_grad.astype(BF16), tail], axis=1)
    me = position(dp_ex, in_kernel)
    core = me % 2
    dp, ex = dp_ex
    for r in range(0, 2 * half, 2):
        even, odd = grads[r * rows : (r + 1) * rows], grads[(r + 1) * rows : (r + 2) * rows]
        rel = r ^ me
        to = (rel % ex) // 2 * dp + rel // ex if in_kernel else r // 2
        keep_ref[to] = jnp.where(core == 0, even, odd)
        send_ref[to] = jnp.where(core == 0, odd, even)


def mix_kernel(experts, hid_ref, ret_ref, rprob_ref, poscol_ref, block_ref):
    tokens, slots = hid_ref.shape[0], ret_ref.shape[0]
    rprob = rprob_ref[...]
    lane = lax.broadcasted_iota(jnp.int32, (tokens, slots), 1)
    rlane = lax.broadcasted_iota(jnp.int32, (tokens, MISC), 1)
    mixed = hid_ref[...]
    for k in range(2):
        pos = poscol_ref[:, k : k + 1]
        picked = mm(one_hot(lane == pos), ret_ref[...])
        hot = (rlane == ROUTER_COL + poscol_ref[:, 2 + k : 3 + k]) & (pos >= 0)
        mixed = mixed + jnp.sum(jnp.where(hot, rprob, 0.0), axis=-1, keepdims=True) * picked
    block_ref[...] = mixed.astype(BF16)


def turn(blocks, at):
    part = blocks[:, :, at : at + VECTOR_ROWS]
    return blocks.at[:, :, at : at + VECTOR_ROWS].set(jnp.swapaxes(part, 1, 2))


def flip(x, stage):
    axis, size, bit = stage
    return lax.ppermute(x, axis, [(i, i ^ bit) for i in range(size)])


def line_permute(x, pairs):
    return lax.ppermute(x, "dp", pairs)


INWARD, ACROSS, OUTWARD = [(0, 1), (3, 2)], [(1, 2), (2, 1)], [(1, 0), (2, 3)]
SIDE = INWARD + OUTWARD


def add(a, b):
    return (a.astype(F32) + b.astype(F32)).astype(BF16)


def on_device(
    tokens, patch_counts, expert_ids, priority, out_grad, first_gain, first_shift, qkv_weight,
    query_bias, value_bias, proj_weight, proj_bias, second_gain, second_shift, router_weight,
    hidden_weight, hidden_bias, return_weight, return_bias, *, dp, ex,
):
    images, patches, width = tokens.shape
    count = images * patches
    top = expert_ids.shape[2]
    experts = router_weight.shape[1]
    capacity = (count * top * 105 + 100 * experts - 1) // (100 * experts)
    stride = (capacity + 2 + 15) // 16 * 16
    slots = experts * stride
    devices = dp * ex
    share_rows = qkv_weight.shape[0]
    ff_share = hidden_weight.shape[1]
    piece = width // dp
    dp_at = lax.axis_index("dp")
    ex_at = lax.axis_index("expert")
    me = dp_at * ex + ex_at
    in_kernel = share_rows % 16 == 0
    on_line = dp == 4

    vectors = [
        first_gain, first_shift, query_bias, value_bias, proj_bias, second_gain, second_shift,
    ]
    small = jnp.pad(router_weight, ((0, 0), (ROUTER_COL, MISC - ROUTER_COL - experts)))
    for j, vector in enumerate(vectors):
        if in_kernel:
            at = ((j, share_rows - 1 - j), (0, MISC - share_rows))
            small = small + jnp.pad(vector[None], at)
        else:
            small = small + jnp.pad(vector[:, None], ((0, 0), (j, MISC - 1 - j)))
    packed = jnp.concatenate([qkv_weight, proj_weight, small], axis=1)[None]
    tail = jnp.pad(hidden_bias, ((0, 15), (0, width - ff_share)))
    tail = tail + jnp.pad(return_bias, ((1, 14), (0, width - piece)))
    own = jnp.concatenate([hidden_weight[0], return_weight[0], tail], axis=0)
    if on_line:
        own, packed = lax.optimization_barrier((own, packed))
        side = line_permute(own, SIDE)
        across1 = line_permute(own, ACROSS)
    else:
        expert_w = lax.all_gather(own, "dp", axis=0)

    packed = jnp.concatenate([flip(packed, ("dp", dp, k)) if k else packed for k in range(dp)], axis=0)
    chips = ex // 2
    core = ("expert", ex, 1)

    if in_kernel:
        packed, patch_counts, expert_ids, priority = lax.optimization_barrier(
            (packed, patch_counts, expert_ids, priority)
        )
    valid = (
        lax.broadcasted_iota(jnp.int32, (images, patches), 1) < patch_counts[:, None]
    ).reshape(count)
    choices = expert_ids.reshape(count, top)
    rank = priority[0]
    earlier = (rank[:, None] > rank[None, :]).astype(BF16)
    iota = jnp.arange(experts, dtype=jnp.int32)
    hot = choices[:, :, None] == iota[None, None, :]
    hot_valid = (hot & valid[:, None, None]).astype(BF16).reshape(count, top * experts)
    before = jnp.dot(earlier, hot_valid, preferred_element_type=F32).reshape(count, top, experts)
    totals = jnp.sum(hot_valid.astype(F32), axis=0).reshape(top, experts)
    start = jnp.cumsum(totals, axis=0) - totals
    slot = jnp.sum(jnp.where(hot, before + start[None], 0.0), axis=-1).astype(jnp.int32)
    kept = valid[:, None] & (slot < capacity)
    pos = jnp.where(kept, choices * stride + slot, -1)
    pos_row = pos.T
    meta = jnp.concatenate([pos_row, choices.T], axis=0)
    meta = jnp.pad(meta, ((0, 4), (0, -count % MISC)))

    pick = jnp.zeros((slots, count), jnp.bool_)
    slot_iota = lax.broadcasted_iota(jnp.int32, (slots, count), 0)
    for k in range(top):
        pick = pick | (slot_iota == pos_row[k][None, :])
    up = out_grad.reshape(count, width)
    up_slots = jnp.dot(pick.astype(BF16), up, preferred_element_type=F32).astype(BF16)

    pieces = [flip(packed, ("expert", ex, 2 * j)) if j else packed for j in range(chips)]
    pieces += [flip(p, core) for p in pieces]
    rels = [[k * ex + 2 * j + b for k in range(dp)] for b in range(2) for j in range(chips)]
    if in_kernel:
        block_rows = share_rows
        kernel_rels = rels
    else:
        blocks, block_rows = width // 16, 16
        kernel_rels = [list(range(blocks))]
        at = np.argsort(np.array(sum(rels, [])))
        whole = jnp.concatenate(pieces, axis=0)[jnp.asarray(at)[jnp.arange(devices) ^ me]]
        pieces = [turn(whole.reshape(blocks, 16, -1), 4 * width)]

    def exchange(x):
        x = lax.all_to_all(
            x.reshape(experts, stride, width), "expert", split_axis=0, concat_axis=0, tiled=True
        )
        return x.reshape(slots, width)

    up_arrived = exchange(up_slots)

    tok = tokens.reshape(count, width)
    pairs = images * (HEADS // QUAD)
    if on_line:
        tails = biases([side, across1, own], 2 * ff_share, HOP1_COST)
        pieces, tails, side, across1 = lax.optimization_barrier((pieces, tails, side, across1))
        across2 = line_permute(side, ACROSS)
        out2 = line_permute(across1, OUTWARD)
    wa, wb, qkv, probs, ctx, hidden, rprob, dispatch, misc, pos_col = pl.pallas_call(
        functools.partial(
            front_kernel, (images, patches, experts, (dp, ex), in_kernel, kernel_rels)
        ),
        out_shape=(
            shape((width, 2 * width)),
            shape((width, 2 * width + MISC)),
            shape((count, 3 * width)),
            shape((pairs, QUAD * patches, patches)),
            shape((count, width)),
            shape((count, width), F32),
            shape((count, MISC), F32),
            shape((slots, width)),
            shape((width, MISC)),
            shape((count, MISC), jnp.int32),
        ),
        in_specs=[smem()] + [vmem()] * (2 + len(pieces)),
        out_specs=(vmem(),) * 10,
        compiler_params=params(56),
        cost_estimate=cost(0),
        name="front",
    )(patch_counts, tok, meta, *pieces)

    dispatch, up_arrived = lax.optimization_barrier((dispatch, up_arrived))
    arrived = exchange(dispatch)
    if on_line:
        chunks = [(out2, across1), (side, across2), (own,)]
        tails2 = biases([across2, out2], 2 * ff_share, HOP2_COST)
        out3 = line_permute(across2, OUTWARD)
        last = (out3, side)
        tails3 = biases([out3], 2 * ff_share, HOP3_COST)
        early_tails, last_tails = (tails, tails2), (tails, tails3)
        rows_of = [((1, 16), (0, 16)), ((0, 0), (1, 0)), ((0, 32),), ((1, 0), (0, 0))]
        return_add = jnp.zeros((1, width), F32)
    else:
        chunks = [(expert_w[c],) for c in range(dp)]
        chunks, last = chunks[:-1], chunks[-1]
        tails = expert_w[:, 2 * ff_share :].reshape(dp * 16, width)
        early_tails = last_tails = (tails, tails)
        rows_of = [((0, c * 16),) for c in range(dp)]
        return_add = expert_w[:, 2 * ff_share + 1, :piece].reshape(1, width).astype(F32)

    sem = pltpu.SemaphoreType.DMA
    early = dp - 1
    options = [len(c) for c in chunks]
    wide = shape((slots, width))
    matrix = pltpu.VMEM((ff_share, width), BF16)
    grad_rows = 2 * ff_share + 16
    grad = pltpu.VMEM((grad_rows, width), BF16)
    g, part_out, part_in, d_all = pl.pallas_call(
        functools.partial(early_expert_kernel, options, experts, on_line, rows_of[:-1]),
        out_shape=(wide,)
        + (shape((slots, width), F32),) * 2
        + (shape((dp, grad_rows, width)),),
        in_specs=[anywhere()] * sum(options) + [vmem()] * 6,
        out_specs=(vmem(),) * 3 + (hbm(),),
        scratch_shapes=[pltpu.VMEM((slots, early * ff_share), BF16)] * 2
        + [pltpu.VMEM((early * ff_share, width), BF16)] * 2
        + [pltpu.VMEM((early, grad_rows, width), BF16)]
        + [pltpu.SemaphoreType.DMA((early,))] * 2,
        compiler_params=params(40),
        cost_estimate=cost(0),
        name="experts_early",
    )(*sum(chunks, ()), *early_tails, arrived, up_arrived, misc, return_add)
    operands = (*last, *last_tails, arrived, g, up_arrived, part_out, part_in, d_all)
    expert_out, in_grad, d_all = pl.pallas_call(
        functools.partial(
            last_expert_kernel, len(last), (experts, capacity, stride, on_line), rows_of[-1]
        ),
        out_shape=(wide, wide, shape((dp, grad_rows, width))),
        in_specs=[anywhere()] * len(last) + [vmem()] * 7 + [hbm()],
        out_specs=(hbm(),) * 3,
        scratch_shapes=[matrix, matrix] + [pltpu.VMEM((slots, width), BF16)] * 2 + [grad, sem],
        input_output_aliases={len(operands) - 1: 2},
        compiler_params=params(32),
        cost_estimate=cost(0),
        name="experts_last",
    )(*operands)
    grad_back = exchange(in_grad)
    d_sum = lax.psum_scatter(d_all, "dp", scatter_dimension=0, tiled=False)

    half = width // block_rows // 2
    tokens_grad, keep, send = pl.pallas_call(
        functools.partial(
            back_kernel, (images, patches, experts, capacity, stride, (dp, ex), in_kernel)
        ),
        out_shape=(shape((count, width)),) + (shape((half, block_rows, 4 * width + MISC)),) * 2,
        in_specs=[vmem()] * 11,
        out_specs=(vmem(),) * 3,
        scratch_shapes=[pltpu.VMEM((count, 3 * width), BF16), pltpu.VMEM((count, width), BF16)],
        compiler_params=params(56),
        cost_estimate=cost(0),
        name="back",
    )(tok, up, grad_back, hidden, rprob, pos_col, wa, wb, qkv, probs, ctx)

    if not in_kernel:
        whole = jnp.stack([keep, send], axis=1).reshape(2 * half, block_rows, -1)
        whole = turn(whole, 4 * width).reshape(devices, share_rows, -1)
        whole = whole[jnp.asarray(np.array(sum(rels, []))) ^ me]
        keep, send = whole[: devices // 2], whole[devices // 2 :]
    came = flip(send, core)
    came, expert_out = lax.optimization_barrier((came, expert_out))
    returned = exchange(expert_out)
    parts = [add(keep[j * dp : (j + 1) * dp], came[j * dp : (j + 1) * dp]) for j in range(chips)]
    moved = [flip(parts[j], ("expert", ex, 2 * j)) for j in range(1, chips)]
    total = functools.reduce(lambda t, m: t + m.astype(F32), moved, parts[0].astype(F32)).astype(BF16)
    block_out = pl.pallas_call(
        functools.partial(mix_kernel, experts),
        out_shape=shape((count, width)),
        in_specs=[vmem()] * 4,
        out_specs=vmem(),
        compiler_params=params(56),
        cost_estimate=cost(0),
        name="mix",
    )(hidden, returned, rprob, pos_col)
    final = functools.reduce(
        lambda t, k: t + flip(total[k], ("dp", dp, k)).astype(F32), range(1, dp), total[0].astype(F32)
    )
    qkv_sum = final[:, : 3 * width]
    proj_sum = final[:, 3 * width : 4 * width]
    if in_kernel:
        vec = [final[j, 4 * width : 4 * width + share_rows] for j in range(7)]
    else:
        vec = [final[:, 4 * width + j] for j in range(7)]
    router_sum = final[:, 4 * width + ROUTER_COL : 4 * width + ROUTER_COL + experts]
    return_bias_sum = lax.dynamic_slice(d_sum, (2 * ff_share + 1, dp_at * piece), (1, piece))
    return (
        block_out.reshape(tokens.shape),
        tokens_grad.reshape(tokens.shape),
        vec[0], vec[1], qkv_sum, vec[2], vec[3], proj_sum, vec[4], vec[5], vec[6], router_sum,
        d_sum[ff_share : 2 * ff_share].astype(F32)[None],
        d_sum[2 * ff_share, :ff_share].astype(F32)[None],
        d_sum[:ff_share].astype(F32)[None],
        return_bias_sum.astype(F32),
    )


def solution(mesh):
    both, rows = P(("dp", "expert")), P(("dp", "expert"), None)
    cube = P(("dp", "expert"), None, None)
    weight, bias = P("expert", "dp", None), P("expert", "dp")
    in_specs = (
        cube, both, cube, rows, cube, both, both, rows, both, both, rows, both, both, both, rows,
        weight, bias, weight, bias,
    )
    out_specs = (
        cube, cube, both, both, rows, both, both, rows, both, both, both, rows,
        weight, bias, weight, bias,
    )
    return jax.shard_map(
        functools.partial(on_device, dp=mesh.shape["dp"], ex=mesh.shape["expert"]),
        mesh=mesh,
        in_specs=in_specs,
        out_specs=out_specs,
        check_vma=False,
    )
```

```python
import functools
import math

import jax
import jax.numpy as jnp
import numpy as np
from jax import lax
from jax.experimental import pallas as pl
from jax.experimental.pallas import tpu as pltpu
from jax.sharding import PartitionSpec as P

HEADS = 8
QUAD = 4
norm_eps = 1e-06
neg_large = -1e30
F32 = jnp.float32
BF16 = jnp.bfloat16
ROUTER_COL = 32
MISC = 128
VECTOR_ROWS = 16
HOP1_COST, HOP2_COST, HOP3_COST = 10, 40, 40
GELU_C = math.sqrt(2.0 / math.pi)
GELU_A = 0.044715

NN = (((1,), (0,)), ((), ()))
NT = (((1,), (1,)), ((), ()))
TN = (((0,), (0,)), ((), ()))


def mm(a, b, dims=NN):
    return lax.dot_general(a, b, dims, preferred_element_type=F32)


def params(mib=28):
    return pltpu.CompilerParams(vmem_limit_bytes=mib * 1024 * 1024)


def cost(us):
    return pl.CostEstimate(flops=us * 10**9, bytes_accessed=0, transcendentals=0)


def vmem():
    return pl.BlockSpec(memory_space=pltpu.VMEM)


def smem():
    return pl.BlockSpec(memory_space=pltpu.SMEM)


def anywhere():
    return pl.BlockSpec(memory_space=pl.ANY)


def hbm():
    return pl.BlockSpec(memory_space=pltpu.HBM)


def load(pairs, sems, first=0):
    copies = [
        pltpu.make_async_copy(source, dst, sems.at[first + n]) for n, (source, dst) in enumerate(pairs)
    ]
    for copy in copies:
        copy.start()
    return copies


def wait_for(copies):
    for copy in copies:
        copy.wait()


def shape(dims, dtype=BF16):
    return jax.ShapeDtypeStruct(dims, dtype)


def one_hot(mask):
    return mask.astype(F32).astype(BF16)


def normed(values):
    center = values - jnp.mean(values, axis=-1, keepdims=True)
    rstd = lax.rsqrt(jnp.mean(center * center, axis=-1, keepdims=True) + norm_eps)
    return center * rstd, rstd


def norm_back(grad, gain, unit, rstd):
    q = grad * gain
    return rstd * (
        q
        - jnp.mean(q, axis=-1, keepdims=True)
        - unit * jnp.mean(q * unit, axis=-1, keepdims=True)
    )


def vectors_of(misc, rows):
    width = misc.shape[0]
    lane = lax.broadcasted_iota(jnp.int32, (rows, width), 1)
    row = lax.broadcasted_iota(jnp.int32, (rows, width), 0)
    spread = mm(misc[:, :rows], one_hot(lane % rows == row))
    lane = lax.broadcasted_iota(jnp.int32, (width, width), 1)
    row = lax.broadcasted_iota(jnp.int32, (width, width), 0)
    spread = jnp.where(lane // rows == row // rows, spread, 0.0)
    return jnp.sum(spread.reshape(width // rows, rows, width), axis=0)


def blocks_of(vectors):
    rows, width = vectors.shape
    spread = jnp.concatenate([vectors] * (width // rows), axis=0)
    lane = lax.broadcasted_iota(jnp.int32, (width, width), 1)
    row = lax.broadcasted_iota(jnp.int32, (width, width), 0)
    spread = jnp.where(lane // rows == row // rows, spread, 0.0).astype(BF16)
    row = lax.broadcasted_iota(jnp.int32, (width, MISC), 0)
    lane = lax.broadcasted_iota(jnp.int32, (width, MISC), 1)
    return mm(spread, one_hot(row % rows == lane))


def masked_softmax(logits, experts):
    lane = lax.broadcasted_iota(jnp.int32, logits.shape, 1)
    inside = (lane >= ROUTER_COL) & (lane < ROUTER_COL + experts)
    logits = jnp.where(inside, logits, neg_large)
    raised = jnp.exp(logits - jnp.max(logits, axis=-1, keepdims=True))
    return raised / jnp.sum(raised, axis=-1, keepdims=True)


def head_stack(rows, head_size):
    lane = lax.broadcasted_iota(jnp.int32, rows.shape, 1) // head_size
    return jnp.concatenate(
        [jnp.where(lane == h, rows, jnp.zeros_like(rows)) for h in range(QUAD)], axis=0
    )


def head_merge(stacked, patches, head_size):
    lane = lax.broadcasted_iota(jnp.int32, (patches, stacked.shape[1]), 1) // head_size
    total = jnp.zeros((patches, stacked.shape[1]), F32)
    for h in range(QUAD):
        total = jnp.where(lane == h, stacked[h * patches : (h + 1) * patches], total)
    return total


def position(dp_ex, in_kernel):
    if not in_kernel:
        return jnp.int32(0)
    return lax.axis_index("dp") * dp_ex[1] + lax.axis_index("expert")


def front_kernel(dims, cnt_ref, tok_ref, meta_ref, *refs):
    images, patches, experts, dp_ex, in_kernel, rels = dims
    pieces, refs = refs[: len(rels)], refs[len(rels) :]
    (
        wa_ref, wb_ref, qkv_ref, probs_ref, ctx_ref, hid_ref, rprob_ref, disp_ref, misc_ref, col_ref,
    ) = refs
    width = tok_ref.shape[1]
    head_size = width // HEADS
    rows = pieces[0].shape[1]
    me = position(dp_ex, in_kernel)
    for ref, rel in zip(pieces, rels):
        for slot, code in enumerate(rel):
            at = pl.multiple_of((me ^ code) * rows, rows)
            wa_ref[pl.ds(at, rows), :] = ref[slot, :, : 2 * width]
            wb_ref[pl.ds(at, rows), :] = ref[slot, :, 2 * width :]
    misc_ref[...] = wb_ref[:, 2 * width :]
    misc = vectors_of(wb_ref[:, 2 * width :], VECTOR_ROWS)
    x = tok_ref[...].astype(F32)
    unit, _ = normed(x)
    first_low = (unit * misc[0:1] + misc[1:2]).astype(BF16)
    qk = mm(first_low, wa_ref[...])
    qkv_ref[:, :width] = (qk[:, :width] + misc[2:3]).astype(BF16)
    qkv_ref[:, width : 2 * width] = qk[:, width:].astype(BF16)
    qkv_ref[:, 2 * width :] = (mm(first_low, wb_ref[:, :width]) + misc[3:4]).astype(BF16)
    scale = 1.0 / math.sqrt(head_size)
    quad_width = QUAD * head_size
    for i in range(images):
        at = slice(i * patches, (i + 1) * patches)
        valid = lax.broadcasted_iota(jnp.int32, (QUAD * patches, patches), 1) < cnt_ref[i]
        for quad in range(HEADS // QUAD):
            lo = quad * quad_width
            q = qkv_ref[at, lo : lo + quad_width]
            k = qkv_ref[at, width + lo : width + lo + quad_width]
            v = qkv_ref[at, 2 * width + lo : 2 * width + lo + quad_width]
            scores = jnp.where(valid, mm(head_stack(q, head_size), k, NT) * scale, neg_large)
            raised = jnp.exp(scores - jnp.max(scores, axis=-1, keepdims=True))
            probs = (raised / jnp.sum(raised, axis=-1, keepdims=True)).astype(BF16)
            probs_ref[i * (HEADS // QUAD) + quad] = probs
            ctx = head_merge(mm(probs, v), patches, head_size)
            ctx_ref[at, lo : lo + quad_width] = ctx.astype(BF16)
    hidden = x + mm(ctx_ref[...], wb_ref[:, width : 2 * width]) + misc[4:5]
    hid_ref[...] = hidden
    unit2, _ = normed(hidden)
    second_low = (unit2 * misc[5:6] + misc[6:7]).astype(BF16)
    rprob_ref[...] = masked_softmax(mm(second_low, wb_ref[:, 2 * width :]), experts)
    slots = disp_ref.shape[0]
    count = tok_ref.shape[0]
    row = lax.broadcasted_iota(jnp.int32, (slots, count), 0)
    pick = (row == meta_ref[0:1, :count]) | (row == meta_ref[1:2, :count])
    disp_ref[...] = mm(one_hot(pick), second_low).astype(BF16)
    meta = meta_ref[...].astype(F32)
    meta = jnp.concatenate([meta, jnp.zeros((MISC - 8, meta.shape[1]), F32)], axis=0)
    col_ref[...] = meta.T[:count].astype(jnp.int32)


def by_code(array, buffer, stride):
    me = lax.axis_index("expert")
    return [
        (array.at[pl.ds(pl.multiple_of((me ^ k) * stride, 16), stride)], buffer.at[pl.ds(k * stride, stride)])
        for k in range(array.shape[0] // stride)
    ]


def fetch(options, parts, sem):
    def copies(source):
        return [
            pltpu.make_async_copy(source.at[pl.ds(at, dst.shape[0])], dst, sem) for at, dst in parts
        ]

    if len(options) == 1:
        for copy in copies(options[0]):
            copy.start()
    else:

        @pl.when(jnp.logical_not(is_inner()))
        def _():
            for copy in copies(options[0]):
                copy.start()

        @pl.when(is_inner())
        def _():
            for copy in copies(options[1]):
                copy.start()

    return copies(options[0])


def chunk_parts(share, wh, wr):
    return [(0, wh), (share, wr)]


def bias_kernel(start, *refs):
    sources, (tails, sem) = refs[:-2], refs[-2:]
    copies = [
        pltpu.make_async_copy(source.at[pl.ds(start, 16)], tails.at[pl.ds(c * 16, 16)], sem)
        for c, source in enumerate(sources)
    ]
    for copy in copies:
        copy.start()
    for copy in copies:
        copy.wait()


def biases(chunks, start, us):
    return pl.pallas_call(
        functools.partial(bias_kernel, start),
        out_shape=shape((len(chunks) * 16, chunks[0].shape[1])),
        in_specs=[anywhere()] * len(chunks),
        out_specs=vmem(),
        scratch_shapes=[pltpu.SemaphoreType.DMA],
        compiler_params=params(4),
        cost_estimate=cost(us),
        name="biases",
    )(*chunks)


def tail_of(places):
    tails = [ref[at : at + 16].astype(F32) for ref, at in places]
    if len(tails) == 1:
        return tails[0]
    at = lax.axis_index("dp")
    return jnp.where((at == 1) | (at == 2), tails[1], tails[0])


def expert_pair(x, g, wh, wr, hb):
    pre = mm(x, wh, NT) + hb
    square = pre * pre
    half = 0.5 + 0.5 * jnp.tanh(pre * (GELU_C + (GELU_C * GELU_A) * square))
    act = (pre * half).astype(BF16)
    slope = half * (
        1.0 + (1.0 - half) * (pre * (2.0 * GELU_C + (6.0 * GELU_C * GELU_A) * square))
    )
    pg = (mm(g, wr, NT) * slope).astype(BF16)
    return act, pg


def hidden_bias_of(tail, share):
    return tail[0:1, :share]


def is_inner():
    at = lax.axis_index("dp")
    return (at == 1) | (at == 2)


def place_of(role, on_line):
    if not on_line:
        return role
    at = lax.axis_index("dp")
    inner = (at == 1) | (at == 2)
    mirror = 3 - at
    step = jnp.where(at < 2, 1, -1)
    return (
        jnp.where(inner, mirror, at + 2 * step),
        jnp.where(inner, mirror + step, at + step),
        at,
        jnp.where(inner, at - step, mirror),
    )[role]


def return_bias_of(tail, role, width):
    piece = width // 4
    row = tail[1:2]
    own = jnp.concatenate([row[:, :piece]] * 4, axis=1)
    lane = lax.broadcasted_iota(jnp.int32, (1, width), 1) // piece
    return jnp.where(lane == place_of(role, True), own, 0.0)


def weight_grads(x, g, act, pg, d_ref):
    share, width = act.shape[1], x.shape[1]
    row = lax.broadcasted_iota(jnp.int32, (16, width), 0)
    d_ref[:share] = mm(act, g, TN).astype(BF16)
    d_ref[share : 2 * share] = mm(pg, x, TN).astype(BF16)
    bias = jnp.sum(pg.astype(F32), axis=0, keepdims=True)
    if share < width:
        bias = jnp.concatenate([bias, jnp.zeros((1, width - share), F32)], axis=1)
    sums = jnp.sum(g.astype(F32), axis=0, keepdims=True)
    d_ref[2 * share :] = jnp.where(row == 0, bias, jnp.where(row == 1, sums, 0.0)).astype(BF16)


def early_expert_kernel(n_opts, experts, stride, on_line, rows_of, *refs):
    options = []
    for n in n_opts:
        options.append(refs[:n])
        refs = refs[n:]
    chunks = len(n_opts)
    tails, refs = refs[:2], refs[2:]
    tails = [tail_of([(tails[i], r) for i, r in role]) for role in rows_of]
    x_in, up_in, misc_ref, g_out, acts_out, pgs_out, d_ref = refs[:7]
    x_ref, up_ref, g_ref, acts_ref, pgs_ref, wh_ref, wr_ref, d_scr = refs[7:15]
    in_sems, sems, d_sems, out_sems = refs[15:]
    share, width = wh_ref.shape[0] // chunks, x_ref.shape[1]
    rows = [slice(c * share, (c + 1) * share) for c in range(chunks)]
    x_copies = load(by_code(x_in, x_ref, stride), in_sems)
    waits = [
        fetch(
            options[c],
            chunk_parts(
                share, wh_ref.at[pl.ds(c * share, share)], wr_ref.at[pl.ds(c * share, share)]
            ),
            sems.at[c],
        )
        for c in range(chunks)
    ]
    up_copies = load(by_code(up_in, up_ref, stride), in_sems, experts)
    wait_for(x_copies)
    prob = masked_softmax(mm(x_ref[...], misc_ref[...]), experts)
    lane = lax.broadcasted_iota(jnp.int32, prob.shape, 1)
    mine = lane == ROUTER_COL + lax.axis_index("expert")
    gate = jnp.sum(jnp.where(mine, prob, 0.0), axis=-1, keepdims=True)
    wait_for(up_copies)
    g_ref[...] = (gate * up_ref[...].astype(F32)).astype(BF16)
    copies = load([(g_ref, g_out)], out_sems)
    for c in reversed(range(chunks)):
        wait_for(waits[c])
        act, pg = expert_pair(
            x_ref[...], g_ref[...], wh_ref[rows[c]], wr_ref[rows[c]], hidden_bias_of(tails[c], share)
        )
        acts_ref[c] = act
        pgs_ref[c] = pg
        copies += load(
            [(acts_ref.at[c], acts_out.at[c]), (pgs_ref.at[c], pgs_out.at[c])], out_sems, 1 + 2 * c
        )
        weight_grads(x_ref[...], g_ref[...], act, pg, d_scr.at[c])
        copies += load([(d_scr.at[c], d_ref.at[place_of(c, on_line)])], d_sems, c)
    wait_for(copies)


def last_grads_kernel(n_opt, stride, on_line, roles, *refs):
    options, refs = refs[:n_opt], refs[n_opt:]
    tails, refs = refs[:2], refs[2:]
    tail = tail_of([(tails[i], r) for i, r in roles])
    x_in, g_in, _, act_out, pg_out, d_ref = refs[:6]
    x_ref, g_ref, wh_ref, wr_ref, act_ref, pg_ref, d_scr, sem, sems, x_sems = refs[6:]
    share = wh_ref.shape[0]
    waits = fetch(options, chunk_parts(share, wh_ref, wr_ref), sem)
    wait_for(load(by_code(x_in, x_ref, stride), x_sems) + load([(g_in, g_ref)], sems) + waits)
    act, pg = expert_pair(
        x_ref[...], g_ref[...], wh_ref[...], wr_ref[...], hidden_bias_of(tail, share)
    )
    act_ref[...] = act
    pg_ref[...] = pg
    copies = load([(act_ref, act_out), (pg_ref, pg_out)], sems, 2)
    weight_grads(x_ref[...], g_ref[...], act, pg, d_scr)
    last = place_of(3, True) if on_line else d_ref.shape[0] - 1
    wait_for(copies + load([(d_scr, d_ref.at[last])], sems, 4))


def last_expert_kernel(n_opts, dims, rows_of, *refs):
    experts, capacity, stride, on_line = dims
    options = []
    for n in n_opts:
        options.append(refs[:n])
        refs = refs[n:]
    chunks = len(n_opts)
    tails, refs = refs[: 2 * chunks], refs[2 * chunks :]
    tails = [
        tail_of([(tails[2 * c + i], r) for i, r in role]) for c, role in enumerate(rows_of)
    ]
    act_in, pg_in, acts_in, pgs_in, up_in, rb_ref, out_hbm = refs[:7]
    ing_outs, refs = refs[7 : 7 + experts // 2], refs[7 + experts // 2 :]
    acts_ref, pgs_ref, up_ref, wh_ref, wr_ref, out_ref, ing_ref, w_sems, sems, row_sems = refs
    width = up_ref.shape[1]
    share = wh_ref.shape[0] // chunks
    own = chunks - 1
    waits = []
    for c in range(chunks):
        rows = pl.ds(c * share, share)
        waits += fetch(options[c], chunk_parts(share, wh_ref.at[rows], wr_ref.at[rows]), w_sems.at[c])
    loads = load([(acts_in.at[c], acts_ref.at[c]) for c in range(own)] + [(act_in, acts_ref.at[own])], sems)
    later = load(
        [(pgs_in.at[c], pgs_ref.at[c]) for c in range(own)] + [(pg_in, pgs_ref.at[own])], sems, chunks
    )
    later += load(by_code(up_in, up_ref, stride), row_sems)
    wait_for(waits + loads)
    joined = jnp.concatenate([acts_ref[c] for c in range(chunks)], axis=1)
    bias = rb_ref[...]
    if on_line:
        for c in range(chunks):
            bias = bias + return_bias_of(tails[c], c, width)
    out = (mm(joined, wr_ref[...]) + bias).astype(BF16)
    out_ref[...] = out
    copies = load([(row, at) for at, row in by_code(out_hbm, out_ref, stride)], row_sems, experts)
    wait_for(later)
    joined = jnp.concatenate([pgs_ref[c] for c in range(chunks)], axis=1)
    ing_ref[...] = mm(joined, wh_ref[...]).astype(BF16)
    product = jnp.sum(up_ref[...].astype(F32) * out.astype(F32), axis=-1, keepdims=True)
    lane = lax.broadcasted_iota(jnp.int32, (stride, width), 1)
    row = lax.broadcasted_iota(jnp.int32, (stride, width), 0)
    tail_row = lax.broadcasted_iota(jnp.int32, (16, width), 0) + (stride - 16)
    for s in range(experts):
        own = product[s * stride : (s + 1) * stride]
        line = jnp.sum(jnp.where(lane == row, own, 0.0), axis=0, keepdims=True)
        high = line.astype(BF16).astype(F32)
        at = slice((s + 1) * stride - 16, (s + 1) * stride)
        end = ing_ref[at].astype(F32)
        end = jnp.where(tail_row == capacity, high, end)
        ing_ref[at] = jnp.where(tail_row == capacity + 1, line - high, end).astype(BF16)
    pair = 2 * stride
    copies += load(
        [(ing_ref.at[pl.ds(j * pair, pair)], ref) for j, ref in enumerate(ing_outs)], sems, 2 * chunks
    )
    wait_for(copies)


def finish_kernel(sum_ref, hidden_ref, return_ref, hb_ref, rb_ref):
    share, width = hidden_ref.shape
    return_ref[...] = sum_ref[:share].astype(F32)
    hidden_ref[...] = sum_ref[share : 2 * share].astype(F32)
    tail = sum_ref[2 * share :].astype(F32)
    hb_ref[...] = tail[0:1, :share]
    piece, at = rb_ref.shape[1], lax.axis_index("dp")
    own = jnp.zeros((1, piece), F32)
    for j in range(width // piece):
        own = jnp.where(at == j, tail[1:2, j * piece : (j + 1) * piece], own)
    rb_ref[...] = own


def back_kernel(
    dims, hid_in, up_in, rprob_in, poscol_in, wb_in, ctx_in, qkv_in, probs_in, wa_in, tok_in, *refs,
):
    images, patches, experts, capacity, stride, dp_ex, in_kernel = dims
    (*ing_ins, tgrad_out), refs = refs[: experts + 1], refs[experts + 1 :]
    (
        ing_ref, hid_ref, up_ref, rprob_ref, poscol_ref, wb_ref, ctx_ref, qkv_ref, probs_ref, wa_ref,
        tok_ref, tgrad_ref, sent_ref, dqkv_ref, cg_ref, sems,
    ) = refs[-16:]
    sent_outs = refs[:-16]
    loads = load(
        [
            (
                ing_ins[k // 2 + k % 2 * (experts // 2)].at[pl.ds(k % 2 * stride, stride)],
                ing_ref.at[pl.ds(k * stride, stride)],
            )
            for k in range(experts)
        ]
        + [
            (hid_in, hid_ref), (up_in, up_ref), (rprob_in, rprob_ref), (poscol_in, poscol_ref),
            (wb_in, wb_ref), (ctx_in, ctx_ref), (qkv_in, qkv_ref), (probs_in, probs_ref),
            (wa_in, wa_ref), (tok_in, tok_ref),
        ],
        sems,
    )
    wait_for(loads[: experts + 5])
    tokens, width = tok_ref.shape
    head_size = width // HEADS
    slots = ing_ref.shape[0]
    half, rows = sent_ref.shape[0] // 2, sent_ref.shape[1]
    misc = vectors_of(wb_ref[:, 2 * width :], VECTOR_ROWS)
    hidden = hid_ref[...]
    up = up_ref[...].astype(F32)
    rprob = rprob_ref[...]
    lane = lax.broadcasted_iota(jnp.int32, (stride, width), 1)
    row = lax.broadcasted_iota(jnp.int32, (stride, width), 0)
    mlane = lax.broadcasted_iota(jnp.int32, (stride, MISC), 1)
    columns = []
    expert_at = lax.axis_index("expert")
    for e in range(experts):
        tail = ing_ref[(e + 1) * stride - 16 : (e + 1) * stride].astype(F32)
        block = jnp.zeros((stride, MISC), F32)
        for part in range(2):
            at = capacity - stride + 16 + part
            line = tail[at : at + 1]
            column = jnp.sum(jnp.where(lane == row, line, 0.0), axis=-1, keepdims=True)
            block = jnp.where(mlane == ROUTER_COL * (1 + part) + (expert_at ^ e), column, block)
        columns.append(block.astype(BF16))
    gate_grads = jnp.concatenate(columns, axis=0)
    slane = lax.broadcasted_iota(jnp.int32, (1, slots), 1)
    block_of = jnp.zeros((1, slots), jnp.int32)
    for e in range(experts):
        block_of = jnp.where(slane >= e * stride, (expert_at ^ e) - e, block_of)
    slane = slane + block_of * stride
    either = one_hot((slane == poscol_ref[:, 0:1]) | (slane == poscol_ref[:, 1:2]))
    spread = mm(either, gate_grads)
    rlane = lax.broadcasted_iota(jnp.int32, (tokens, MISC), 1)
    inside = (rlane >= ROUTER_COL) & (rlane < ROUTER_COL + experts)
    prob_grad = jnp.where(inside, spread + pltpu.roll(spread, MISC - ROUTER_COL, 1), 0.0)
    logit_low = (
        rprob * (prob_grad - jnp.sum(prob_grad * rprob, axis=-1, keepdims=True))
    ).astype(BF16)
    unit2, rstd2 = normed(hidden)
    second_low = (unit2 * misc[5:6] + misc[6:7]).astype(BF16)
    router_grad = mm(second_low, logit_low, TN)
    second_grad = mm(logit_low, wb_ref[:, 2 * width :], NT) + mm(either, ing_ref[...])
    gain2_grad = jnp.sum(second_grad * unit2, axis=0, keepdims=True)
    shift2_grad = jnp.sum(second_grad, axis=0, keepdims=True)
    residual = up + norm_back(second_grad, misc[5:6], unit2, rstd2)
    proj_in = residual.astype(BF16)
    proj_b_grad = jnp.sum(proj_in.astype(F32), axis=0, keepdims=True)
    cg_ref[...] = mm(proj_in, wb_ref[:, width : 2 * width], NT).astype(BF16)
    wait_for(loads[experts + 5 :])
    proj_w_grad = mm(ctx_ref[...], proj_in, TN)
    scale = 1.0 / math.sqrt(head_size)
    quad_width = QUAD * head_size
    for i in range(images):
        at = slice(i * patches, (i + 1) * patches)
        for quad in range(HEADS // QUAD):
            lo = quad * quad_width
            q = qkv_ref[at, lo : lo + quad_width]
            k = qkv_ref[at, width + lo : width + lo + quad_width]
            v = qkv_ref[at, 2 * width + lo : 2 * width + lo + quad_width]
            cg = head_stack(cg_ref[at, lo : lo + quad_width], head_size)
            probs_low = probs_ref[i * (HEADS // QUAD) + quad]
            probs = probs_low.astype(F32)
            weight_grad = mm(cg, v, NT)
            value_grad = mm(probs_low, cg, TN)
            score_grad = (
                probs * (weight_grad - jnp.sum(weight_grad * probs, axis=-1, keepdims=True))
            ).astype(BF16)
            query_grad = head_merge(mm(score_grad, k), patches, head_size) * scale
            key_grad = mm(score_grad, head_stack(q, head_size), TN) * scale
            dqkv_ref[at, lo : lo + quad_width] = query_grad.astype(BF16)
            dqkv_ref[at, width + lo : width + lo + quad_width] = key_grad.astype(BF16)
            dqkv_ref[at, 2 * width + lo : 2 * width + lo + quad_width] = value_grad.astype(BF16)
    unit1, rstd1 = normed(tok_ref[...].astype(F32))
    first_low = (unit1 * misc[0:1] + misc[1:2]).astype(BF16)
    query_b_grad = jnp.sum(dqkv_ref[:, :width].astype(F32), axis=0, keepdims=True)
    value_b_grad = jnp.sum(dqkv_ref[:, 2 * width :].astype(F32), axis=0, keepdims=True)
    first_grad = mm(dqkv_ref[:, : 2 * width], wa_ref[...], NT) + mm(
        dqkv_ref[:, 2 * width :], wb_ref[:, :width], NT
    )
    gain1_grad = jnp.sum(first_grad * unit1, axis=0, keepdims=True)
    shift1_grad = jnp.sum(first_grad, axis=0, keepdims=True)
    tgrad_ref[...] = (residual + norm_back(first_grad, misc[0:1], unit1, rstd1)).astype(BF16)
    copies = load([(tgrad_ref, tgrad_out)], sems)
    small = jnp.concatenate(
        [
            gain1_grad, shift1_grad, query_b_grad, value_b_grad,
            proj_b_grad, gain2_grad, shift2_grad, jnp.zeros((VECTOR_ROWS - 7, width), F32),
        ],
        axis=0,
    )
    tail = (router_grad + blocks_of(small)).astype(BF16)
    first_t = first_low.astype(F32).T.astype(BF16)
    da = mm(first_t, dqkv_ref[:, : 2 * width]).astype(BF16)
    dv = mm(first_t, dqkv_ref[:, 2 * width :]).astype(BF16)
    grads = jnp.concatenate([da, dv, proj_w_grad.astype(BF16), tail], axis=1)
    me = position(dp_ex, in_kernel)
    core = me % 2
    dp, ex = dp_ex
    for r in range(0, 2 * half, 2):
        even, odd = grads[r * rows : (r + 1) * rows], grads[(r + 1) * rows : (r + 2) * rows]
        rel = r ^ me
        to = (rel % ex) // 2 * dp + rel // ex if in_kernel else r // 2
        sent_ref[to] = jnp.where(core == 0, even, odd)
        sent_ref[half + to] = jnp.where(core == 0, odd, even)
    each = 2 * half // len(sent_outs)
    copies += load(
        [(sent_ref.at[pl.ds(n * each, each)], out) for n, out in enumerate(sent_outs)], sems, 1
    )
    wait_for(copies)


def mix_kernel(experts, hid_ref, ret_ref, rprob_ref, poscol_ref, block_ref):
    tokens, slots = hid_ref.shape[0], ret_ref.shape[0]
    rprob = rprob_ref[...]
    lane = lax.broadcasted_iota(jnp.int32, (tokens, slots), 1)
    rlane = lax.broadcasted_iota(jnp.int32, (tokens, MISC), 1)
    mixed = hid_ref[...]
    for k in range(2):
        pos = poscol_ref[:, k : k + 1]
        picked = mm(one_hot(lane == pos), ret_ref[...])
        hot = (rlane == ROUTER_COL + poscol_ref[:, 2 + k : 3 + k]) & (pos >= 0)
        mixed = mixed + jnp.sum(jnp.where(hot, rprob, 0.0), axis=-1, keepdims=True) * picked
    block_ref[...] = mixed.astype(BF16)


def turn(blocks, at):
    part = blocks[:, :, at : at + VECTOR_ROWS]
    return blocks.at[:, :, at : at + VECTOR_ROWS].set(jnp.swapaxes(part, 1, 2))


def flip(x, stage):
    axis, size, bit = stage
    return lax.ppermute(x, axis, [(i, i ^ bit) for i in range(size)])


def line_permute(x, pairs):
    return lax.ppermute(x, "dp", pairs)


INWARD, ACROSS, OUTWARD = [(0, 1), (3, 2)], [(1, 2), (2, 1)], [(1, 0), (2, 3)]
SIDE = INWARD + OUTWARD


def add(a, b):
    return (a.astype(F32) + b.astype(F32)).astype(BF16)


def on_device(
    tokens, patch_counts, expert_ids, priority, out_grad, first_gain, first_shift, qkv_weight,
    query_bias, value_bias, proj_weight, proj_bias, second_gain, second_shift, router_weight,
    hidden_weight, hidden_bias, return_weight, return_bias, *, dp, ex,
):
    images, patches, width = tokens.shape
    count = images * patches
    top = expert_ids.shape[2]
    experts = router_weight.shape[1]
    capacity = (count * top * 105 + 100 * experts - 1) // (100 * experts)
    stride = (capacity + 2 + 15) // 16 * 16
    slots = experts * stride
    devices = dp * ex
    share_rows = qkv_weight.shape[0]
    ff_share = hidden_weight.shape[1]
    piece = width // dp
    dp_at = lax.axis_index("dp")
    ex_at = lax.axis_index("expert")
    me = dp_at * ex + ex_at
    in_kernel = share_rows % 16 == 0
    on_line = dp == 4

    vectors = [
        first_gain, first_shift, query_bias, value_bias, proj_bias, second_gain, second_shift,
    ]
    small = jnp.pad(router_weight, ((0, 0), (ROUTER_COL, MISC - ROUTER_COL - experts)))
    for j, vector in enumerate(vectors):
        if in_kernel:
            at = ((j, share_rows - 1 - j), (0, MISC - share_rows))
            small = small + jnp.pad(vector[None], at)
        else:
            small = small + jnp.pad(vector[:, None], ((0, 0), (j, MISC - 1 - j)))
    packed = jnp.concatenate([qkv_weight, proj_weight, small], axis=1)[None]
    tail = jnp.pad(hidden_bias, ((0, 15), (0, width - ff_share)))
    tail = tail + jnp.pad(return_bias, ((1, 14), (0, width - piece)))
    own = jnp.concatenate([hidden_weight[0], return_weight[0], tail], axis=0)
    if on_line:
        own, packed = lax.optimization_barrier((own, packed))
        side = line_permute(own, SIDE)
        across1 = line_permute(own, ACROSS)
    else:
        expert_w = lax.all_gather(own, "dp", axis=0)

    packed = jnp.concatenate([flip(packed, ("dp", dp, k)) if k else packed for k in range(dp)], axis=0)
    chips = ex // 2
    core = ("expert", ex, 1)

    if in_kernel:
        packed, patch_counts, expert_ids, priority = lax.optimization_barrier(
            (packed, patch_counts, expert_ids, priority)
        )
    valid = (
        lax.broadcasted_iota(jnp.int32, (images, patches), 1) < patch_counts[:, None]
    ).reshape(count)
    choices = expert_ids.reshape(count, top)
    rank = priority[0]
    earlier = (rank[:, None] > rank[None, :]).astype(BF16)
    iota = jnp.arange(experts, dtype=jnp.int32)
    hot = choices[:, :, None] == iota[None, None, :]
    hot_valid = (hot & valid[:, None, None]).astype(BF16).reshape(count, top * experts)
    before = jnp.dot(earlier, hot_valid, preferred_element_type=F32).reshape(count, top, experts)
    totals = jnp.sum(hot_valid.astype(F32), axis=0).reshape(top, experts)
    start = jnp.cumsum(totals, axis=0) - totals
    slot = jnp.sum(jnp.where(hot, before + start[None], 0.0), axis=-1).astype(jnp.int32)
    kept = valid[:, None] & (slot < capacity)
    pos = jnp.where(kept, choices * stride + slot, -1)
    pos_row = pos.T
    meta = jnp.concatenate([pos_row, choices.T], axis=0)
    meta = jnp.pad(meta, ((0, 4), (0, -count % MISC)))

    pieces = [flip(packed, ("expert", ex, 2 * j)) if j else packed for j in range(chips)]
    pieces += [flip(p, core) for p in pieces]
    rels = [[k * ex + 2 * j + b for k in range(dp)] for b in range(2) for j in range(chips)]
    if in_kernel:
        block_rows = share_rows
        kernel_rels = rels
    else:
        blocks, block_rows = width // 16, 16
        kernel_rels = [list(range(blocks))]
        at = np.argsort(np.array(sum(rels, [])))
        whole = jnp.concatenate(pieces, axis=0)[jnp.asarray(at)[jnp.arange(devices) ^ me]]
        pieces = [turn(whole.reshape(blocks, 16, -1), 4 * width)]

    pick = jnp.zeros((slots, count), jnp.bool_)
    slot_iota = lax.broadcasted_iota(jnp.int32, (slots, count), 0)
    for k in range(top):
        pick = pick | (slot_iota == pos_row[k][None, :])
    up = out_grad.reshape(count, width)
    up_slots = jnp.dot(pick.astype(BF16), up, preferred_element_type=F32).astype(BF16)

    pieces = [flip(packed, ("expert", ex, 2 * j)) if j else packed for j in range(chips)]
    pieces += [flip(p, core) for p in pieces]
    rels = [[k * ex + 2 * j + b for k in range(dp)] for b in range(2) for j in range(chips)]
    if in_kernel:
        block_rows = share_rows
        kernel_rels = rels
    else:
        blocks, block_rows = width // 16, 16
        kernel_rels = [list(range(blocks))]
        at = np.argsort(np.array(sum(rels, [])))
        whole = jnp.concatenate(pieces, axis=0)[jnp.asarray(at)[jnp.arange(devices) ^ me]]
        pieces = [turn(whole.reshape(blocks, 16, -1), 4 * width)]

    def exchange(x):
        x = lax.all_to_all(
            x.reshape(experts, stride, width), "expert", split_axis=0, concat_axis=0, tiled=True
        )
        return x.reshape(slots, width)


    tok = tokens.reshape(count, width)
    pairs = images * (HEADS // QUAD)
    if on_line:
        tails = biases([side, across1, own], 2 * ff_share, HOP1_COST)
        pieces, tails, side, across1 = lax.optimization_barrier((pieces, tails, side, across1))
        across2 = line_permute(side, ACROSS)
        out2 = line_permute(across1, OUTWARD)
    up_arrived = exchange(up_slots)
    made = (
        ((width, 2 * width), BF16),
        ((width, 2 * width + MISC), BF16),
        ((count, 3 * width), BF16),
        ((pairs, QUAD * patches, patches), BF16),
        ((count, width), BF16),
        ((count, width), F32),
        ((count, MISC), F32),
        ((slots, width), BF16),
        ((width, MISC), BF16),
        ((count, MISC), jnp.int32),
    )
    wa, wb, qkv, probs, ctx, hidden, rprob, dispatch, misc, pos_col = pl.pallas_call(
        functools.partial(
            front_kernel, (images, patches, experts, (dp, ex), in_kernel, kernel_rels)
        ),
        out_shape=tuple(shape(*m) for m in made),
        in_specs=[smem()] + [vmem()] * (2 + len(pieces)),
        out_specs=(vmem(),) * 10,
        compiler_params=params(56),
        cost_estimate=cost(0),
        name="front",
    )(patch_counts, tok, meta, *pieces)

    dispatch, up_arrived = lax.optimization_barrier((dispatch, up_arrived))
    arrived = exchange(dispatch)
    if on_line:
        chunks = [(out2, across1), (side, across2), (own,)]
        tails2 = biases([across2, out2], 2 * ff_share, HOP2_COST)
        out3 = line_permute(across2, OUTWARD)
        last, early_tails = (out3, side), (tails, tails2)
        rows_of = [((1, 16), (0, 16)), ((0, 0), (1, 0)), ((0, 32),), ((1, 0), (0, 0))]
        return_add = jnp.zeros((1, width), F32)
    else:
        chunks = [(expert_w[c],) for c in range(dp)]
        chunks, last = chunks[:-1], chunks[-1]
        tails = expert_w[:, 2 * ff_share :].reshape(dp * 16, width)
        early_tails = last_tails = (tails, tails)
        rows_of = [((0, c * 16),) for c in range(dp)]
        return_add = expert_w[:, 2 * ff_share + 1, :piece].reshape(1, width).astype(F32)

    sem = pltpu.SemaphoreType.DMA
    early = dp - 1
    options = [len(c) for c in chunks]
    wide = shape((slots, width))
    matrix = pltpu.VMEM((ff_share, width), BF16)
    grad_rows = 2 * ff_share + 16
    grad = pltpu.VMEM((grad_rows, width), BF16)
    row_buffer, sum_buffer = pltpu.VMEM((slots, width), BF16), pltpu.VMEM((slots, width), F32)
    dma = lambda n: pltpu.SemaphoreType.DMA((n,))
    several = shape((early, slots, ff_share))
    g, acts, pgs, d_all = pl.pallas_call(
        functools.partial(early_expert_kernel, options, experts, stride, on_line, rows_of[:-1]),
        out_shape=(wide, several, several, shape((dp, grad_rows, width))),
        in_specs=[anywhere()] * sum(options) + [vmem()] * 2 + [anywhere()] * 2 + [vmem()],
        out_specs=(anywhere(),) * 4,
        scratch_shapes=[row_buffer] * 3
        + [pltpu.VMEM(several.shape, BF16)] * 2
        + [pltpu.VMEM((early * ff_share, width), BF16)] * 2
        + [pltpu.VMEM((early, grad_rows, width), BF16)]
        + [dma(2 * experts), dma(early), dma(early), dma(1 + 2 * early)],
        compiler_params=params(56),
        cost_estimate=cost(0),
        name="experts_early",
    )(*sum(chunks, ()), *early_tails, arrived, up_arrived, misc)
    if on_line:
        out3, g = lax.optimization_barrier((out3, g))
        tails3 = biases([out3], 2 * ff_share, HOP3_COST)
        last, last_tails = (out3, side), (tails, tails3)
    operands = (*last, *last_tails, arrived, g, d_all)
    narrow, part_buffer = shape((slots, ff_share)), pltpu.VMEM((slots, ff_share), BF16)
    act, pg, d_all = pl.pallas_call(
        functools.partial(last_grads_kernel, len(last), stride, on_line, rows_of[-1]),
        out_shape=(narrow, narrow, shape((dp, grad_rows, width))),
        in_specs=[anywhere()] * len(last) + [vmem()] * 2 + [anywhere()] * 3,
        out_specs=(anywhere(),) * 3,
        scratch_shapes=[row_buffer, row_buffer, matrix, matrix, part_buffer, part_buffer, grad]
        + [sem, dma(5), dma(experts)],
        input_output_aliases={len(operands) - 1: 2},
        compiler_params=params(56),
        cost_estimate=cost(0),
        name="last_grads",
    )(*operands)
    options = options + [len(last)]
    expert_out, *in_grad = pl.pallas_call(
        functools.partial(
            last_expert_kernel, options, (experts, capacity, stride, on_line), rows_of
        ),
        out_shape=(wide,) + (shape((2 * stride, width)),) * chips,
        in_specs=[anywhere()] * sum(options) + [vmem()] * (2 * dp) + [anywhere()] * 5 + [vmem()],
        out_specs=(anywhere(),) * (1 + chips),
        scratch_shapes=[pltpu.VMEM((dp, slots, ff_share), BF16)] * 2
        + [row_buffer]
        + [pltpu.VMEM((dp * ff_share, width), BF16)] * 2
        + [row_buffer, row_buffer, dma(dp), dma(2 * dp + chips), dma(2 * experts)],
        compiler_params=params(56),
        cost_estimate=cost(0),
        name="experts_last",
    )(
        *sum(chunks, ()), *last, *(early_tails * early), *last_tails,
        act, pg, acts, pgs, up_arrived, return_add,
    )
    gone = [flip(d, ("expert", ex, 2 * j)) if j else d for j, d in enumerate(in_grad)]
    expert_out, gone[1:] = lax.optimization_barrier((expert_out, gone[1:]))
    gone += [flip(d, core) for d in gone]
    returned = exchange(expert_out)
    d_sum = lax.psum_scatter(d_all, "dp", scatter_dimension=0, tiled=False)

    half = width // block_rows // 2
    pieces_out = chips if in_kernel else 1
    operands = (hidden, up, rprob, pos_col, wb, ctx, qkv, probs, wa, tok)
    tokens_grad, *sent = pl.pallas_call(
        functools.partial(
            back_kernel, (images, patches, experts, capacity, stride, (dp, ex), in_kernel)
        ),
        out_shape=(shape((count, width)),)
        + (shape((half // pieces_out, block_rows, 4 * width + MISC)),) * (2 * pieces_out),
        in_specs=[anywhere()] * (10 + experts),
        out_specs=(anywhere(),) * (1 + 2 * pieces_out),
        scratch_shapes=[row_buffer]
        + [pltpu.VMEM(b.shape, b.dtype) for b in operands]
        + [
            pltpu.VMEM((count, width), BF16),
            pltpu.VMEM((2 * half, block_rows, 4 * width + MISC), BF16),
            pltpu.VMEM((count, 3 * width), BF16),
            pltpu.VMEM((count, width), BF16),
            dma(10 + max(experts, 2 * pieces_out)),
        ],
        compiler_params=params(56),
        cost_estimate=cost(0),
        name="back",
    )(*operands, *gone)

    if not in_kernel:
        whole = jnp.stack(sent, axis=1).reshape(2 * half, block_rows, -1)
        whole = turn(whole, 4 * width).reshape(devices, share_rows, -1)
        whole = whole[jnp.asarray(np.array(sum(rels, []))) ^ me]
        sent = [whole[j * dp : (j + 1) * dp] for j in range(2 * chips)]
    sent, returned = lax.optimization_barrier((sent, returned))
    came = [flip(d, core) for d in sent[chips:]]
    parts = [add(k, c) for k, c in zip(sent[:chips], came)]
    moved = [flip(parts[j], ("expert", ex, 2 * j)) for j in range(1, chips)]
    total = functools.reduce(lambda t, m: t + m.astype(F32), moved, parts[0].astype(F32)).astype(BF16)
    block_out = pl.pallas_call(
        functools.partial(mix_kernel, experts),
        out_shape=shape((count, width)),
        in_specs=[vmem()] * 4,
        out_specs=vmem(),
        compiler_params=params(56),
        cost_estimate=cost(0),
        name="mix",
    )(hidden, returned, rprob, pos_col)
    total, block_out = lax.optimization_barrier((total, block_out))
    last_came = [flip(total[k], ("dp", dp, k)) for k in range(1, dp)]
    hidden_sum, return_sum, hidden_bias_sum, return_bias_sum = pl.pallas_call(
        finish_kernel,
        out_shape=(
            shape((ff_share, width), F32), shape((ff_share, width), F32),
            shape((1, ff_share), F32), shape((1, piece), F32),
        ),
        in_specs=[vmem()],
        out_specs=(vmem(),) * 4,
        compiler_params=params(56),
        cost_estimate=cost(0),
        name="finish",
    )(d_sum)
    last_came, hidden_sum, return_sum = lax.optimization_barrier((last_came, hidden_sum, return_sum))
    final = functools.reduce(lambda t, d: t + d.astype(F32), last_came, total[0].astype(F32))
    qkv_sum = final[:, : 3 * width]
    proj_sum = final[:, 3 * width : 4 * width]
    if in_kernel:
        vec = [final[j, 4 * width : 4 * width + share_rows] for j in range(7)]
    else:
        vec = [final[:, 4 * width + j] for j in range(7)]
    router_sum = final[:, 4 * width + ROUTER_COL : 4 * width + ROUTER_COL + experts]
    return (
        block_out.reshape(tokens.shape),
        tokens_grad.reshape(tokens.shape),
        vec[0], vec[1], qkv_sum, vec[2], vec[3], proj_sum, vec[4], vec[5], vec[6], router_sum,
        hidden_sum[None],
        hidden_bias_sum,
        return_sum[None],
        return_bias_sum,
    )


def solution(mesh):
    both, rows = P(("dp", "expert")), P(("dp", "expert"), None)
    cube = P(("dp", "expert"), None, None)
    weight, bias = P("expert", "dp", None), P("expert", "dp")
    in_specs = (
        cube, both, cube, rows, cube, both, both, rows, both, both, rows, both, both, both, rows,
        weight, bias, weight, bias,
    )
    out_specs = (
        cube, cube, both, both, rows, both, both, rows, both, both, both, rows,
        weight, bias, weight, bias,
    )
    return jax.shard_map(
        functools.partial(on_device, dp=mesh.shape["dp"], ex=mesh.shape["expert"]),
        mesh=mesh,
        in_specs=in_specs,
        out_specs=out_specs,
        check_vma=False,
    )
```

```python
import functools
import math

import jax
import jax.numpy as jnp
import numpy as np
from jax import lax
from jax.experimental import pallas as pl
from jax.experimental.pallas import tpu as pltpu
from jax.sharding import PartitionSpec as P

HEADS = 8
QUAD = 4
norm_eps = 1e-06
neg_large = -1e30
F32 = jnp.float32
BF16 = jnp.bfloat16
ROUTER_COL = 32
MISC = 128
VECTOR_ROWS = 16
HOP1_COST, HOP2_COST, HOP3_COST = 10, 40, 40
GELU_C = math.sqrt(2.0 / math.pi)
GELU_A = 0.044715

NN = (((1,), (0,)), ((), ()))
NT = (((1,), (1,)), ((), ()))
TN = (((0,), (0,)), ((), ()))


def mm(a, b, dims=NN):
    return lax.dot_general(a, b, dims, preferred_element_type=F32)


def params(mib=28):
    return pltpu.CompilerParams(vmem_limit_bytes=mib * 1024 * 1024)


def cost(us):
    return pl.CostEstimate(flops=us * 10**9, bytes_accessed=0, transcendentals=0)


def vmem():
    return pl.BlockSpec(memory_space=pltpu.VMEM)


def smem():
    return pl.BlockSpec(memory_space=pltpu.SMEM)


def anywhere():
    return pl.BlockSpec(memory_space=pl.ANY)


def hbm():
    return pl.BlockSpec(memory_space=pltpu.HBM)


def load(pairs, sems, first=0):
    copies = [
        pltpu.make_async_copy(source, dst, sems.at[first + n]) for n, (source, dst) in enumerate(pairs)
    ]
    for copy in copies:
        copy.start()
    return copies


def wait_for(copies):
    for copy in copies:
        copy.wait()


def shape(dims, dtype=BF16):
    return jax.ShapeDtypeStruct(dims, dtype)


def one_hot(mask):
    return mask.astype(F32).astype(BF16)


def normed(values):
    center = values - jnp.mean(values, axis=-1, keepdims=True)
    rstd = lax.rsqrt(jnp.mean(center * center, axis=-1, keepdims=True) + norm_eps)
    return center * rstd, rstd


def norm_back(grad, gain, unit, rstd):
    q = grad * gain
    return rstd * (
        q
        - jnp.mean(q, axis=-1, keepdims=True)
        - unit * jnp.mean(q * unit, axis=-1, keepdims=True)
    )


def vectors_of(misc, rows):
    width = misc.shape[0]
    lane = lax.broadcasted_iota(jnp.int32, (rows, width), 1)
    row = lax.broadcasted_iota(jnp.int32, (rows, width), 0)
    spread = mm(misc[:, :rows], one_hot(lane % rows == row))
    lane = lax.broadcasted_iota(jnp.int32, (width, width), 1)
    row = lax.broadcasted_iota(jnp.int32, (width, width), 0)
    spread = jnp.where(lane // rows == row // rows, spread, 0.0)
    return jnp.sum(spread.reshape(width // rows, rows, width), axis=0)


def blocks_of(vectors):
    rows, width = vectors.shape
    spread = jnp.concatenate([vectors] * (width // rows), axis=0)
    lane = lax.broadcasted_iota(jnp.int32, (width, width), 1)
    row = lax.broadcasted_iota(jnp.int32, (width, width), 0)
    spread = jnp.where(lane // rows == row // rows, spread, 0.0).astype(BF16)
    row = lax.broadcasted_iota(jnp.int32, (width, MISC), 0)
    lane = lax.broadcasted_iota(jnp.int32, (width, MISC), 1)
    return mm(spread, one_hot(row % rows == lane))


def masked_softmax(logits, experts):
    lane = lax.broadcasted_iota(jnp.int32, logits.shape, 1)
    inside = (lane >= ROUTER_COL) & (lane < ROUTER_COL + experts)
    logits = jnp.where(inside, logits, neg_large)
    raised = jnp.exp(logits - jnp.max(logits, axis=-1, keepdims=True))
    return raised / jnp.sum(raised, axis=-1, keepdims=True)


def head_stack(rows, head_size):
    lane = lax.broadcasted_iota(jnp.int32, rows.shape, 1) // head_size
    return jnp.concatenate(
        [jnp.where(lane == h, rows, jnp.zeros_like(rows)) for h in range(QUAD)], axis=0
    )


def head_merge(stacked, patches, head_size):
    lane = lax.broadcasted_iota(jnp.int32, (patches, stacked.shape[1]), 1) // head_size
    total = jnp.zeros((patches, stacked.shape[1]), F32)
    for h in range(QUAD):
        total = jnp.where(lane == h, stacked[h * patches : (h + 1) * patches], total)
    return total


def position(dp_ex, in_kernel):
    if not in_kernel:
        return jnp.int32(0)
    return lax.axis_index("dp") * dp_ex[1] + lax.axis_index("expert")


def front_kernel(dims, cnt_ref, tok_ref, meta_ref, *refs):
    images, patches, experts, dp_ex, in_kernel, rels = dims
    pieces, refs = refs[: len(rels)], refs[len(rels) :]
    (
        wa_ref, wb_ref, qkv_ref, probs_ref, ctx_ref, hid_ref, rprob_ref, disp_ref, misc_ref, col_ref,
    ) = refs
    width = tok_ref.shape[1]
    head_size = width // HEADS
    rows = pieces[0].shape[1]
    me = position(dp_ex, in_kernel)
    for ref, rel in zip(pieces, rels):
        for slot, code in enumerate(rel):
            at = pl.multiple_of((me ^ code) * rows, rows)
            wa_ref[pl.ds(at, rows), :] = ref[slot, :, : 2 * width]
            wb_ref[pl.ds(at, rows), :] = ref[slot, :, 2 * width :]
    misc_ref[...] = wb_ref[:, 2 * width :]
    misc = vectors_of(wb_ref[:, 2 * width :], VECTOR_ROWS)
    x = tok_ref[...].astype(F32)
    unit, _ = normed(x)
    first_low = (unit * misc[0:1] + misc[1:2]).astype(BF16)
    qk = mm(first_low, wa_ref[...])
    qkv_ref[:, :width] = (qk[:, :width] + misc[2:3]).astype(BF16)
    qkv_ref[:, width : 2 * width] = qk[:, width:].astype(BF16)
    qkv_ref[:, 2 * width :] = (mm(first_low, wb_ref[:, :width]) + misc[3:4]).astype(BF16)
    scale = 1.0 / math.sqrt(head_size)
    quad_width = QUAD * head_size
    for i in range(images):
        at = slice(i * patches, (i + 1) * patches)
        valid = lax.broadcasted_iota(jnp.int32, (QUAD * patches, patches), 1) < cnt_ref[i]
        for quad in range(HEADS // QUAD):
            lo = quad * quad_width
            q = qkv_ref[at, lo : lo + quad_width]
            k = qkv_ref[at, width + lo : width + lo + quad_width]
            v = qkv_ref[at, 2 * width + lo : 2 * width + lo + quad_width]
            scores = jnp.where(valid, mm(head_stack(q, head_size), k, NT) * scale, neg_large)
            raised = jnp.exp(scores - jnp.max(scores, axis=-1, keepdims=True))
            probs = (raised / jnp.sum(raised, axis=-1, keepdims=True)).astype(BF16)
            probs_ref[i * (HEADS // QUAD) + quad] = probs
            ctx = head_merge(mm(probs, v), patches, head_size)
            ctx_ref[at, lo : lo + quad_width] = ctx.astype(BF16)
    hidden = x + mm(ctx_ref[...], wb_ref[:, width : 2 * width]) + misc[4:5]
    hid_ref[...] = hidden
    unit2, _ = normed(hidden)
    second_low = (unit2 * misc[5:6] + misc[6:7]).astype(BF16)
    rprob_ref[...] = masked_softmax(mm(second_low, wb_ref[:, 2 * width :]), experts)
    slots = disp_ref.shape[0]
    count = tok_ref.shape[0]
    row = lax.broadcasted_iota(jnp.int32, (slots, count), 0)
    pick = (row == meta_ref[0:1, :count]) | (row == meta_ref[1:2, :count])
    disp_ref[...] = mm(one_hot(pick), second_low).astype(BF16)
    meta = meta_ref[...].astype(F32)
    meta = jnp.concatenate([meta, jnp.zeros((MISC - 8, meta.shape[1]), F32)], axis=0)
    col_ref[...] = meta.T[:count].astype(jnp.int32)


def by_code(array, buffer, stride):
    me = lax.axis_index("expert")
    return [
        (array.at[pl.ds(pl.multiple_of((me ^ k) * stride, 16), stride)], buffer.at[pl.ds(k * stride, stride)])
        for k in range(array.shape[0] // stride)
    ]


def fetch(options, parts, sem):
    def copies(source):
        return [
            pltpu.make_async_copy(source.at[pl.ds(at, dst.shape[0])], dst, sem) for at, dst in parts
        ]

    if len(options) == 1:
        for copy in copies(options[0]):
            copy.start()
    else:

        @pl.when(jnp.logical_not(is_inner()))
        def _():
            for copy in copies(options[0]):
                copy.start()

        @pl.when(is_inner())
        def _():
            for copy in copies(options[1]):
                copy.start()

    return copies(options[0])


def chunk_parts(share, wh, wr):
    return [(0, wh), (share, wr)]


def bias_kernel(start, *refs):
    sources, (tails, sem) = refs[:-2], refs[-2:]
    copies = [
        pltpu.make_async_copy(source.at[pl.ds(start, 16)], tails.at[pl.ds(c * 16, 16)], sem)
        for c, source in enumerate(sources)
    ]
    for copy in copies:
        copy.start()
    for copy in copies:
        copy.wait()


def biases(chunks, start, us):
    return pl.pallas_call(
        functools.partial(bias_kernel, start),
        out_shape=shape((len(chunks) * 16, chunks[0].shape[1])),
        in_specs=[anywhere()] * len(chunks),
        out_specs=vmem(),
        scratch_shapes=[pltpu.SemaphoreType.DMA],
        compiler_params=params(4),
        cost_estimate=cost(us),
        name="biases",
    )(*chunks)


def tail_of(places):
    tails = [ref[at : at + 16].astype(F32) for ref, at in places]
    if len(tails) == 1:
        return tails[0]
    at = lax.axis_index("dp")
    return jnp.where((at == 1) | (at == 2), tails[1], tails[0])


def activation(x, wh, hb):
    pre = mm(x, wh, NT) + hb
    half = 0.5 + 0.5 * jnp.tanh(pre * (GELU_C + (GELU_C * GELU_A) * (pre * pre)))
    return pre, half


def gelu_slope(pre, half):
    return half * (
        1.0 + (1.0 - half) * (pre * (2.0 * GELU_C + (6.0 * GELU_C * GELU_A) * (pre * pre)))
    )


def expert_pair(x, g, wh, wr, hb):
    pre, half = activation(x, wh, hb)
    act = (pre * half).astype(BF16)
    pg = (mm(g, wr, NT) * gelu_slope(pre, half)).astype(BF16)
    return act, pg


def hidden_bias_of(tail, share):
    return tail[0:1, :share]


def is_inner():
    at = lax.axis_index("dp")
    return (at == 1) | (at == 2)


def place_of(role, on_line):
    if not on_line:
        return role
    at = lax.axis_index("dp")
    inner = (at == 1) | (at == 2)
    mirror = 3 - at
    step = jnp.where(at < 2, 1, -1)
    return (
        jnp.where(inner, mirror, at + 2 * step),
        jnp.where(inner, mirror + step, at + step),
        at,
        jnp.where(inner, at - step, mirror),
    )[role]


def return_bias_of(tail, role, width):
    piece = width // 4
    row = tail[1:2]
    own = jnp.concatenate([row[:, :piece]] * 4, axis=1)
    lane = lax.broadcasted_iota(jnp.int32, (1, width), 1) // piece
    return jnp.where(lane == place_of(role, True), own, 0.0)


def weight_grads(x, g, act, pg, g_sum, d_ref):
    share, width = act.shape[1], x.shape[1]
    row = lax.broadcasted_iota(jnp.int32, (16, width), 0)
    d_ref[:share] = mm(act, g, TN).astype(BF16)
    d_ref[share : 2 * share] = mm(pg, x, TN).astype(BF16)
    bias = jnp.sum(pg.astype(F32), axis=0, keepdims=True)
    if share < width:
        bias = jnp.concatenate([bias, jnp.zeros((1, width - share), F32)], axis=1)
    d_ref[2 * share :] = jnp.where(row == 0, bias, jnp.where(row == 1, g_sum, 0.0)).astype(BF16)


def early_expert_kernel(n_opts, experts, stride, on_line, rows_of, *refs):
    options = []
    for n in n_opts:
        options.append(refs[:n])
        refs = refs[n:]
    chunks = len(n_opts)
    tails, refs = refs[:2], refs[2:]
    tails = [tail_of([(tails[i], r) for i, r in role]) for role in rows_of]
    x_in, up_in, misc_ref, g_out, acts_out, pgs_out, sum_ref, d_ref = refs[:8]
    x_ref, up_ref, g_ref, acts_ref, pgs_ref, wh_ref, wr_ref, d_scr = refs[8:16]
    in_sems, sems, d_sems, out_sems = refs[16:]
    share, width = wh_ref.shape[0] // chunks, x_ref.shape[1]
    rows = [slice(c * share, (c + 1) * share) for c in range(chunks)]
    x_copies = load(by_code(x_in, x_ref, stride), in_sems)
    waits = [
        fetch(
            options[c],
            chunk_parts(
                share, wh_ref.at[pl.ds(c * share, share)], wr_ref.at[pl.ds(c * share, share)]
            ),
            sems.at[c],
        )
        for c in range(chunks)
    ]
    up_copies = load(by_code(up_in, up_ref, stride), in_sems, experts)
    wait_for(x_copies)
    prob = masked_softmax(mm(x_ref[...], misc_ref[...]), experts)
    lane = lax.broadcasted_iota(jnp.int32, prob.shape, 1)
    mine = lane == ROUTER_COL + lax.axis_index("expert")
    gate = jnp.sum(jnp.where(mine, prob, 0.0), axis=-1, keepdims=True)
    wait_for(up_copies)
    g_ref[...] = (gate * up_ref[...].astype(F32)).astype(BF16)
    copies = load([(g_ref, g_out)], out_sems)
    g_sum = jnp.sum(g_ref[...].astype(F32), axis=0, keepdims=True)
    sum_ref[...] = g_sum
    for c in reversed(range(chunks)):
        wait_for(waits[c])
        act, pg = expert_pair(
            x_ref[...], g_ref[...], wh_ref[rows[c]], wr_ref[rows[c]], hidden_bias_of(tails[c], share)
        )
        acts_ref[c] = act
        pgs_ref[c] = pg
        copies += load(
            [(acts_ref.at[c], acts_out.at[c]), (pgs_ref.at[c], pgs_out.at[c])], out_sems, 1 + 2 * c
        )
        weight_grads(x_ref[...], g_ref[...], act, pg, g_sum, d_scr.at[c])
        copies += load([(d_scr.at[c], d_ref.at[place_of(c, on_line)])], d_sems, c)
    wait_for(copies)


def last_grads_kernel(n_opt, stride, on_line, *refs):
    options, refs = refs[:n_opt], refs[n_opt:]
    sum_ref, x_in, g_in, _, act_out, pg_out, d_ref = refs[:7]
    x_ref, g_ref, wh_ref, wr_ref, tail_ref, act_ref, pg_ref, d_scr, w_sems, sems, x_sems = refs[7:]
    share = wh_ref.shape[0]
    first = load(by_code(x_in, x_ref, stride), x_sems)
    first += fetch(options, [(0, wh_ref), (2 * share, tail_ref)], w_sems.at[0])
    second = load([(g_in, g_ref)], sems) + fetch(options, [(share, wr_ref)], w_sems.at[1])
    wait_for(first)
    pre, half = activation(x_ref[...], wh_ref[...], hidden_bias_of(tail_ref[...].astype(F32), share))
    act = (pre * half).astype(BF16)
    act_ref[...] = act
    copies = load([(act_ref, act_out)], sems, 2)
    wait_for(second)
    pg = (mm(g_ref[...], wr_ref[...], NT) * gelu_slope(pre, half)).astype(BF16)
    pg_ref[...] = pg
    copies += load([(pg_ref, pg_out)], sems, 3)
    weight_grads(x_ref[...], g_ref[...], act, pg, sum_ref[...], d_scr)
    last = place_of(3, True) if on_line else d_ref.shape[0] - 1
    wait_for(copies + load([(d_scr, d_ref.at[last])], sems, 4))


def last_expert_kernel(n_opts, dims, rows_of, *refs):
    experts, capacity, stride, on_line = dims
    options = []
    for n in n_opts:
        options.append(refs[:n])
        refs = refs[n:]
    chunks = len(n_opts)
    tails, refs = refs[: 2 * chunks - 2], refs[2 * chunks - 2 :]
    tails = [
        tail_of([(tails[2 * c + i], r) for i, r in role]) for c, role in enumerate(rows_of)
    ]
    act_in, pg_in, acts_in, pgs_in, up_in, rb_ref, out_hbm = refs[:7]
    ing_outs, refs = refs[7 : 7 + experts // 2], refs[7 + experts // 2 :]
    acts_ref, pgs_ref, up_ref, wh_ref, wr_ref, tail_ref, out_ref, ing_ref, w_sems, sems, row_sems = refs
    width = up_ref.shape[1]
    share = wh_ref.shape[0] // chunks
    own = chunks - 1
    waits = []
    for c in range(chunks):
        rows = pl.ds(c * share, share)
        parts = chunk_parts(share, wh_ref.at[rows], wr_ref.at[rows])
        parts += [(2 * share, tail_ref)] if c == own else []
        waits += fetch(options[c], parts, w_sems.at[c])
    loads = load([(acts_in.at[c], acts_ref.at[c]) for c in range(own)] + [(act_in, acts_ref.at[own])], sems)
    later = load(
        [(pgs_in.at[c], pgs_ref.at[c]) for c in range(own)] + [(pg_in, pgs_ref.at[own])], sems, chunks
    )
    later += load(by_code(up_in, up_ref, stride), row_sems)
    wait_for(waits + loads)
    tails.append(tail_ref[...].astype(F32))
    joined = jnp.concatenate([acts_ref[c] for c in range(chunks)], axis=1)
    bias = rb_ref[...]
    if on_line:
        for c in range(chunks):
            bias = bias + return_bias_of(tails[c], c, width)
    out = (mm(joined, wr_ref[...]) + bias).astype(BF16)
    out_ref[...] = out
    copies = load([(row, at) for at, row in by_code(out_hbm, out_ref, stride)], row_sems, experts)
    wait_for(later)
    joined = jnp.concatenate([pgs_ref[c] for c in range(chunks)], axis=1)
    ing_ref[...] = mm(joined, wh_ref[...]).astype(BF16)
    product = jnp.sum(up_ref[...].astype(F32) * out.astype(F32), axis=-1, keepdims=True)
    lane = lax.broadcasted_iota(jnp.int32, (stride, width), 1)
    row = lax.broadcasted_iota(jnp.int32, (stride, width), 0)
    tail_row = lax.broadcasted_iota(jnp.int32, (16, width), 0) + (stride - 16)
    for s in range(experts):
        own = product[s * stride : (s + 1) * stride]
        line = jnp.sum(jnp.where(lane == row, own, 0.0), axis=0, keepdims=True)
        high = line.astype(BF16).astype(F32)
        at = slice((s + 1) * stride - 16, (s + 1) * stride)
        end = ing_ref[at].astype(F32)
        end = jnp.where(tail_row == capacity, high, end)
        ing_ref[at] = jnp.where(tail_row == capacity + 1, line - high, end).astype(BF16)
    pair = 2 * stride
    copies += load(
        [(ing_ref.at[pl.ds(j * pair, pair)], ref) for j, ref in enumerate(ing_outs)], sems, 2 * chunks
    )
    wait_for(copies)


def finish_kernel(sum_ref, hidden_ref, return_ref, hb_ref, rb_ref):
    share, width = hidden_ref.shape
    return_ref[...] = sum_ref[:share].astype(F32)
    hidden_ref[...] = sum_ref[share : 2 * share].astype(F32)
    tail = sum_ref[2 * share :].astype(F32)
    hb_ref[...] = tail[0:1, :share]
    piece, at = rb_ref.shape[1], lax.axis_index("dp")
    own = jnp.zeros((1, piece), F32)
    for j in range(width // piece):
        own = jnp.where(at == j, tail[1:2, j * piece : (j + 1) * piece], own)
    rb_ref[...] = own


def back_kernel(
    dims, hid_in, up_in, rprob_in, poscol_in, wb_in, ctx_in, qkv_in, probs_in, wa_in, tok_in, *refs,
):
    images, patches, experts, capacity, stride, dp_ex, in_kernel = dims
    (*ing_ins, tgrad_out), refs = refs[: experts + 1], refs[experts + 1 :]
    (
        ing_ref, hid_ref, up_ref, rprob_ref, poscol_ref, wb_ref, ctx_ref, qkv_ref, probs_ref, wa_ref,
        tok_ref, tgrad_ref, sent_ref, dqkv_ref, cg_ref, sems,
    ) = refs[-16:]
    sent_outs = refs[:-16]
    loads = load(
        [
            (
                ing_ins[k // 2 + k % 2 * (experts // 2)].at[pl.ds(k % 2 * stride, stride)],
                ing_ref.at[pl.ds(k * stride, stride)],
            )
            for k in range(experts)
        ]
        + [
            (hid_in, hid_ref), (up_in, up_ref), (rprob_in, rprob_ref), (poscol_in, poscol_ref),
            (wb_in, wb_ref), (ctx_in, ctx_ref), (qkv_in, qkv_ref), (probs_in, probs_ref),
            (wa_in, wa_ref), (tok_in, tok_ref),
        ],
        sems,
    )
    wait_for(loads[: experts + 5])
    tokens, width = tok_ref.shape
    head_size = width // HEADS
    slots = ing_ref.shape[0]
    half, rows = sent_ref.shape[0] // 2, sent_ref.shape[1]
    misc = vectors_of(wb_ref[:, 2 * width :], VECTOR_ROWS)
    hidden = hid_ref[...]
    up = up_ref[...].astype(F32)
    rprob = rprob_ref[...]
    lane = lax.broadcasted_iota(jnp.int32, (stride, width), 1)
    row = lax.broadcasted_iota(jnp.int32, (stride, width), 0)
    mlane = lax.broadcasted_iota(jnp.int32, (stride, MISC), 1)
    columns = []
    expert_at = lax.axis_index("expert")
    for e in range(experts):
        tail = ing_ref[(e + 1) * stride - 16 : (e + 1) * stride].astype(F32)
        block = jnp.zeros((stride, MISC), F32)
        for part in range(2):
            at = capacity - stride + 16 + part
            line = tail[at : at + 1]
            column = jnp.sum(jnp.where(lane == row, line, 0.0), axis=-1, keepdims=True)
            block = jnp.where(mlane == ROUTER_COL * (1 + part) + (expert_at ^ e), column, block)
        columns.append(block.astype(BF16))
    gate_grads = jnp.concatenate(columns, axis=0)
    slane = lax.broadcasted_iota(jnp.int32, (1, slots), 1)
    block_of = jnp.zeros((1, slots), jnp.int32)
    for e in range(experts):
        block_of = jnp.where(slane >= e * stride, (expert_at ^ e) - e, block_of)
    slane = slane + block_of * stride
    either = one_hot((slane == poscol_ref[:, 0:1]) | (slane == poscol_ref[:, 1:2]))
    spread = mm(either, gate_grads)
    rlane = lax.broadcasted_iota(jnp.int32, (tokens, MISC), 1)
    inside = (rlane >= ROUTER_COL) & (rlane < ROUTER_COL + experts)
    prob_grad = jnp.where(inside, spread + pltpu.roll(spread, MISC - ROUTER_COL, 1), 0.0)
    logit_low = (
        rprob * (prob_grad - jnp.sum(prob_grad * rprob, axis=-1, keepdims=True))
    ).astype(BF16)
    unit2, rstd2 = normed(hidden)
    second_low = (unit2 * misc[5:6] + misc[6:7]).astype(BF16)
    router_grad = mm(second_low, logit_low, TN)
    second_grad = mm(logit_low, wb_ref[:, 2 * width :], NT) + mm(either, ing_ref[...])
    gain2_grad = jnp.sum(second_grad * unit2, axis=0, keepdims=True)
    shift2_grad = jnp.sum(second_grad, axis=0, keepdims=True)
    residual = up + norm_back(second_grad, misc[5:6], unit2, rstd2)
    proj_in = residual.astype(BF16)
    proj_b_grad = jnp.sum(proj_in.astype(F32), axis=0, keepdims=True)
    cg_ref[...] = mm(proj_in, wb_ref[:, width : 2 * width], NT).astype(BF16)
    wait_for(loads[experts + 5 :])
    proj_w_grad = mm(ctx_ref[...], proj_in, TN)
    scale = 1.0 / math.sqrt(head_size)
    quad_width = QUAD * head_size
    for i in range(images):
        at = slice(i * patches, (i + 1) * patches)
        for quad in range(HEADS // QUAD):
            lo = quad * quad_width
            q = qkv_ref[at, lo : lo + quad_width]
            k = qkv_ref[at, width + lo : width + lo + quad_width]
            v = qkv_ref[at, 2 * width + lo : 2 * width + lo + quad_width]
            cg = head_stack(cg_ref[at, lo : lo + quad_width], head_size)
            probs_low = probs_ref[i * (HEADS // QUAD) + quad]
            probs = probs_low.astype(F32)
            weight_grad = mm(cg, v, NT)
            value_grad = mm(probs_low, cg, TN)
            score_grad = (
                probs * (weight_grad - jnp.sum(weight_grad * probs, axis=-1, keepdims=True))
            ).astype(BF16)
            query_grad = head_merge(mm(score_grad, k), patches, head_size) * scale
            key_grad = mm(score_grad, head_stack(q, head_size), TN) * scale
            dqkv_ref[at, lo : lo + quad_width] = query_grad.astype(BF16)
            dqkv_ref[at, width + lo : width + lo + quad_width] = key_grad.astype(BF16)
            dqkv_ref[at, 2 * width + lo : 2 * width + lo + quad_width] = value_grad.astype(BF16)
    unit1, rstd1 = normed(tok_ref[...].astype(F32))
    first_low = (unit1 * misc[0:1] + misc[1:2]).astype(BF16)
    query_b_grad = jnp.sum(dqkv_ref[:, :width].astype(F32), axis=0, keepdims=True)
    value_b_grad = jnp.sum(dqkv_ref[:, 2 * width :].astype(F32), axis=0, keepdims=True)
    first_grad = mm(dqkv_ref[:, : 2 * width], wa_ref[...], NT) + mm(
        dqkv_ref[:, 2 * width :], wb_ref[:, :width], NT
    )
    gain1_grad = jnp.sum(first_grad * unit1, axis=0, keepdims=True)
    shift1_grad = jnp.sum(first_grad, axis=0, keepdims=True)
    tgrad_ref[...] = (residual + norm_back(first_grad, misc[0:1], unit1, rstd1)).astype(BF16)
    copies = load([(tgrad_ref, tgrad_out)], sems)
    small = jnp.concatenate(
        [
            gain1_grad, shift1_grad, query_b_grad, value_b_grad,
            proj_b_grad, gain2_grad, shift2_grad, jnp.zeros((VECTOR_ROWS - 7, width), F32),
        ],
        axis=0,
    )
    tail = (router_grad + blocks_of(small)).astype(BF16)
    first_t = first_low.astype(F32).T.astype(BF16)
    da = mm(first_t, dqkv_ref[:, : 2 * width]).astype(BF16)
    dv = mm(first_t, dqkv_ref[:, 2 * width :]).astype(BF16)
    grads = jnp.concatenate([da, dv, proj_w_grad.astype(BF16), tail], axis=1)
    me = position(dp_ex, in_kernel)
    core = me % 2
    dp, ex = dp_ex
    for r in range(0, 2 * half, 2):
        even, odd = grads[r * rows : (r + 1) * rows], grads[(r + 1) * rows : (r + 2) * rows]
        rel = r ^ me
        to = (rel % ex) // 2 * dp + rel // ex if in_kernel else r // 2
        sent_ref[to] = jnp.where(core == 0, even, odd)
        sent_ref[half + to] = jnp.where(core == 0, odd, even)
    each = 2 * half // len(sent_outs)
    copies += load(
        [(sent_ref.at[pl.ds(n * each, each)], out) for n, out in enumerate(sent_outs)], sems, 1
    )
    wait_for(copies)


def final_kernel(*refs):
    ins, (qkv_ref, proj_ref, misc_ref) = refs[:-3], refs[-3:]
    total = functools.reduce(lambda t, r: t + r[...].astype(F32), ins[1:], ins[0][...].astype(F32))
    width = proj_ref.shape[1]
    qkv_ref[...] = total[:, : 3 * width]
    proj_ref[...] = total[:, 3 * width : 4 * width]
    misc_ref[...] = total[:, 4 * width :]


def mix_kernel(experts, hid_ref, ret_ref, rprob_ref, poscol_ref, block_ref):
    tokens, slots = hid_ref.shape[0], ret_ref.shape[0]
    rprob = rprob_ref[...]
    lane = lax.broadcasted_iota(jnp.int32, (tokens, slots), 1)
    rlane = lax.broadcasted_iota(jnp.int32, (tokens, MISC), 1)
    mixed = hid_ref[...]
    for k in range(2):
        pos = poscol_ref[:, k : k + 1]
        picked = mm(one_hot(lane == pos), ret_ref[...])
        hot = (rlane == ROUTER_COL + poscol_ref[:, 2 + k : 3 + k]) & (pos >= 0)
        mixed = mixed + jnp.sum(jnp.where(hot, rprob, 0.0), axis=-1, keepdims=True) * picked
    block_ref[...] = mixed.astype(BF16)


def turn(blocks, at):
    part = blocks[:, :, at : at + VECTOR_ROWS]
    return blocks.at[:, :, at : at + VECTOR_ROWS].set(jnp.swapaxes(part, 1, 2))


def flip(x, stage):
    axis, size, bit = stage
    return lax.ppermute(x, axis, [(i, i ^ bit) for i in range(size)])


def line_permute(x, pairs):
    return lax.ppermute(x, "dp", pairs)


INWARD, ACROSS, OUTWARD = [(0, 1), (3, 2)], [(1, 2), (2, 1)], [(1, 0), (2, 3)]
SIDE = INWARD + OUTWARD


def add(a, b):
    return (a.astype(F32) + b.astype(F32)).astype(BF16)


def on_device(
    tokens, patch_counts, expert_ids, priority, out_grad, first_gain, first_shift, qkv_weight,
    query_bias, value_bias, proj_weight, proj_bias, second_gain, second_shift, router_weight,
    hidden_weight, hidden_bias, return_weight, return_bias, *, dp, ex,
):
    images, patches, width = tokens.shape
    count = images * patches
    top = expert_ids.shape[2]
    experts = router_weight.shape[1]
    capacity = (count * top * 105 + 100 * experts - 1) // (100 * experts)
    stride = (capacity + 2 + 15) // 16 * 16
    slots = experts * stride
    devices = dp * ex
    share_rows = qkv_weight.shape[0]
    ff_share = hidden_weight.shape[1]
    piece = width // dp
    dp_at = lax.axis_index("dp")
    ex_at = lax.axis_index("expert")
    me = dp_at * ex + ex_at
    in_kernel = share_rows % 16 == 0
    on_line = dp == 4

    vectors = [
        first_gain, first_shift, query_bias, value_bias, proj_bias, second_gain, second_shift,
    ]
    small = jnp.pad(router_weight, ((0, 0), (ROUTER_COL, MISC - ROUTER_COL - experts)))
    for j, vector in enumerate(vectors):
        if in_kernel:
            at = ((j, share_rows - 1 - j), (0, MISC - share_rows))
            small = small + jnp.pad(vector[None], at)
        else:
            small = small + jnp.pad(vector[:, None], ((0, 0), (j, MISC - 1 - j)))
    packed = jnp.concatenate([qkv_weight, proj_weight, small], axis=1)[None]
    tail = jnp.pad(hidden_bias, ((0, 15), (0, width - ff_share)))
    tail = tail + jnp.pad(return_bias, ((1, 14), (0, width - piece)))
    own = jnp.concatenate([hidden_weight[0], return_weight[0], tail], axis=0)
    if on_line:
        own, packed = lax.optimization_barrier((own, packed))
        side = line_permute(own, SIDE)
        across1 = line_permute(own, ACROSS)
    else:
        expert_w = lax.all_gather(own, "dp", axis=0)

    packed = jnp.concatenate([flip(packed, ("dp", dp, k)) if k else packed for k in range(dp)], axis=0)
    chips = ex // 2
    core = ("expert", ex, 1)

    if in_kernel:
        packed, patch_counts, expert_ids, priority = lax.optimization_barrier(
            (packed, patch_counts, expert_ids, priority)
        )
    valid = (
        lax.broadcasted_iota(jnp.int32, (images, patches), 1) < patch_counts[:, None]
    ).reshape(count)
    choices = expert_ids.reshape(count, top)
    rank = priority[0]
    earlier = (rank[:, None] > rank[None, :]).astype(BF16)
    iota = jnp.arange(experts, dtype=jnp.int32)
    hot = choices[:, :, None] == iota[None, None, :]
    hot_valid = (hot & valid[:, None, None]).astype(BF16).reshape(count, top * experts)
    before = jnp.dot(earlier, hot_valid, preferred_element_type=F32).reshape(count, top, experts)
    totals = jnp.sum(hot_valid.astype(F32), axis=0).reshape(top, experts)
    start = jnp.cumsum(totals, axis=0) - totals
    slot = jnp.sum(jnp.where(hot, before + start[None], 0.0), axis=-1).astype(jnp.int32)
    kept = valid[:, None] & (slot < capacity)
    pos = jnp.where(kept, choices * stride + slot, -1)
    pos_row = pos.T
    meta = jnp.concatenate([pos_row, choices.T], axis=0)
    meta = jnp.pad(meta, ((0, 4), (0, -count % MISC)))

    pieces = [flip(packed, ("expert", ex, 2 * j)) if j else packed for j in range(chips)]
    pieces += [flip(p, core) for p in pieces]
    rels = [[k * ex + 2 * j + b for k in range(dp)] for b in range(2) for j in range(chips)]
    if in_kernel:
        block_rows = share_rows
        kernel_rels = rels
    else:
        blocks, block_rows = width // 16, 16
        kernel_rels = [list(range(blocks))]
        at = np.argsort(np.array(sum(rels, [])))
        whole = jnp.concatenate(pieces, axis=0)[jnp.asarray(at)[jnp.arange(devices) ^ me]]
        pieces = [turn(whole.reshape(blocks, 16, -1), 4 * width)]

    pick = jnp.zeros((slots, count), jnp.bool_)
    slot_iota = lax.broadcasted_iota(jnp.int32, (slots, count), 0)
    for k in range(top):
        pick = pick | (slot_iota == pos_row[k][None, :])
    up = out_grad.reshape(count, width)
    up_slots = jnp.dot(pick.astype(BF16), up, preferred_element_type=F32).astype(BF16)

    pieces = [flip(packed, ("expert", ex, 2 * j)) if j else packed for j in range(chips)]
    pieces += [flip(p, core) for p in pieces]
    rels = [[k * ex + 2 * j + b for k in range(dp)] for b in range(2) for j in range(chips)]
    if in_kernel:
        block_rows = share_rows
        kernel_rels = rels
    else:
        blocks, block_rows = width // 16, 16
        kernel_rels = [list(range(blocks))]
        at = np.argsort(np.array(sum(rels, [])))
        whole = jnp.concatenate(pieces, axis=0)[jnp.asarray(at)[jnp.arange(devices) ^ me]]
        pieces = [turn(whole.reshape(blocks, 16, -1), 4 * width)]

    def exchange(x):
        x = lax.all_to_all(
            x.reshape(experts, stride, width), "expert", split_axis=0, concat_axis=0, tiled=True
        )
        return x.reshape(slots, width)


    tok = tokens.reshape(count, width)
    pairs = images * (HEADS // QUAD)
    if on_line:
        tails = biases([side, across1, own], 2 * ff_share, HOP1_COST)
        pieces, tails, side, across1 = lax.optimization_barrier((pieces, tails, side, across1))
        across2 = line_permute(side, ACROSS)
        out2 = line_permute(across1, OUTWARD)
    up_arrived = exchange(up_slots)
    made = (
        ((width, 2 * width), BF16),
        ((width, 2 * width + MISC), BF16),
        ((count, 3 * width), BF16),
        ((pairs, QUAD * patches, patches), BF16),
        ((count, width), BF16),
        ((count, width), F32),
        ((count, MISC), F32),
        ((slots, width), BF16),
        ((width, MISC), BF16),
        ((count, MISC), jnp.int32),
    )
    wa, wb, qkv, probs, ctx, hidden, rprob, dispatch, misc, pos_col = pl.pallas_call(
        functools.partial(
            front_kernel, (images, patches, experts, (dp, ex), in_kernel, kernel_rels)
        ),
        out_shape=tuple(shape(*m) for m in made),
        in_specs=[smem()] + [vmem()] * (2 + len(pieces)),
        out_specs=(vmem(),) * 10,
        compiler_params=params(56),
        cost_estimate=cost(0),
        name="front",
    )(patch_counts, tok, meta, *pieces)

    dispatch, up_arrived = lax.optimization_barrier((dispatch, up_arrived))
    arrived = exchange(dispatch)
    if on_line:
        chunks = [(out2, across1), (side, across2), (own,)]
        tails2 = biases([across2, out2], 2 * ff_share, HOP2_COST)
        out3 = line_permute(across2, OUTWARD)
        last, early_tails = (out3, side), (tails, tails2)
        rows_of = [((1, 16), (0, 16)), ((0, 0), (1, 0)), ((0, 32),), ((1, 0), (0, 0))]
        return_add = jnp.zeros((1, width), F32)
    else:
        chunks = [(expert_w[c],) for c in range(dp)]
        chunks, last = chunks[:-1], chunks[-1]
        tails = expert_w[:, 2 * ff_share :].reshape(dp * 16, width)
        early_tails = (tails, tails)
        rows_of = [((0, c * 16),) for c in range(dp)]
        return_add = expert_w[:, 2 * ff_share + 1, :piece].reshape(1, width).astype(F32)

    sem = pltpu.SemaphoreType.DMA
    early = dp - 1
    options = [len(c) for c in chunks]
    wide = shape((slots, width))
    matrix = pltpu.VMEM((ff_share, width), BF16)
    grad_rows = 2 * ff_share + 16
    grad = pltpu.VMEM((grad_rows, width), BF16)
    row_buffer, sum_buffer = pltpu.VMEM((slots, width), BF16), pltpu.VMEM((slots, width), F32)
    dma = lambda n: pltpu.SemaphoreType.DMA((n,))
    several = shape((early, slots, ff_share))
    g, acts, pgs, g_sum, d_all = pl.pallas_call(
        functools.partial(early_expert_kernel, options, experts, stride, on_line, rows_of[:-1]),
        out_shape=(
            wide, several, several, shape((1, width), F32), shape((dp, grad_rows, width)),
        ),
        in_specs=[anywhere()] * sum(options) + [vmem()] * 2 + [anywhere()] * 2 + [vmem()],
        out_specs=(anywhere(),) * 3 + (vmem(), anywhere()),
        scratch_shapes=[row_buffer] * 3
        + [pltpu.VMEM(several.shape, BF16)] * 2
        + [pltpu.VMEM((early * ff_share, width), BF16)] * 2
        + [pltpu.VMEM((early, grad_rows, width), BF16)]
        + [dma(2 * experts), dma(early), dma(early), dma(1 + 2 * early)],
        compiler_params=params(56),
        cost_estimate=cost(0),
        name="experts_early",
    )(*sum(chunks, ()), *early_tails, arrived, up_arrived, misc)
    if on_line:
        out3, g = lax.optimization_barrier((out3, g))
        last = (out3, side)
    operands = (*last, g_sum, arrived, g, d_all)
    narrow, part_buffer = shape((slots, ff_share)), pltpu.VMEM((slots, ff_share), BF16)
    act, pg, d_all = pl.pallas_call(
        functools.partial(last_grads_kernel, len(last), stride, on_line),
        out_shape=(narrow, narrow, shape((dp, grad_rows, width))),
        in_specs=[anywhere()] * len(last) + [vmem()] + [anywhere()] * 3,
        out_specs=(anywhere(),) * 3,
        scratch_shapes=[row_buffer, row_buffer, matrix, matrix, pltpu.VMEM((16, width), BF16)]
        + [part_buffer, part_buffer, grad, dma(2), dma(5), dma(experts)],
        input_output_aliases={len(operands) - 1: 2},
        compiler_params=params(56),
        cost_estimate=cost(HOP3_COST),
        name="last_grads",
    )(*operands)
    options = options + [len(last)]
    expert_out, *in_grad = pl.pallas_call(
        functools.partial(
            last_expert_kernel, options, (experts, capacity, stride, on_line), rows_of[:-1]
        ),
        out_shape=(wide,) + (shape((2 * stride, width)),) * chips,
        in_specs=[anywhere()] * sum(options) + [vmem()] * (2 * early) + [anywhere()] * 5 + [vmem()],
        out_specs=(anywhere(),) * (1 + chips),
        scratch_shapes=[pltpu.VMEM((dp, slots, ff_share), BF16)] * 2
        + [row_buffer]
        + [pltpu.VMEM((dp * ff_share, width), BF16)] * 2
        + [pltpu.VMEM((16, width), BF16), row_buffer, row_buffer, dma(dp), dma(2 * dp + chips), dma(2 * experts)],
        compiler_params=params(56),
        cost_estimate=cost(0),
        name="experts_last",
    )(
        *sum(chunks, ()), *last, *(early_tails * early),
        act, pg, acts, pgs, up_arrived, return_add,
    )
    gone = [flip(d, ("expert", ex, 2 * j)) if j else d for j, d in enumerate(in_grad)]
    expert_out, gone[1:] = lax.optimization_barrier((expert_out, gone[1:]))
    gone += [flip(d, core) for d in gone]
    returned = exchange(expert_out)
    d_sum = lax.psum_scatter(d_all, "dp", scatter_dimension=0, tiled=False)

    half = width // block_rows // 2
    pieces_out = chips if in_kernel else 1
    operands = (hidden, up, rprob, pos_col, wb, ctx, qkv, probs, wa, tok)
    tokens_grad, *sent = pl.pallas_call(
        functools.partial(
            back_kernel, (images, patches, experts, capacity, stride, (dp, ex), in_kernel)
        ),
        out_shape=(shape((count, width)),)
        + (shape((half // pieces_out, block_rows, 4 * width + MISC)),) * (2 * pieces_out),
        in_specs=[anywhere()] * (10 + experts),
        out_specs=(anywhere(),) * (1 + 2 * pieces_out),
        scratch_shapes=[row_buffer]
        + [pltpu.VMEM(b.shape, b.dtype) for b in operands]
        + [
            pltpu.VMEM((count, width), BF16),
            pltpu.VMEM((2 * half, block_rows, 4 * width + MISC), BF16),
            pltpu.VMEM((count, 3 * width), BF16),
            pltpu.VMEM((count, width), BF16),
            dma(10 + max(experts, 2 * pieces_out)),
        ],
        compiler_params=params(56),
        cost_estimate=cost(0),
        name="back",
    )(*operands, *gone)

    if not in_kernel:
        whole = jnp.stack(sent, axis=1).reshape(2 * half, block_rows, -1)
        whole = turn(whole, 4 * width).reshape(devices, share_rows, -1)
        whole = whole[jnp.asarray(np.array(sum(rels, []))) ^ me]
        sent = [whole[j * dp : (j + 1) * dp] for j in range(2 * chips)]
    sent, returned = lax.optimization_barrier((sent, returned))
    came = [flip(d, core) for d in sent[chips:]]
    parts = [add(k, c) for k, c in zip(sent[:chips], came)]
    moved = [flip(parts[j], ("expert", ex, 2 * j)) for j in range(1, chips)]
    total = functools.reduce(lambda t, m: t + m.astype(F32), moved, parts[0].astype(F32)).astype(BF16)
    block_out = pl.pallas_call(
        functools.partial(mix_kernel, experts),
        out_shape=shape((count, width)),
        in_specs=[vmem()] * 4,
        out_specs=vmem(),
        compiler_params=params(56),
        cost_estimate=cost(0),
        name="mix",
    )(hidden, returned, rprob, pos_col)
    total, block_out = lax.optimization_barrier((total, block_out))
    last_came = [flip(total[k], ("dp", dp, k)) for k in range(1, dp)]
    hidden_sum, return_sum, hidden_bias_sum, return_bias_sum = pl.pallas_call(
        finish_kernel,
        out_shape=(
            shape((ff_share, width), F32), shape((ff_share, width), F32),
            shape((1, ff_share), F32), shape((1, piece), F32),
        ),
        in_specs=[vmem()],
        out_specs=(vmem(),) * 4,
        compiler_params=params(56),
        cost_estimate=cost(0),
        name="finish",
    )(d_sum)
    last_came, hidden_sum, return_sum = lax.optimization_barrier((last_came, hidden_sum, return_sum))
    final_shapes = (shape((share_rows, 3 * width), F32), shape((share_rows, width), F32))
    qkv_sum, proj_sum, final = pl.pallas_call(
        final_kernel,
        out_shape=final_shapes + (shape((share_rows, MISC), F32),),
        in_specs=[vmem()] * dp,
        out_specs=(vmem(),) * 3,
        compiler_params=params(24),
        cost_estimate=cost(0),
        name="final",
    )(total[0], *last_came)
    if in_kernel:
        vec = [final[j, :share_rows] for j in range(7)]
    else:
        vec = [final[:, j] for j in range(7)]
    router_sum = final[:, ROUTER_COL : ROUTER_COL + experts]
    return (
        block_out.reshape(tokens.shape),
        tokens_grad.reshape(tokens.shape),
        vec[0], vec[1], qkv_sum, vec[2], vec[3], proj_sum, vec[4], vec[5], vec[6], router_sum,
        hidden_sum[None],
        hidden_bias_sum,
        return_sum[None],
        return_bias_sum,
    )


def solution(mesh):
    both, rows = P(("dp", "expert")), P(("dp", "expert"), None)
    cube = P(("dp", "expert"), None, None)
    weight, bias = P("expert", "dp", None), P("expert", "dp")
    in_specs = (
        cube, both, cube, rows, cube, both, both, rows, both, both, rows, both, both, both, rows,
        weight, bias, weight, bias,
    )
    out_specs = (
        cube, cube, both, both, rows, both, both, rows, both, both, both, rows,
        weight, bias, weight, bias,
    )
    return jax.shard_map(
        functools.partial(on_device, dp=mesh.shape["dp"], ex=mesh.shape["expert"]),
        mesh=mesh,
        in_specs=in_specs,
        out_specs=out_specs,
        check_vma=False,
    )
```

```python
import functools
import math

import jax
import jax.numpy as jnp
import numpy as np
from jax import lax
from jax.experimental import pallas as pl
from jax.experimental.pallas import tpu as pltpu
from jax.sharding import PartitionSpec as P

HEADS = 8
QUAD = 4
norm_eps = 1e-06
neg_large = -1e30
F32 = jnp.float32
BF16 = jnp.bfloat16
ROUTER_COL = 32
MISC = 128
VECTOR_ROWS = 16
HOP1_COST, HOP2_COST, HOP3_COST = 10, 40, 40
GELU_C = math.sqrt(2.0 / math.pi)
GELU_A = 0.044715

NN = (((1,), (0,)), ((), ()))
NT = (((1,), (1,)), ((), ()))
TN = (((0,), (0,)), ((), ()))


def mm(a, b, dims=NN):
    return lax.dot_general(a, b, dims, preferred_element_type=F32)


def params(mib=28):
    return pltpu.CompilerParams(vmem_limit_bytes=mib * 1024 * 1024)


def cost(us):
    return pl.CostEstimate(flops=us * 10**9, bytes_accessed=0, transcendentals=0)


def vmem():
    return pl.BlockSpec(memory_space=pltpu.VMEM)


def smem():
    return pl.BlockSpec(memory_space=pltpu.SMEM)


def anywhere():
    return pl.BlockSpec(memory_space=pl.ANY)


def hbm():
    return pl.BlockSpec(memory_space=pltpu.HBM)


def load(pairs, sems, first=0):
    copies = [
        pltpu.make_async_copy(source, dst, sems.at[first + n]) for n, (source, dst) in enumerate(pairs)
    ]
    for copy in copies:
        copy.start()
    return copies


def wait_for(copies):
    for copy in copies:
        copy.wait()


def shape(dims, dtype=BF16):
    return jax.ShapeDtypeStruct(dims, dtype)


def one_hot(mask):
    return mask.astype(F32).astype(BF16)


def normed(values):
    center = values - jnp.mean(values, axis=-1, keepdims=True)
    rstd = lax.rsqrt(jnp.mean(center * center, axis=-1, keepdims=True) + norm_eps)
    return center * rstd, rstd


def norm_back(grad, gain, unit, rstd):
    q = grad * gain
    return rstd * (
        q
        - jnp.mean(q, axis=-1, keepdims=True)
        - unit * jnp.mean(q * unit, axis=-1, keepdims=True)
    )


def vectors_of(misc, rows):
    width = misc.shape[0]
    lane = lax.broadcasted_iota(jnp.int32, (rows, width), 1)
    row = lax.broadcasted_iota(jnp.int32, (rows, width), 0)
    spread = mm(misc[:, :rows], one_hot(lane % rows == row))
    lane = lax.broadcasted_iota(jnp.int32, (width, width), 1)
    row = lax.broadcasted_iota(jnp.int32, (width, width), 0)
    spread = jnp.where(lane // rows == row // rows, spread, 0.0)
    return jnp.sum(spread.reshape(width // rows, rows, width), axis=0)


def blocks_of(vectors):
    rows, width = vectors.shape
    spread = jnp.concatenate([vectors] * (width // rows), axis=0)
    lane = lax.broadcasted_iota(jnp.int32, (width, width), 1)
    row = lax.broadcasted_iota(jnp.int32, (width, width), 0)
    spread = jnp.where(lane // rows == row // rows, spread, 0.0).astype(BF16)
    row = lax.broadcasted_iota(jnp.int32, (width, MISC), 0)
    lane = lax.broadcasted_iota(jnp.int32, (width, MISC), 1)
    return mm(spread, one_hot(row % rows == lane))


def masked_softmax(logits, experts):
    lane = lax.broadcasted_iota(jnp.int32, logits.shape, 1)
    inside = (lane >= ROUTER_COL) & (lane < ROUTER_COL + experts)
    logits = jnp.where(inside, logits, neg_large)
    raised = jnp.exp(logits - jnp.max(logits, axis=-1, keepdims=True))
    return raised / jnp.sum(raised, axis=-1, keepdims=True)


def head_stack(rows, head_size):
    lane = lax.broadcasted_iota(jnp.int32, rows.shape, 1) // head_size
    return jnp.concatenate(
        [jnp.where(lane == h, rows, jnp.zeros_like(rows)) for h in range(QUAD)], axis=0
    )


def head_merge(stacked, patches, head_size):
    lane = lax.broadcasted_iota(jnp.int32, (patches, stacked.shape[1]), 1) // head_size
    total = jnp.zeros((patches, stacked.shape[1]), F32)
    for h in range(QUAD):
        total = jnp.where(lane == h, stacked[h * patches : (h + 1) * patches], total)
    return total


def position(dp_ex, in_kernel):
    if not in_kernel:
        return jnp.int32(0)
    return lax.axis_index("dp") * dp_ex[1] + lax.axis_index("expert")


def front_kernel(dims, cnt_ref, tok_ref, meta_ref, *refs):
    images, patches, experts, dp_ex, in_kernel, rels = dims
    pieces, refs = refs[: len(rels)], refs[len(rels) :]
    (
        wa_ref, wb_ref, qkv_ref, probs_ref, ctx_ref, hid_ref, rprob_ref, disp_ref, misc_ref, col_ref,
    ) = refs
    width = tok_ref.shape[1]
    head_size = width // HEADS
    rows = pieces[0].shape[1]
    me = position(dp_ex, in_kernel)
    for ref, rel in zip(pieces, rels):
        for slot, code in enumerate(rel):
            at = pl.multiple_of((me ^ code) * rows, rows)
            wa_ref[pl.ds(at, rows), :] = ref[slot, :, : 2 * width]
            wb_ref[pl.ds(at, rows), :] = ref[slot, :, 2 * width :]
    misc_ref[...] = wb_ref[:, 2 * width :]
    misc = vectors_of(wb_ref[:, 2 * width :], VECTOR_ROWS)
    x = tok_ref[...].astype(F32)
    unit, _ = normed(x)
    first_low = (unit * misc[0:1] + misc[1:2]).astype(BF16)
    qk = mm(first_low, wa_ref[...])
    qkv_ref[:, :width] = (qk[:, :width] + misc[2:3]).astype(BF16)
    qkv_ref[:, width : 2 * width] = qk[:, width:].astype(BF16)
    qkv_ref[:, 2 * width :] = (mm(first_low, wb_ref[:, :width]) + misc[3:4]).astype(BF16)
    scale = 1.0 / math.sqrt(head_size)
    quad_width = QUAD * head_size
    for i in range(images):
        at = slice(i * patches, (i + 1) * patches)
        valid = lax.broadcasted_iota(jnp.int32, (QUAD * patches, patches), 1) < cnt_ref[i]
        for quad in range(HEADS // QUAD):
            lo = quad * quad_width
            q = qkv_ref[at, lo : lo + quad_width]
            k = qkv_ref[at, width + lo : width + lo + quad_width]
            v = qkv_ref[at, 2 * width + lo : 2 * width + lo + quad_width]
            scores = jnp.where(valid, mm(head_stack(q, head_size), k, NT) * scale, neg_large)
            raised = jnp.exp(scores - jnp.max(scores, axis=-1, keepdims=True))
            probs = (raised / jnp.sum(raised, axis=-1, keepdims=True)).astype(BF16)
            probs_ref[i * (HEADS // QUAD) + quad] = probs
            ctx = head_merge(mm(probs, v), patches, head_size)
            ctx_ref[at, lo : lo + quad_width] = ctx.astype(BF16)
    hidden = x + mm(ctx_ref[...], wb_ref[:, width : 2 * width]) + misc[4:5]
    hid_ref[...] = hidden
    unit2, _ = normed(hidden)
    second_low = (unit2 * misc[5:6] + misc[6:7]).astype(BF16)
    rprob_ref[...] = masked_softmax(mm(second_low, wb_ref[:, 2 * width :]), experts)
    slots = disp_ref.shape[0]
    count = tok_ref.shape[0]
    row = lax.broadcasted_iota(jnp.int32, (slots, count), 0)
    pick = (row == meta_ref[0:1, :count]) | (row == meta_ref[1:2, :count])
    disp_ref[...] = mm(one_hot(pick), second_low).astype(BF16)
    meta = meta_ref[...].astype(F32)
    meta = jnp.concatenate([meta, jnp.zeros((MISC - 8, meta.shape[1]), F32)], axis=0)
    col_ref[...] = meta.T[:count].astype(jnp.int32)


def by_code(array, buffer, stride):
    me = lax.axis_index("expert")
    return [
        (array.at[pl.ds(pl.multiple_of((me ^ k) * stride, 16), stride)], buffer.at[pl.ds(k * stride, stride)])
        for k in range(array.shape[0] // stride)
    ]


def fetch(options, parts, sem):
    def copies(source):
        return [
            pltpu.make_async_copy(source.at[pl.ds(at, dst.shape[0])], dst, sem) for at, dst in parts
        ]

    if len(options) == 1:
        for copy in copies(options[0]):
            copy.start()
    else:

        @pl.when(jnp.logical_not(is_inner()))
        def _():
            for copy in copies(options[0]):
                copy.start()

        @pl.when(is_inner())
        def _():
            for copy in copies(options[1]):
                copy.start()

    return copies(options[0])


def chunk_parts(share, wh, wr):
    return [(0, wh), (share, wr)]


def bias_kernel(start, *refs):
    sources, (tails, sem) = refs[:-2], refs[-2:]
    copies = [
        pltpu.make_async_copy(source.at[pl.ds(start, 16)], tails.at[pl.ds(c * 16, 16)], sem)
        for c, source in enumerate(sources)
    ]
    for copy in copies:
        copy.start()
    for copy in copies:
        copy.wait()


def biases(chunks, start, us):
    return pl.pallas_call(
        functools.partial(bias_kernel, start),
        out_shape=shape((len(chunks) * 16, chunks[0].shape[1])),
        in_specs=[anywhere()] * len(chunks),
        out_specs=vmem(),
        scratch_shapes=[pltpu.SemaphoreType.DMA],
        compiler_params=params(4),
        cost_estimate=cost(us),
        name="biases",
    )(*chunks)


def tail_of(places):
    tails = [ref[at : at + 16].astype(F32) for ref, at in places]
    if len(tails) == 1:
        return tails[0]
    at = lax.axis_index("dp")
    return jnp.where((at == 1) | (at == 2), tails[1], tails[0])


def activation(x, wh, hb):
    pre = mm(x, wh, NT) + hb
    half = 0.5 + 0.5 * jnp.tanh(pre * (GELU_C + (GELU_C * GELU_A) * (pre * pre)))
    return pre, half


def gelu_slope(pre, half):
    return half * (
        1.0 + (1.0 - half) * (pre * (2.0 * GELU_C + (6.0 * GELU_C * GELU_A) * (pre * pre)))
    )


def expert_pair(x, g, wh, wr, hb):
    pre, half = activation(x, wh, hb)
    act = (pre * half).astype(BF16)
    pg = (mm(g, wr, NT) * gelu_slope(pre, half)).astype(BF16)
    return act, pg


def hidden_bias_of(tail, share):
    return tail[0:1, :share]


def is_inner():
    at = lax.axis_index("dp")
    return (at == 1) | (at == 2)


def place_of(role, on_line):
    if not on_line:
        return role
    at = lax.axis_index("dp")
    inner = (at == 1) | (at == 2)
    mirror = 3 - at
    step = jnp.where(at < 2, 1, -1)
    return (
        jnp.where(inner, mirror, at + 2 * step),
        jnp.where(inner, mirror + step, at + step),
        at,
        jnp.where(inner, at - step, mirror),
    )[role]


def return_bias_of(tail, role, width):
    piece = width // 4
    row = tail[1:2]
    own = jnp.concatenate([row[:, :piece]] * 4, axis=1)
    lane = lax.broadcasted_iota(jnp.int32, (1, width), 1) // piece
    return jnp.where(lane == place_of(role, True), own, 0.0)


def weight_grads(x, g, act, pg, g_sum, d_ref):
    share, width = act.shape[1], x.shape[1]
    row = lax.broadcasted_iota(jnp.int32, (16, width), 0)
    d_ref[:share] = mm(act, g, TN).astype(BF16)
    d_ref[share : 2 * share] = mm(pg, x, TN).astype(BF16)
    bias = jnp.sum(pg.astype(F32), axis=0, keepdims=True)
    if share < width:
        bias = jnp.concatenate([bias, jnp.zeros((1, width - share), F32)], axis=1)
    d_ref[2 * share :] = jnp.where(row == 0, bias, jnp.where(row == 1, g_sum, 0.0)).astype(BF16)


def early_expert_kernel(n_opts, experts, stride, on_line, rows_of, *refs):
    options = []
    for n in n_opts:
        options.append(refs[:n])
        refs = refs[n:]
    chunks = len(n_opts)
    tails, refs = refs[:2], refs[2:]
    tails = [tail_of([(tails[i], r) for i, r in role]) for role in rows_of]
    x_in, up_in, misc_ref, g_out, acts_out, pgs_out, sum_ref, d_ref = refs[:8]
    x_ref, up_ref, g_ref, acts_ref, pgs_ref, wh_ref, wr_ref, d_scr = refs[8:16]
    in_sems, sems, d_sems, out_sems = refs[16:]
    share, width = wh_ref.shape[0] // chunks, x_ref.shape[1]
    rows = [slice(c * share, (c + 1) * share) for c in range(chunks)]
    x_copies = load(by_code(x_in, x_ref, stride), in_sems)
    waits = [
        fetch(
            options[c],
            chunk_parts(
                share, wh_ref.at[pl.ds(c * share, share)], wr_ref.at[pl.ds(c * share, share)]
            ),
            sems.at[c],
        )
        for c in range(chunks)
    ]
    up_copies = load(by_code(up_in, up_ref, stride), in_sems, experts)
    wait_for(x_copies)
    prob = masked_softmax(mm(x_ref[...], misc_ref[...]), experts)
    lane = lax.broadcasted_iota(jnp.int32, prob.shape, 1)
    mine = lane == ROUTER_COL + lax.axis_index("expert")
    gate = jnp.sum(jnp.where(mine, prob, 0.0), axis=-1, keepdims=True)
    wait_for(up_copies)
    g_ref[...] = (gate * up_ref[...].astype(F32)).astype(BF16)
    copies = load([(g_ref, g_out)], out_sems)
    g_sum = jnp.sum(g_ref[...].astype(F32), axis=0, keepdims=True)
    sum_ref[...] = g_sum
    for c in reversed(range(chunks)):
        wait_for(waits[c])
        act, pg = expert_pair(
            x_ref[...], g_ref[...], wh_ref[rows[c]], wr_ref[rows[c]], hidden_bias_of(tails[c], share)
        )
        acts_ref[c] = act
        pgs_ref[c] = pg
        copies += load(
            [(acts_ref.at[c], acts_out.at[c]), (pgs_ref.at[c], pgs_out.at[c])], out_sems, 1 + 2 * c
        )
        weight_grads(x_ref[...], g_ref[...], act, pg, g_sum, d_scr.at[c])
        copies += load([(d_scr.at[c], d_ref.at[place_of(c, on_line)])], d_sems, c)
    wait_for(copies)


def last_grads_kernel(n_opt, stride, on_line, *refs):
    options, refs = refs[:n_opt], refs[n_opt:]
    sum_ref, x_in, g_in, _, act_out, pg_out, d_ref = refs[:7]
    x_ref, g_ref, wh_ref, wr_ref, tail_ref, act_ref, pg_ref, d_scr, w_sems, sems, x_sems = refs[7:]
    share = wh_ref.shape[0]
    first = load(by_code(x_in, x_ref, stride), x_sems)
    first += fetch(options, [(0, wh_ref), (2 * share, tail_ref)], w_sems.at[0])
    second = load([(g_in, g_ref)], sems) + fetch(options, [(share, wr_ref)], w_sems.at[1])
    wait_for(first)
    pre, half = activation(x_ref[...], wh_ref[...], hidden_bias_of(tail_ref[...].astype(F32), share))
    act = (pre * half).astype(BF16)
    act_ref[...] = act
    copies = load([(act_ref, act_out)], sems, 2)
    wait_for(second)
    pg = (mm(g_ref[...], wr_ref[...], NT) * gelu_slope(pre, half)).astype(BF16)
    pg_ref[...] = pg
    copies += load([(pg_ref, pg_out)], sems, 3)
    weight_grads(x_ref[...], g_ref[...], act, pg, sum_ref[...], d_scr)
    last = place_of(3, True) if on_line else d_ref.shape[0] - 1
    wait_for(copies + load([(d_scr, d_ref.at[last])], sems, 4))


def last_expert_kernel(n_opts, dims, rows_of, *refs):
    experts, capacity, stride, on_line = dims
    options = []
    for n in n_opts:
        options.append(refs[:n])
        refs = refs[n:]
    chunks = len(n_opts)
    tails, refs = refs[: 2 * chunks - 2], refs[2 * chunks - 2 :]
    tails = [
        tail_of([(tails[2 * c + i], r) for i, r in role]) for c, role in enumerate(rows_of)
    ]
    act_in, pg_in, acts_in, pgs_in, up_in, rb_ref, out_hbm = refs[:7]
    ing_outs, refs = refs[7 : 7 + experts // 2], refs[7 + experts // 2 :]
    acts_ref, pgs_ref, up_ref, wh_ref, wr_ref, tail_ref, out_ref, ing_ref, w_sems, sems, row_sems = refs
    width = up_ref.shape[1]
    share = wh_ref.shape[0] // chunks
    own = chunks - 1
    waits = []
    for c in range(chunks):
        rows = pl.ds(c * share, share)
        parts = chunk_parts(share, wh_ref.at[rows], wr_ref.at[rows])
        parts += [(2 * share, tail_ref)] if c == own else []
        waits += fetch(options[c], parts, w_sems.at[c])
    loads = load([(acts_in.at[c], acts_ref.at[c]) for c in range(own)] + [(act_in, acts_ref.at[own])], sems)
    later = load(
        [(pgs_in.at[c], pgs_ref.at[c]) for c in range(own)] + [(pg_in, pgs_ref.at[own])], sems, chunks
    )
    later += load(by_code(up_in, up_ref, stride), row_sems)
    wait_for(waits + loads)
    tails.append(tail_ref[...].astype(F32))
    joined = jnp.concatenate([acts_ref[c] for c in range(chunks)], axis=1)
    bias = rb_ref[...]
    if on_line:
        for c in range(chunks):
            bias = bias + return_bias_of(tails[c], c, width)
    out = (mm(joined, wr_ref[...]) + bias).astype(BF16)
    out_ref[...] = out
    copies = load([(row, at) for at, row in by_code(out_hbm, out_ref, stride)], row_sems, experts)
    wait_for(later)
    joined = jnp.concatenate([pgs_ref[c] for c in range(chunks)], axis=1)
    ing_ref[...] = mm(joined, wh_ref[...]).astype(BF16)
    product = jnp.sum(up_ref[...].astype(F32) * out.astype(F32), axis=-1, keepdims=True)
    lane = lax.broadcasted_iota(jnp.int32, (stride, width), 1)
    row = lax.broadcasted_iota(jnp.int32, (stride, width), 0)
    tail_row = lax.broadcasted_iota(jnp.int32, (16, width), 0) + (stride - 16)
    for s in range(experts):
        own = product[s * stride : (s + 1) * stride]
        line = jnp.sum(jnp.where(lane == row, own, 0.0), axis=0, keepdims=True)
        high = line.astype(BF16).astype(F32)
        at = slice((s + 1) * stride - 16, (s + 1) * stride)
        end = ing_ref[at].astype(F32)
        end = jnp.where(tail_row == capacity, high, end)
        ing_ref[at] = jnp.where(tail_row == capacity + 1, line - high, end).astype(BF16)
    pair = 2 * stride
    copies += load(
        [(ing_ref.at[pl.ds(j * pair, pair)], ref) for j, ref in enumerate(ing_outs)], sems, 2 * chunks
    )
    wait_for(copies)


def finish_kernel(sum_ref, hidden_ref, return_ref, hb_ref, rb_ref):
    share, width = hidden_ref.shape
    return_ref[...] = sum_ref[:share].astype(F32)
    hidden_ref[...] = sum_ref[share : 2 * share].astype(F32)
    tail = sum_ref[2 * share :].astype(F32)
    hb_ref[...] = tail[0:1, :share]
    piece, at = rb_ref.shape[1], lax.axis_index("dp")
    own = jnp.zeros((1, piece), F32)
    for j in range(width // piece):
        own = jnp.where(at == j, tail[1:2, j * piece : (j + 1) * piece], own)
    rb_ref[...] = own


def back_kernel(
    dims, hid_in, up_in, rprob_in, poscol_in, wb_in, ctx_in, qkv_in, probs_in, wa_in, tok_in, *refs,
):
    images, patches, experts, capacity, stride, dp_ex, in_kernel = dims
    (*ing_ins, tgrad_out), refs = refs[: experts + 1], refs[experts + 1 :]
    (
        ing_ref, hid_ref, up_ref, rprob_ref, poscol_ref, wb_ref, ctx_ref, qkv_ref, probs_ref, wa_ref,
        tok_ref, tgrad_ref, sent_ref, dqkv_ref, cg_ref, sems,
    ) = refs[-16:]
    sent_outs = refs[:-16]
    loads = load(
        [
            (
                ing_ins[k // 2 + k % 2 * (experts // 2)].at[pl.ds(k % 2 * stride, stride)],
                ing_ref.at[pl.ds(k * stride, stride)],
            )
            for k in range(experts)
        ]
        + [
            (hid_in, hid_ref), (up_in, up_ref), (rprob_in, rprob_ref), (poscol_in, poscol_ref),
            (wb_in, wb_ref), (ctx_in, ctx_ref), (qkv_in, qkv_ref), (probs_in, probs_ref),
            (wa_in, wa_ref), (tok_in, tok_ref),
        ],
        sems,
    )
    wait_for(loads[: experts + 5])
    tokens, width = tok_ref.shape
    head_size = width // HEADS
    slots = ing_ref.shape[0]
    half, rows = sent_ref.shape[0] // 2, sent_ref.shape[1]
    misc = vectors_of(wb_ref[:, 2 * width :], VECTOR_ROWS)
    hidden = hid_ref[...]
    up = up_ref[...].astype(F32)
    rprob = rprob_ref[...]
    lane = lax.broadcasted_iota(jnp.int32, (stride, width), 1)
    row = lax.broadcasted_iota(jnp.int32, (stride, width), 0)
    mlane = lax.broadcasted_iota(jnp.int32, (stride, MISC), 1)
    columns = []
    expert_at = lax.axis_index("expert")
    for e in range(experts):
        tail = ing_ref[(e + 1) * stride - 16 : (e + 1) * stride].astype(F32)
        block = jnp.zeros((stride, MISC), F32)
        for part in range(2):
            at = capacity - stride + 16 + part
            line = tail[at : at + 1]
            column = jnp.sum(jnp.where(lane == row, line, 0.0), axis=-1, keepdims=True)
            block = jnp.where(mlane == ROUTER_COL * (1 + part) + (expert_at ^ e), column, block)
        columns.append(block.astype(BF16))
    gate_grads = jnp.concatenate(columns, axis=0)
    slane = lax.broadcasted_iota(jnp.int32, (1, slots), 1)
    block_of = jnp.zeros((1, slots), jnp.int32)
    for e in range(experts):
        block_of = jnp.where(slane >= e * stride, (expert_at ^ e) - e, block_of)
    slane = slane + block_of * stride
    either = one_hot((slane == poscol_ref[:, 0:1]) | (slane == poscol_ref[:, 1:2]))
    spread = mm(either, gate_grads)
    rlane = lax.broadcasted_iota(jnp.int32, (tokens, MISC), 1)
    inside = (rlane >= ROUTER_COL) & (rlane < ROUTER_COL + experts)
    prob_grad = jnp.where(inside, spread + pltpu.roll(spread, MISC - ROUTER_COL, 1), 0.0)
    logit_low = (
        rprob * (prob_grad - jnp.sum(prob_grad * rprob, axis=-1, keepdims=True))
    ).astype(BF16)
    unit2, rstd2 = normed(hidden)
    second_low = (unit2 * misc[5:6] + misc[6:7]).astype(BF16)
    router_grad = mm(second_low, logit_low, TN)
    second_grad = mm(logit_low, wb_ref[:, 2 * width :], NT) + mm(either, ing_ref[...])
    gain2_grad = jnp.sum(second_grad * unit2, axis=0, keepdims=True)
    shift2_grad = jnp.sum(second_grad, axis=0, keepdims=True)
    residual = up + norm_back(second_grad, misc[5:6], unit2, rstd2)
    proj_in = residual.astype(BF16)
    proj_b_grad = jnp.sum(proj_in.astype(F32), axis=0, keepdims=True)
    cg_ref[...] = mm(proj_in, wb_ref[:, width : 2 * width], NT).astype(BF16)
    wait_for(loads[experts + 5 :])
    proj_w_grad = mm(ctx_ref[...], proj_in, TN)
    scale = 1.0 / math.sqrt(head_size)
    quad_width = QUAD * head_size
    for i in range(images):
        at = slice(i * patches, (i + 1) * patches)
        for quad in range(HEADS // QUAD):
            lo = quad * quad_width
            q = qkv_ref[at, lo : lo + quad_width]
            k = qkv_ref[at, width + lo : width + lo + quad_width]
            v = qkv_ref[at, 2 * width + lo : 2 * width + lo + quad_width]
            cg = head_stack(cg_ref[at, lo : lo + quad_width], head_size)
            probs_low = probs_ref[i * (HEADS // QUAD) + quad]
            probs = probs_low.astype(F32)
            weight_grad = mm(cg, v, NT)
            value_grad = mm(probs_low, cg, TN)
            score_grad = (
                probs * (weight_grad - jnp.sum(weight_grad * probs, axis=-1, keepdims=True))
            ).astype(BF16)
            query_grad = head_merge(mm(score_grad, k), patches, head_size) * scale
            key_grad = mm(score_grad, head_stack(q, head_size), TN) * scale
            dqkv_ref[at, lo : lo + quad_width] = query_grad.astype(BF16)
            dqkv_ref[at, width + lo : width + lo + quad_width] = key_grad.astype(BF16)
            dqkv_ref[at, 2 * width + lo : 2 * width + lo + quad_width] = value_grad.astype(BF16)
    unit1, rstd1 = normed(tok_ref[...].astype(F32))
    first_low = (unit1 * misc[0:1] + misc[1:2]).astype(BF16)
    query_b_grad = jnp.sum(dqkv_ref[:, :width].astype(F32), axis=0, keepdims=True)
    value_b_grad = jnp.sum(dqkv_ref[:, 2 * width :].astype(F32), axis=0, keepdims=True)
    first_grad = mm(dqkv_ref[:, : 2 * width], wa_ref[...], NT) + mm(
        dqkv_ref[:, 2 * width :], wb_ref[:, :width], NT
    )
    gain1_grad = jnp.sum(first_grad * unit1, axis=0, keepdims=True)
    shift1_grad = jnp.sum(first_grad, axis=0, keepdims=True)
    tgrad_ref[...] = (residual + norm_back(first_grad, misc[0:1], unit1, rstd1)).astype(BF16)
    copies = load([(tgrad_ref, tgrad_out)], sems)
    small = jnp.concatenate(
        [
            gain1_grad, shift1_grad, query_b_grad, value_b_grad,
            proj_b_grad, gain2_grad, shift2_grad, jnp.zeros((VECTOR_ROWS - 7, width), F32),
        ],
        axis=0,
    )
    tail = (router_grad + blocks_of(small)).astype(BF16)
    first_t = first_low.astype(F32).T.astype(BF16)
    da = mm(first_t, dqkv_ref[:, : 2 * width]).astype(BF16)
    dv = mm(first_t, dqkv_ref[:, 2 * width :]).astype(BF16)
    grads = jnp.concatenate([da, dv, proj_w_grad.astype(BF16), tail], axis=1)
    me = position(dp_ex, in_kernel)
    core = me % 2
    dp, ex = dp_ex
    for r in range(0, 2 * half, 2):
        even, odd = grads[r * rows : (r + 1) * rows], grads[(r + 1) * rows : (r + 2) * rows]
        rel = r ^ me
        to = (rel % ex) // 2 * dp + rel // ex if in_kernel else r // 2
        sent_ref[to] = jnp.where(core == 0, even, odd)
        sent_ref[half + to] = jnp.where(core == 0, odd, even)
    each = 2 * half // len(sent_outs)
    copies += load(
        [(sent_ref.at[pl.ds(n * each, each)], out) for n, out in enumerate(sent_outs)], sems, 1
    )
    wait_for(copies)


def final_kernel(*refs):
    ins, (qkv_ref, proj_ref, misc_ref, turned_ref) = refs[:-4], refs[-4:]
    total = functools.reduce(lambda t, r: t + r[...].astype(F32), ins[1:], ins[0][...].astype(F32))
    width = proj_ref.shape[1]
    qkv_ref[...] = total[:, : 3 * width]
    proj_ref[...] = total[:, 3 * width : 4 * width]
    misc = total[:, 4 * width :]
    misc_ref[...] = misc
    if turned_ref.shape[1] == VECTOR_ROWS:
        experts = turned_ref.shape[0]
        turned_ref[...] = misc.T[ROUTER_COL : ROUTER_COL + experts]
    else:
        turned_ref[...] = jnp.zeros_like(turned_ref)


def mix_kernel(experts, hid_ref, ret_ref, rprob_ref, poscol_ref, block_ref):
    tokens, slots = hid_ref.shape[0], ret_ref.shape[0]
    rprob = rprob_ref[...]
    lane = lax.broadcasted_iota(jnp.int32, (tokens, slots), 1)
    rlane = lax.broadcasted_iota(jnp.int32, (tokens, MISC), 1)
    mixed = hid_ref[...]
    for k in range(2):
        pos = poscol_ref[:, k : k + 1]
        picked = mm(one_hot(lane == pos), ret_ref[...])
        hot = (rlane == ROUTER_COL + poscol_ref[:, 2 + k : 3 + k]) & (pos >= 0)
        mixed = mixed + jnp.sum(jnp.where(hot, rprob, 0.0), axis=-1, keepdims=True) * picked
    block_ref[...] = mixed.astype(BF16)


def turn(blocks, at):
    part = blocks[:, :, at : at + VECTOR_ROWS]
    return blocks.at[:, :, at : at + VECTOR_ROWS].set(jnp.swapaxes(part, 1, 2))


def flip(x, stage):
    axis, size, bit = stage
    return lax.ppermute(x, axis, [(i, i ^ bit) for i in range(size)])


def line_permute(x, pairs):
    return lax.ppermute(x, "dp", pairs)


INWARD, ACROSS, OUTWARD = [(0, 1), (3, 2)], [(1, 2), (2, 1)], [(1, 0), (2, 3)]
SIDE = INWARD + OUTWARD


def add(a, b):
    return (a.astype(F32) + b.astype(F32)).astype(BF16)


def on_device(
    tokens, patch_counts, expert_ids, priority, out_grad, first_gain, first_shift, qkv_weight,
    query_bias, value_bias, proj_weight, proj_bias, second_gain, second_shift, router_weight,
    hidden_weight, hidden_bias, return_weight, return_bias, *, dp, ex,
):
    images, patches, width = tokens.shape
    count = images * patches
    top = expert_ids.shape[2]
    experts = router_weight.shape[1]
    capacity = (count * top * 105 + 100 * experts - 1) // (100 * experts)
    stride = (capacity + 2 + 15) // 16 * 16
    slots = experts * stride
    devices = dp * ex
    share_rows = qkv_weight.shape[0]
    ff_share = hidden_weight.shape[1]
    piece = width // dp
    dp_at = lax.axis_index("dp")
    ex_at = lax.axis_index("expert")
    me = dp_at * ex + ex_at
    in_kernel = share_rows % 16 == 0
    on_line = dp == 4

    vectors = [
        first_gain, first_shift, query_bias, value_bias, proj_bias, second_gain, second_shift,
    ]
    small = jnp.pad(router_weight, ((0, 0), (ROUTER_COL, MISC - ROUTER_COL - experts)))
    for j, vector in enumerate(vectors):
        if in_kernel:
            at = ((j, share_rows - 1 - j), (0, MISC - share_rows))
            small = small + jnp.pad(vector[None], at)
        else:
            small = small + jnp.pad(vector[:, None], ((0, 0), (j, MISC - 1 - j)))
    packed = jnp.concatenate([qkv_weight, proj_weight, small], axis=1)[None]
    tail = jnp.pad(hidden_bias, ((0, 15), (0, width - ff_share)))
    tail = tail + jnp.pad(return_bias, ((1, 14), (0, width - piece)))
    own = jnp.concatenate([hidden_weight[0], return_weight[0], tail], axis=0)
    if on_line:
        own, packed = lax.optimization_barrier((own, packed))
        side = line_permute(own, SIDE)
        across1 = line_permute(own, ACROSS)
    else:
        expert_w = lax.all_gather(own, "dp", axis=0)

    packed = jnp.concatenate([flip(packed, ("dp", dp, k)) if k else packed for k in range(dp)], axis=0)
    chips = ex // 2
    core = ("expert", ex, 1)

    if in_kernel:
        packed, patch_counts, expert_ids, priority = lax.optimization_barrier(
            (packed, patch_counts, expert_ids, priority)
        )
    valid = (
        lax.broadcasted_iota(jnp.int32, (images, patches), 1) < patch_counts[:, None]
    ).reshape(count)
    choices = expert_ids.reshape(count, top)
    rank = priority[0]
    earlier = (rank[:, None] > rank[None, :]).astype(BF16)
    iota = jnp.arange(experts, dtype=jnp.int32)
    hot = choices[:, :, None] == iota[None, None, :]
    hot_valid = (hot & valid[:, None, None]).astype(BF16).reshape(count, top * experts)
    before = jnp.dot(earlier, hot_valid, preferred_element_type=F32).reshape(count, top, experts)
    totals = jnp.sum(hot_valid.astype(F32), axis=0).reshape(top, experts)
    start = jnp.cumsum(totals, axis=0) - totals
    slot = jnp.sum(jnp.where(hot, before + start[None], 0.0), axis=-1).astype(jnp.int32)
    kept = valid[:, None] & (slot < capacity)
    pos = jnp.where(kept, choices * stride + slot, -1)
    pos_row = pos.T
    meta = jnp.concatenate([pos_row, choices.T], axis=0)
    meta = jnp.pad(meta, ((0, 4), (0, -count % MISC)))

    pieces = [flip(packed, ("expert", ex, 2 * j)) if j else packed for j in range(chips)]
    pieces += [flip(p, core) for p in pieces]
    rels = [[k * ex + 2 * j + b for k in range(dp)] for b in range(2) for j in range(chips)]
    if in_kernel:
        block_rows = share_rows
        kernel_rels = rels
    else:
        blocks, block_rows = width // 16, 16
        kernel_rels = [list(range(blocks))]
        at = np.argsort(np.array(sum(rels, [])))
        whole = jnp.concatenate(pieces, axis=0)[jnp.asarray(at)[jnp.arange(devices) ^ me]]
        pieces = [turn(whole.reshape(blocks, 16, -1), 4 * width)]

    pick = jnp.zeros((slots, count), jnp.bool_)
    slot_iota = lax.broadcasted_iota(jnp.int32, (slots, count), 0)
    for k in range(top):
        pick = pick | (slot_iota == pos_row[k][None, :])
    up = out_grad.reshape(count, width)
    up_slots = jnp.dot(pick.astype(BF16), up, preferred_element_type=F32).astype(BF16)

    pieces = [flip(packed, ("expert", ex, 2 * j)) if j else packed for j in range(chips)]
    pieces += [flip(p, core) for p in pieces]
    rels = [[k * ex + 2 * j + b for k in range(dp)] for b in range(2) for j in range(chips)]
    if in_kernel:
        block_rows = share_rows
        kernel_rels = rels
    else:
        blocks, block_rows = width // 16, 16
        kernel_rels = [list(range(blocks))]
        at = np.argsort(np.array(sum(rels, [])))
        whole = jnp.concatenate(pieces, axis=0)[jnp.asarray(at)[jnp.arange(devices) ^ me]]
        pieces = [turn(whole.reshape(blocks, 16, -1), 4 * width)]

    def exchange(x):
        x = lax.all_to_all(
            x.reshape(experts, stride, width), "expert", split_axis=0, concat_axis=0, tiled=True
        )
        return x.reshape(slots, width)


    tok = tokens.reshape(count, width)
    pairs = images * (HEADS // QUAD)
    if on_line:
        tails = biases([side, across1, own], 2 * ff_share, HOP1_COST)
        pieces, tails, side, across1 = lax.optimization_barrier((pieces, tails, side, across1))
        across2 = line_permute(side, ACROSS)
        out2 = line_permute(across1, OUTWARD)
    up_arrived = exchange(up_slots)
    made = (
        ((width, 2 * width), BF16),
        ((width, 2 * width + MISC), BF16),
        ((count, 3 * width), BF16),
        ((pairs, QUAD * patches, patches), BF16),
        ((count, width), BF16),
        ((count, width), F32),
        ((count, MISC), F32),
        ((slots, width), BF16),
        ((width, MISC), BF16),
        ((count, MISC), jnp.int32),
    )
    wa, wb, qkv, probs, ctx, hidden, rprob, dispatch, misc, pos_col = pl.pallas_call(
        functools.partial(
            front_kernel, (images, patches, experts, (dp, ex), in_kernel, kernel_rels)
        ),
        out_shape=tuple(shape(*m) for m in made),
        in_specs=[smem()] + [vmem()] * (2 + len(pieces)),
        out_specs=(vmem(),) * 10,
        compiler_params=params(56),
        cost_estimate=cost(0),
        name="front",
    )(patch_counts, tok, meta, *pieces)

    dispatch, up_arrived = lax.optimization_barrier((dispatch, up_arrived))
    arrived = exchange(dispatch)
    if on_line:
        chunks = [(out2, across1), (side, across2), (own,)]
        tails2 = biases([across2, out2], 2 * ff_share, HOP2_COST)
        out3 = line_permute(across2, OUTWARD)
        last, early_tails = (out3, side), (tails, tails2)
        rows_of = [((1, 16), (0, 16)), ((0, 0), (1, 0)), ((0, 32),), ((1, 0), (0, 0))]
        return_add = jnp.zeros((1, width), F32)
    else:
        chunks = [(expert_w[c],) for c in range(dp)]
        chunks, last = chunks[:-1], chunks[-1]
        tails = expert_w[:, 2 * ff_share :].reshape(dp * 16, width)
        early_tails = (tails, tails)
        rows_of = [((0, c * 16),) for c in range(dp)]
        return_add = expert_w[:, 2 * ff_share + 1, :piece].reshape(1, width).astype(F32)

    sem = pltpu.SemaphoreType.DMA
    early = dp - 1
    options = [len(c) for c in chunks]
    wide = shape((slots, width))
    matrix = pltpu.VMEM((ff_share, width), BF16)
    grad_rows = 2 * ff_share + 16
    grad = pltpu.VMEM((grad_rows, width), BF16)
    row_buffer, sum_buffer = pltpu.VMEM((slots, width), BF16), pltpu.VMEM((slots, width), F32)
    dma = lambda n: pltpu.SemaphoreType.DMA((n,))
    several = shape((early, slots, ff_share))
    g, acts, pgs, g_sum, d_all = pl.pallas_call(
        functools.partial(early_expert_kernel, options, experts, stride, on_line, rows_of[:-1]),
        out_shape=(
            wide, several, several, shape((1, width), F32), shape((dp, grad_rows, width)),
        ),
        in_specs=[anywhere()] * sum(options) + [vmem()] * 2 + [anywhere()] * 2 + [vmem()],
        out_specs=(anywhere(),) * 3 + (vmem(), anywhere()),
        scratch_shapes=[row_buffer] * 3
        + [pltpu.VMEM(several.shape, BF16)] * 2
        + [pltpu.VMEM((early * ff_share, width), BF16)] * 2
        + [pltpu.VMEM((early, grad_rows, width), BF16)]
        + [dma(2 * experts), dma(early), dma(early), dma(1 + 2 * early)],
        compiler_params=params(56),
        cost_estimate=cost(0),
        name="experts_early",
    )(*sum(chunks, ()), *early_tails, arrived, up_arrived, misc)
    if on_line:
        out3, g = lax.optimization_barrier((out3, g))
        last = (out3, side)
    operands = (*last, g_sum, arrived, g, d_all)
    narrow, part_buffer = shape((slots, ff_share)), pltpu.VMEM((slots, ff_share), BF16)
    act, pg, d_all = pl.pallas_call(
        functools.partial(last_grads_kernel, len(last), stride, on_line),
        out_shape=(narrow, narrow, shape((dp, grad_rows, width))),
        in_specs=[anywhere()] * len(last) + [vmem()] + [anywhere()] * 3,
        out_specs=(anywhere(),) * 3,
        scratch_shapes=[row_buffer, row_buffer, matrix, matrix, pltpu.VMEM((16, width), BF16)]
        + [part_buffer, part_buffer, grad, dma(2), dma(5), dma(experts)],
        input_output_aliases={len(operands) - 1: 2},
        compiler_params=params(56),
        cost_estimate=cost(HOP3_COST),
        name="last_grads",
    )(*operands)
    options = options + [len(last)]
    expert_out, *in_grad = pl.pallas_call(
        functools.partial(
            last_expert_kernel, options, (experts, capacity, stride, on_line), rows_of[:-1]
        ),
        out_shape=(wide,) + (shape((2 * stride, width)),) * chips,
        in_specs=[anywhere()] * sum(options) + [vmem()] * (2 * early) + [anywhere()] * 5 + [vmem()],
        out_specs=(anywhere(),) * (1 + chips),
        scratch_shapes=[pltpu.VMEM((dp, slots, ff_share), BF16)] * 2
        + [row_buffer]
        + [pltpu.VMEM((dp * ff_share, width), BF16)] * 2
        + [pltpu.VMEM((16, width), BF16), row_buffer, row_buffer, dma(dp), dma(2 * dp + chips), dma(2 * experts)],
        compiler_params=params(56),
        cost_estimate=cost(0),
        name="experts_last",
    )(
        *sum(chunks, ()), *last, *(early_tails * early),
        act, pg, acts, pgs, up_arrived, return_add,
    )
    gone = [flip(d, ("expert", ex, 2 * j)) if j else d for j, d in enumerate(in_grad)]
    expert_out, gone[1:] = lax.optimization_barrier((expert_out, gone[1:]))
    gone += [flip(d, core) for d in gone]
    returned = exchange(expert_out)
    d_sum = lax.psum_scatter(d_all, "dp", scatter_dimension=0, tiled=False)

    half = width // block_rows // 2
    pieces_out = chips if in_kernel else 1
    operands = (hidden, up, rprob, pos_col, wb, ctx, qkv, probs, wa, tok)
    tokens_grad, *sent = pl.pallas_call(
        functools.partial(
            back_kernel, (images, patches, experts, capacity, stride, (dp, ex), in_kernel)
        ),
        out_shape=(shape((count, width)),)
        + (shape((half // pieces_out, block_rows, 4 * width + MISC)),) * (2 * pieces_out),
        in_specs=[anywhere()] * (10 + experts),
        out_specs=(anywhere(),) * (1 + 2 * pieces_out),
        scratch_shapes=[row_buffer]
        + [pltpu.VMEM(b.shape, b.dtype) for b in operands]
        + [
            pltpu.VMEM((count, width), BF16),
            pltpu.VMEM((2 * half, block_rows, 4 * width + MISC), BF16),
            pltpu.VMEM((count, 3 * width), BF16),
            pltpu.VMEM((count, width), BF16),
            dma(10 + max(experts, 2 * pieces_out)),
        ],
        compiler_params=params(56),
        cost_estimate=cost(0),
        name="back",
    )(*operands, *gone)

    if not in_kernel:
        whole = jnp.stack(sent, axis=1).reshape(2 * half, block_rows, -1)
        whole = turn(whole, 4 * width).reshape(devices, share_rows, -1)
        whole = whole[jnp.asarray(np.array(sum(rels, []))) ^ me]
        sent = [whole[j * dp : (j + 1) * dp] for j in range(2 * chips)]
    sent, returned = lax.optimization_barrier((sent, returned))
    came = [flip(d, core) for d in sent[chips:]]
    parts = [add(k, c) for k, c in zip(sent[:chips], came)]
    moved = [flip(parts[j], ("expert", ex, 2 * j)) for j in range(1, chips)]
    total = functools.reduce(lambda t, m: t + m.astype(F32), moved, parts[0].astype(F32)).astype(BF16)
    block_out = pl.pallas_call(
        functools.partial(mix_kernel, experts),
        out_shape=shape((count, width)),
        in_specs=[vmem()] * 4,
        out_specs=vmem(),
        compiler_params=params(56),
        cost_estimate=cost(0),
        name="mix",
    )(hidden, returned, rprob, pos_col)
    total, block_out = lax.optimization_barrier((total, block_out))
    last_came = [flip(total[k], ("dp", dp, k)) for k in range(1, dp)]
    hidden_sum, return_sum, hidden_bias_sum, return_bias_sum = pl.pallas_call(
        finish_kernel,
        out_shape=(
            shape((ff_share, width), F32), shape((ff_share, width), F32),
            shape((1, ff_share), F32), shape((1, piece), F32),
        ),
        in_specs=[vmem()],
        out_specs=(vmem(),) * 4,
        compiler_params=params(56),
        cost_estimate=cost(0),
        name="finish",
    )(d_sum)
    last_came, hidden_sum, return_sum = lax.optimization_barrier((last_came, hidden_sum, return_sum))
    final_shapes = (shape((share_rows, 3 * width), F32), shape((share_rows, width), F32))
    qkv_sum, proj_sum, final, turned = pl.pallas_call(
        final_kernel,
        out_shape=final_shapes + (shape((share_rows, MISC), F32), shape((experts, share_rows), F32)),
        in_specs=[vmem()] * dp,
        out_specs=(vmem(),) * 4,
        compiler_params=params(24),
        cost_estimate=cost(0),
        name="final",
    )(total[0], *last_came)
    if in_kernel:
        vec = [final[j, :share_rows] for j in range(7)]
    else:
        vec = [final[:, j] for j in range(7)]
    router_sum = turned.T if in_kernel else final[:, ROUTER_COL : ROUTER_COL + experts]
    return (
        block_out.reshape(tokens.shape),
        tokens_grad.reshape(tokens.shape),
        vec[0], vec[1], qkv_sum, vec[2], vec[3], proj_sum, vec[4], vec[5], vec[6], router_sum,
        hidden_sum[None],
        hidden_bias_sum,
        return_sum[None],
        return_bias_sum,
    )


def solution(mesh):
    both, rows = P(("dp", "expert")), P(("dp", "expert"), None)
    cube = P(("dp", "expert"), None, None)
    weight, bias = P("expert", "dp", None), P("expert", "dp")
    in_specs = (
        cube, both, cube, rows, cube, both, both, rows, both, both, rows, both, both, both, rows,
        weight, bias, weight, bias,
    )
    out_specs = (
        cube, cube, both, both, rows, both, both, rows, both, both, both, rows,
        weight, bias, weight, bias,
    )
    return jax.shard_map(
        functools.partial(on_device, dp=mesh.shape["dp"], ex=mesh.shape["expert"]),
        mesh=mesh,
        in_specs=in_specs,
        out_specs=out_specs,
        check_vma=False,
    )
```
